32 devices in a mesh: dp: 8 (over z, y), mp: 4 (over x, core).
Axes of the slice: x: 2, y: 2, z: 4, core: 2. Of those that a mesh axis runs over, the one named last changes fastest.
Arguments:
- frames: bfloat16 [8704, 84, 336], P(('dp', 'mp')), may hold values from -4 to 4
- send_rows: int32 [16384], P(('dp', 'mp')), may hold values from 0 to 271, as said below
- recv_counts: int32 [256], P(('dp', 'mp')), may hold values from 1 to 64, as said below
- actions: int32 [16384], P(('dp', 'mp')), may hold values from 0 to 17
- target_dist: float32 [16384, 51], P(('dp', 'mp')), may hold values from 0 to 1, as said below
- sample_weight: float32 [16384], P(('dp', 'mp')), may hold values from 0.1 to 1
- conv_first: float32 [256, 32], P('dp'), may hold values from -0.5 to 0.5
- conv_second: float32 [512, 64], P('dp'), may hold values from -0.5 to 0.5
- conv_third: float32 [576, 64], P('dp'), may hold values from -0.5 to 0.5
- hidden_mean: float32 [2, 3136, 512], P(None, None, ('mp', 'dp')), may hold values from -0.15625 to 0.15625
- hidden_spread: float32 [2, 3136, 512], P(None, None, ('mp', 'dp')), may hold values from -0.078125 to 0.078125
- hidden_bias: float32 [2, 512], P(None, ('mp', 'dp')), may hold values from -1.5 to 1.5
- feature_noise: float32 [2, 3136], replicated, may hold values from -4 to 4
- hidden_noise: float32 [2, 2, 512], P(None, None, ('mp', 'dp')), may hold values from -4 to 4
- value_mean: float32 [512, 51], P(('mp', 'dp')), may hold values from -0.75 to 0.75
- value_spread: float32 [512, 51], P(('mp', 'dp')), may hold values from -0.375 to 0.375
- advantage_mean: float32 [512, 918], P(('mp', 'dp')), may hold values from -0.75 to 0.75
- advantage_spread: float32 [512, 918], P(('mp', 'dp')), may hold values from -0.375 to 0.375
- output_noise: float32 [969], replicated, may hold values from -4 to 4
- output_bias: float32 [969], replicated, may hold values from -2.5 to 2.5
Outputs:
- mean_loss: float32 [], replicated
- conv_first_grad: float32 [256, 32], P('dp')
- conv_second_grad: float32 [512, 64], P('dp')
- conv_third_grad: float32 [576, 64], P('dp')
- hidden_mean_grad: float32 [2, 3136, 512], P(None, None, ('mp', 'dp'))
- hidden_spread_grad: float32 [2, 3136, 512], P(None, None, ('mp', 'dp'))
- hidden_bias_grad: float32 [2, 512], P(None, ('mp', 'dp'))
- value_mean_grad: float32 [512, 51], P(('mp', 'dp'))
- value_spread_grad: float32 [512, 51], P(('mp', 'dp'))
- advantage_mean_grad: float32 [512, 918], P(('mp', 'dp'))
- advantage_spread_grad: float32 [512, 918], P(('mp', 'dp'))
- output_bias_grad: float32 [969], replicated
- priorities: float32 [16384], P(('dp', 'mp'))
The draws below stay inside these ranges and needn't reach their ends.
Inputs may be any that keep to these rules, and one draw needn't show every extreme that they name: `send_rows`: the 64 send slots that one replay shard sends to one learner name different rows of that shard; a row may go to several learners, and every row of a shard is sent. `recv_counts`: entry g * 8 + s: how many of the 64 slots that device s * 4 + (g % 4) sends to device g are used, always its first ones; in every draw some device uses all 64 slots from every source. `target_dist`: each row is positive and sums to one.
All inputs are finite; a program needn't handle non-finite values.
Results may differ from the reference program's by a relative error of at most 0.011.
Values may be sent and summed in bfloat16 or wider, within the bound.
A program may use at most 384 MiB of HBM per device.

```python
import math
import jax
import jax.numpy as jnp
from jax import lax

SIDE = 84
C1 = 32
C2 = 64
C3 = 64
HID = 512
ATOMS = 51
ACTIONS = 18
SLOTS_DEV = 512
R_DEV = 272
GROUPS = 32
SOURCES = 8
CAP = 64
BATCH = 16384
REPLAY = 8704
FEAT = 3136
OUTS = 969
N_DP = 8
N_MP = 4


def shard_order(key_one):
    return jax.random.permutation(key_one, R_DEV)


def draw_send_rows(key, part):
    key = jax.random.fold_in(key, 5)
    shard_keys = jax.random.split(key, GROUPS)
    orders = jax.vmap(shard_order)(shard_keys)
    cyclic = jnp.arange(SLOTS_DEV, dtype=jnp.int32) % R_DEV
    return orders[:, cyclic].reshape(BATCH).astype(jnp.int32)


def draw_recv_counts(key, part):
    key = jax.random.fold_in(key, 7)
    key_low, key_fill, key_full = jax.random.split(key, 3)
    lowest = jax.random.randint(key_low, (GROUPS, 1), 1, CAP + 1)
    spread_draw = jax.random.randint(key_fill, (GROUPS, SOURCES), 0, 1 << 20)
    counts_drawn = lowest + spread_draw % (CAP + 1 - lowest)
    full_group = jax.random.randint(key_full, (), 0, GROUPS)
    group_index = jnp.arange(GROUPS)[:, None]
    counts_drawn = jnp.where(group_index == full_group, CAP, counts_drawn)
    return counts_drawn.reshape(GROUPS * SOURCES).astype(jnp.int32)


def draw_target_dist(key, part):
    key = jax.random.fold_in(key, 11)
    scores = 1.5 * jax.random.normal(key, (BATCH, ATOMS), jnp.float32)
    weights_exp = jnp.exp(scores)
    return weights_exp / jnp.sum(weights_exp, axis=1, keepdims=True)


def set_ends(array, key, least, largest):
    place = [jax.random.randint(jax.random.fold_in(key, axis), (), 0, length) for axis, length in enumerate(array.shape)]
    longest = array.shape.index(max(array.shape))
    next_to = place[:longest] + [(place[longest] + 1) % array.shape[longest]] + place[longest + 1:]
    return array.at[tuple(place)].set(least).at[tuple(next_to)].set(largest)


def levels(rng, dims, cuts, smallest, high):
    loudness, own = 1.0, jax.random.fold_in(rng, 6)
    for position, shards_of in cuts:
        draws = jnp.exp(jax.random.uniform(jax.random.fold_in(own, position), (shards_of,), jnp.float32, smallest / len(cuts), high / len(cuts)))
        loudness = loudness * jnp.repeat(draws, dims[position] // shards_of).reshape([-1 if axis == position else 1 for axis in range(len(dims))])
    return loudness


def gaussian(own_key, dims, spread, most, shards=(), kind=jnp.bfloat16):
    drawn = jax.random.normal(own_key, dims, jnp.float32) * spread
    if len(shards) > 0:
        drawn = levels(own_key, dims, shards, -0.22, 0.18) * drawn
    return jnp.clip(drawn, min=-most, max=most).astype(kind)


def setup_inputs(seed: int = 0) -> dict:
    key_of = jax.random.split(jax.random.key(seed), 21)
    frames = gaussian(key_of[0], (REPLAY, SIDE, 4 * SIDE), 1.0, 4.0, ((0, 32),))
    send_rows = draw_send_rows(jax.random.fold_in(key_of[20], 71), 0)
    recv_counts = draw_recv_counts(jax.random.fold_in(key_of[20], 71), 0)
    actions = set_ends(jax.random.randint(key_of[3], (BATCH,), 0, ACTIONS), jax.random.fold_in(key_of[3], 1), 0, ACTIONS - 1).astype(jnp.int32)
    target_dist = draw_target_dist(jax.random.fold_in(key_of[20], 71), 0)
    sample_weight = jnp.clip(jnp.exp(math.log(1.0) - 2.3025851 * jax.random.uniform(key_of[5], (BATCH,), jnp.float32) ** levels(key_of[5], (BATCH,), ((0, 32),), -0.2, 0.2)), 0.1, 1.0)
    conv_first = gaussian(key_of[6], (256, C1), 128 ** -0.5, 0.5, ((0, 8),), jnp.float32)
    conv_second = gaussian(key_of[7], (16 * C1, C2), (4 * C1) ** -0.5, 0.5, ((0, 8),), jnp.float32)
    conv_third = gaussian(key_of[8], (9 * C2, C3), (2 * C2) ** -0.5, 0.5, ((0, 8),), jnp.float32)
    hidden_mean = gaussian(key_of[9], (2, FEAT, HID), (FEAT // 2) ** -0.5, 0.15625, ((2, 32),), jnp.float32)
    hidden_spread = gaussian(key_of[10], (2, FEAT, HID), (2 * FEAT) ** -0.5, 0.078125, ((2, 32),), jnp.float32)
    hidden_bias = gaussian(key_of[11], (2, HID), 0.3, 1.5, ((1, 32),), jnp.float32)
    feature_noise = gaussian(key_of[12], (2, FEAT), 1.0, 4.0, (), jnp.float32)
    hidden_noise = gaussian(key_of[13], (2, 2, HID), 1.0, 4.0, ((2, 32),), jnp.float32)
    value_mean = gaussian(key_of[14], (HID, ATOMS), (HID // 8) ** -0.5, 0.75, ((0, 32),), jnp.float32)
    value_spread = gaussian(key_of[15], (HID, ATOMS), (HID // 2) ** -0.5, 0.375, ((0, 32),), jnp.float32)
    advantage_mean = gaussian(key_of[16], (HID, ACTIONS * ATOMS), (HID // 8) ** -0.5, 0.75, ((0, 32),), jnp.float32)
    advantage_spread = gaussian(key_of[17], (HID, ACTIONS * ATOMS), (HID // 2) ** -0.5, 0.375, ((0, 32),), jnp.float32)
    output_noise = gaussian(key_of[18], (OUTS,), 1.0, 4.0, (), jnp.float32)
    output_bias = gaussian(key_of[19], (OUTS,), 0.5, 2.5, (), jnp.float32)
    return dict(frames=frames, send_rows=send_rows, recv_counts=recv_counts, actions=actions, target_dist=target_dist, sample_weight=sample_weight, conv_first=conv_first, conv_second=conv_second, conv_third=conv_third, hidden_mean=hidden_mean, hidden_spread=hidden_spread, hidden_bias=hidden_bias, feature_noise=feature_noise, hidden_noise=hidden_noise, value_mean=value_mean, value_spread=value_spread, advantage_mean=advantage_mean, advantage_spread=advantage_spread, output_noise=output_noise, output_bias=output_bias)


@jax.custom_vjp
def low(v):
    return lax.optimization_barrier(v.astype(jnp.bfloat16)).astype(jnp.float32)

@jax.custom_vjp
def low_back(v):
    return v

def low_keep(v):
    return (low(v), None)

def low_pass(kept, grad):
    return (grad,)

def back_keep(v):
    return (v, None)

def back_low(kept, grad):
    return (low(grad),)
low.defvjp(low_keep, low_pass)
low_back.defvjp(back_keep, back_low)

def silu_value(values):
    return values * jax.nn.sigmoid(values)

def space_depth(values, factor):
    batch_rows, height, breadth, channels = values.shape
    moved = values.reshape(batch_rows, height // factor, factor, breadth // factor, factor, channels)
    moved = moved.transpose(0, 1, 3, 2, 4, 5)
    return moved.reshape(batch_rows, height // factor, breadth // factor, factor * factor * channels)

def conv_patch(source, kernel, extent):
    out_side = source.shape[1] - extent + 1
    pieces = [source[:, shift_row:shift_row + out_side, shift_col:shift_col + out_side, :] for shift_row in range(extent) for shift_col in range(extent)]
    return jnp.einsum('npqc,cd->npqd', jnp.concatenate(pieces, axis=3), kernel, precision=lax.Precision.HIGHEST)

def reference(frames, send_rows, recv_counts, actions, target_dist, sample_weight, conv_first, conv_second, conv_third, hidden_mean, hidden_spread, hidden_bias, feature_noise, hidden_noise, value_mean, value_spread, advantage_mean, advantage_spread, output_noise, output_bias):
    group_ids = jnp.arange(GROUPS, dtype=jnp.int32)
    learner_dp = group_ids // N_MP
    learner_mp = group_ids % N_MP
    source_ids = jnp.arange(N_DP, dtype=jnp.int32)
    slot_ids = jnp.arange(CAP, dtype=jnp.int32)
    sender = source_ids[None, :, None] * N_MP + learner_mp[:, None, None]
    sender_slot = learner_dp[:, None, None] * CAP + slot_ids[None, None, :]
    local_rows = send_rows.reshape(GROUPS, SLOTS_DEV)[sender, sender_slot]
    replay_rows = (sender * R_DEV + local_rows).reshape(GROUPS, SLOTS_DEV).astype(jnp.int32)
    is_valid = slot_ids[None, None, :] < recv_counts.reshape(GROUPS, N_DP)[:, :, None]
    is_valid = is_valid.astype(jnp.float32).reshape(BATCH)
    chosen_mask = (actions[:, None] == jnp.arange(ACTIONS, dtype=jnp.int32)[None, :]).astype(jnp.float32)
    loss_coeff = is_valid * sample_weight

    def forward(kern_first, kern_second, kern_third, mean_one, spread_one, bias_one, mean_val, spread_val, mean_adv, spread_adv, bias_out):
        kern_one = low(kern_first)
        kern_two = low(kern_second)
        kern_three = low(kern_third)

        def torso_block(rows_block):
            frame_block = frames[rows_block].astype(jnp.float32).reshape(SLOTS_DEV, SIDE, SIDE, 4)
            pre_one = low_back(conv_patch(space_depth(frame_block, 4), kern_one, 2))
            act_one = low(silu_value(pre_one))
            pre_two = low_back(conv_patch(space_depth(act_one, 2), kern_two, 2))
            act_two = low(silu_value(pre_two))
            pre_three = low_back(conv_patch(act_two, kern_three, 3))
            return low(silu_value(pre_three)).reshape(SLOTS_DEV, FEAT)
        features = low_back(lax.map(jax.checkpoint(torso_block), replay_rows).reshape(BATCH, FEAT))
        weight_one = low(mean_one + spread_one * feature_noise[:, :, None] * hidden_noise[0][:, None, :])
        pre_hid = jnp.einsum('rf,ifh->rih', features, weight_one, precision=lax.Precision.HIGHEST)
        pre_hid = low_back(pre_hid + low(bias_one)[None, :, :])
        hidden = low(silu_value(pre_hid))
        weight_val = low(mean_val + spread_val * hidden_noise[1, 0][:, None] * output_noise[None, :ATOMS])
        weight_adv = low(mean_adv + spread_adv * hidden_noise[1, 1][:, None] * output_noise[None, ATOMS:])
        logits = jnp.concatenate([jnp.dot(hidden[:, 0], weight_val, precision=lax.Precision.HIGHEST), jnp.dot(hidden[:, 1], weight_adv, precision=lax.Precision.HIGHEST)], axis=1)
        logits = low_back(logits + bias_out[None, :])
        value_part = logits[:, :ATOMS]
        adv_part = logits[:, ATOMS:].reshape(BATCH, ACTIONS, ATOMS)
        chosen = lax.optimization_barrier(jnp.sum(chosen_mask[:, :, None] * adv_part, axis=1))
        q_atoms = value_part + chosen - lax.optimization_barrier(jnp.mean(adv_part, axis=1))
        row_top = lax.optimization_barrier(jnp.max(q_atoms, axis=1, keepdims=True))
        total_exp = lax.optimization_barrier(jnp.sum(jnp.exp(q_atoms - row_top), axis=1, keepdims=True))
        log_prob = q_atoms - row_top - jnp.log(total_exp)
        cross = -lax.optimization_barrier(jnp.sum(target_dist * log_prob, axis=1))
        return (jnp.sum(loss_coeff * cross), cross)
    total, pullback, cross = jax.vjp(forward, conv_first, conv_second, conv_third, hidden_mean, hidden_spread, hidden_bias, value_mean, value_spread, advantage_mean, advantage_spread, output_bias, has_aux=True)
    grads = pullback(jnp.ones_like(total))
    count_sum = jnp.sum(is_valid)
    priorities = (is_valid * cross).reshape(N_DP, N_MP, N_DP, CAP).transpose(2, 1, 0, 3).reshape(BATCH)
    return (total / count_sum, grads[0] / count_sum, grads[1] / count_sum, grads[2] / count_sum, grads[3] / count_sum, grads[4] / count_sum, grads[5] / count_sum, grads[6] / count_sum, grads[7] / count_sum, grads[8] / count_sum, grads[9] / count_sum, grads[10] / count_sum, priorities)
```

```python
import functools

import jax
import jax.numpy as jnp
from jax import lax
from jax.experimental import pallas as pl
from jax.experimental.pallas import tpu as pltpu
from jax.sharding import PartitionSpec as P

F32 = jnp.float32
BF16 = jnp.bfloat16
VMEM_LIMIT = 60 * 1024 * 1024


def sigmoid(v):
    return 0.5 * jnp.tanh(0.5 * v) + 0.5


def silu_and_slope(v):
    s = sigmoid(v)
    a = v * s
    return a, s + a * (1.0 - s)


def dot(a, b):
    return lax.dot_general(a, b, (((1,), (0,)), ((), ())), preferred_element_type=F32)


def dot_nt(a, b):
    return lax.dot_general(a, b, (((1,), (1,)), ((), ())), preferred_element_type=F32)


def dot_tn(a, b):
    return lax.dot_general(a, b, (((0,), (0,)), ((), ())), preferred_element_type=F32)


def columns_of_one():
    return [7 * (g // 8) + g % 8 if g % 8 < 7 and 7 * (g // 8) + g % 8 < 20 else -9 for g in range(24)]


def band_one(kern):
    w = kern.reshape(2, 2, 4, 16, 32).transpose(0, 2, 1, 3, 4).reshape(8, 2, 1, 16, 1, 32)
    group = lax.broadcasted_iota(jnp.int32, (8, 16, 8, 32), 0)
    col = lax.broadcasted_iota(jnp.int32, (8, 16, 8, 32), 2)
    zero = jnp.zeros((), kern.dtype)
    band = jnp.where((group == col) & (col < 7), w[:, 0], zero) + jnp.where((group == col + 1) & (col < 7), w[:, 1], zero)
    return band.reshape(8 * 128, 256)


def band_two(kern):
    w = kern.reshape(2, 2, 2, 2, 32, 64).transpose(0, 2, 1, 3, 4, 5).reshape(4, 4, 1, 32, 1, 64)
    grp = lax.broadcasted_iota(jnp.int32, (24, 32, 10, 64), 0)
    inside = grp % 8
    source = jnp.where(inside < 7, 7 * (grp // 8) + inside, -9)
    col = lax.broadcasted_iota(jnp.int32, (24, 32, 10, 64), 2)
    zero = jnp.zeros((), kern.dtype)
    band = sum(jnp.where((source == 2 * col + v) & (col < 9), w[:, v], zero) for v in range(4))
    return band.reshape(4, 768, 640)


def band_three(kern):
    w = kern.reshape(3, 3, 1, 64, 1, 64)
    source = lax.broadcasted_iota(jnp.int32, (10, 64, 8, 64), 0)
    col = lax.broadcasted_iota(jnp.int32, (10, 64, 8, 64), 2)
    zero = jnp.zeros((), kern.dtype)
    band = sum(jnp.where((source == col + v) & (col < 7), w[:, v], zero) for v in range(3))
    return band.reshape(3, 640, 512)


def unband_one(g):
    g = g.reshape(8, 8, 16, 8, 32)
    taps = jnp.stack([sum(g[:, c + v, :, c] for c in range(7)) for v in range(2)], axis=1)
    return taps.reshape(2, 4, 2, 16, 32).transpose(0, 2, 1, 3, 4).reshape(256, 32)


def unband_two(ga, gb, gc):
    blocks = ((ga.reshape(4, 12, 32, 4, 64), 0, 0, 4), (gb.reshape(4, 12, 32, 4, 64), 8, 4, 4), (gc.reshape(4, 8, 32, 2, 64), 16, 8, 1))
    cols = columns_of_one()
    taps = []
    for v in range(4):
        total = 0.0
        for g, first, c0, count in blocks:
            for c in range(count):
                total = total + g[:, cols.index(2 * (c0 + c) + v) - first, :, c]
        taps.append(total)
    taps = jnp.stack(taps, axis=1)
    return taps.reshape(2, 2, 2, 2, 32, 64).transpose(0, 2, 1, 3, 4, 5).reshape(512, 64)


def unband_three(g):
    g = g.reshape(3, 6, 64, 4, 64)
    taps = jnp.stack([sum(g[:, c + v, :, c] for c in range(4)) for v in range(3)], axis=1)
    return taps.reshape(576, 64)


def shifted_blocks(x):
    rows = x.shape[0]
    return (
        x[:, 0:128],
        x[:, 112:240],
        jnp.concatenate([x[:, 224:336], jnp.zeros((rows, 16), x.dtype)], axis=1),
    )


def forward_kernel(x_ref, xn_ref, b1_ref, b2_ref, b3_ref, a1_ref, s1_ref, a2_ref, s2_ref, f_ref, s3_ref, xs, a1s, a2s):
    i = pl.program_id(0)
    rows = x_ref.shape[2]
    for big in range(5):
        for r in range(4):
            src = x_ref[big, r] if big < 4 else xn_ref[0, r]
            for j, blk in enumerate(shifted_blocks(src)):
                xs[big, j, :, 128 * r : 128 * r + 128] = blk
    for pp in range(4):
        for j in range(3):
            lhs = jnp.concatenate([xs[pp, j], xs[pp + 1, j]], axis=1)
            act, slope = silu_and_slope(dot(lhs, b1_ref[...]))
            act = act.astype(BF16)
            a1_ref[pp // 2, pp % 2, :, 256 * j : 256 * j + 256] = act
            a1s[2 * i + pp // 2, pp % 2, :, 256 * j : 256 * j + 256] = act
            s1_ref[pp // 2, pp % 2, :, 256 * j : 256 * j + 256] = slope.astype(BF16)

    def second(p):
        for lo, hi, n0, n1 in ((0, 384, 0, 256), (256, 640, 256, 512), (512, 768, 512, 640)):
            lhs = jnp.concatenate([a1s[p + u // 2, u % 2, :, lo:hi] for u in range(4)], axis=1)
            rhs = jnp.concatenate([b2_ref[u, lo:hi, n0:n1] for u in range(4)], axis=0)
            act, slope = silu_and_slope(dot(lhs, rhs))
            act = act.astype(BF16)
            a2_ref[p, :, n0:n1] = act
            a2s[p, :, n0:n1] = act
            s2_ref[p, :, n0:n1] = slope.astype(BF16)

    def third(p, odd):
        acts, slopes = [], []
        for lo, hi, n0, n1 in ((0, 384, 0, 256), (256, 640, 256, 512)):
            lhs = jnp.concatenate([a2s[p + u, :, lo:hi] for u in range(3)], axis=1)
            rhs = jnp.concatenate([b3_ref[u, lo:hi, n0:n1] for u in range(3)], axis=0)
            act, slope = silu_and_slope(dot(lhs, rhs))
            acts.append(act)
            slopes.append(slope)
        lane = lax.broadcasted_iota(jnp.int32, (rows, 512), 1)
        base = (p // 2) * 896
        for out, parts in ((f_ref, acts), (s3_ref, slopes)):
            whole = jnp.where(lane < 448, jnp.concatenate(parts, axis=1), 0.0)
            if not odd:
                out[:, pl.ds(pl.multiple_of(base, 128), 512)] = whole.astype(BF16)
            else:
                whole = pltpu.roll(whole, 64, 1)
                at = pl.ds(pl.multiple_of(base + 384, 128), 128)
                out[:, at] = (out[:, at].astype(F32) + whole[:, :128]).astype(BF16)
                out[:, pl.ds(pl.multiple_of(base + 512, 128), 384)] = whole[:, 128:].astype(BF16)

    @pl.when(i >= 1)
    def _():
        second(2 * i - 1)

    second(2 * i)

    @pl.when(i >= 2)
    def _():
        third(2 * i - 3, True)

    @pl.when(i >= 1)
    def _():
        third(2 * i - 2, False)

    @pl.when(i == 4)
    def _():
        lane = lax.broadcasted_iota(jnp.int32, (rows, 128), 1)
        last = f_ref[:, 3072:3200].astype(F32)
        f_ref[:, 3072:3200] = jnp.where(lane == 64, 1.0, last).astype(BF16)


def full(shape):
    return pl.BlockSpec(shape, lambda *_: (0,) * len(shape))


def once(shape):
    return pl.BlockSpec(shape, lambda *_: (0,) * len(shape), pipeline_mode=pl.Buffered(1))


def torso_forward(x, band1, band2, band3):
    rows = x.shape[2]
    shapes = [(10, 2, rows, 768)] * 2 + [(9, rows, 640)] * 2 + [(rows, 3200)] * 2
    return pl.pallas_call(
        forward_kernel,
        grid=(5,),
        in_specs=[
            pl.BlockSpec((4, 4, rows, 336), lambda i: (i, 0, 0, 0)),
            pl.BlockSpec((1, 4, rows, 336), lambda i: (4 * i + 4, 0, 0, 0)),
            once(band1.shape),
            once(band2.shape),
            once(band3.shape),
        ],
        out_specs=[pl.BlockSpec((2, 2, rows, 768), lambda i: (i, 0, 0, 0))] * 2
        + [once((9, rows, 640))] * 2
        + [once((rows, 3200))] * 2,
        out_shape=[jax.ShapeDtypeStruct(s, BF16) for s in shapes],
        scratch_shapes=[
            pltpu.VMEM((5, 3, rows, 512), BF16),
            pltpu.VMEM((10, 2, rows, 768), BF16),
            pltpu.VMEM((9, rows, 640), BF16),
        ],
        compiler_params=pltpu.CompilerParams(vmem_limit_bytes=VMEM_LIMIT),
        name="torso_forward",
    )(x, x, band1, band2, band3)


def backward_kernel(
    x_ref, xn_ref, a1_ref, s1_ref, a2_ref, s2_ref, s3_ref, fg_ref, b2_ref, b3_ref, d1_ref, d2a_ref, d2b_ref, d2c_ref, d3_ref, xs, g3, g2
):
    i = pl.program_id(0)
    rows = x_ref.shape[2]

    @pl.when(i == 0)
    def _():
        for at in (0, 1, 9, 10):
            g3[at] = jnp.zeros((rows, 512), BF16)
        for at in (0, 10):
            g2[at] = jnp.zeros((rows, 640), BF16)
        lane = lax.broadcasted_iota(jnp.int32, (rows, 512), 1)
        for p in range(7):
            base = (p // 2) * 896 + (384 if p % 2 else 0)
            both = fg_ref[:, base : base + 512].astype(F32) * s3_ref[:, base : base + 512].astype(F32)
            if p % 2:
                both = pltpu.roll(both, 448, 1)
            g3[p + 2] = jnp.where(lane < 448, both, 0.0).astype(BF16)
        for u in range(3):
            total = 0.0
            for m in range(2):
                lhs = a2_ref[u : u + 7, :, 256 * m : 256 * m + 384].reshape(7 * rows, 384)
                rhs = g3[2:9, :, 256 * m : 256 * m + 256].reshape(7 * rows, 256)
                total = total + dot_tn(lhs, rhs)
            d3_ref[u] = total
        d1_ref[...] = jnp.zeros_like(d1_ref)
        d2a_ref[...] = jnp.zeros_like(d2a_ref)
        d2b_ref[...] = jnp.zeros_like(d2b_ref)
        d2c_ref[...] = jnp.zeros_like(d2c_ref)
        for lo, hi, n0, n1 in ((0, 256, 0, 256), (256, 512, 128, 512), (512, 640, 384, 512)):
            rhs = jnp.concatenate([b3_ref[u, lo:hi, n0:n1] for u in range(3)], axis=1)

            def one(p, _):
                lhs = jnp.concatenate([g3[p + 2 - u, :, n0:n1] for u in range(3)], axis=1)
                back = dot_nt(lhs, rhs) * s2_ref[p, :, lo:hi].astype(F32)
                g2[p + 1, :, lo:hi] = back.astype(BF16)
                return 0

            lax.fori_loop(0, 9, one, 0)

    for r in range(2):
        for t in range(2):
            for ref, lo, hi, n0, n1 in ((d2a_ref, 0, 384, 0, 256), (d2b_ref, 256, 640, 256, 512), (d2c_ref, 512, 768, 512, 640)):
                lhs = a1_ref[:, r, :, lo:hi].reshape(2 * rows, hi - lo)
                rhs = g2[pl.ds(2 * i + 1 - t, 2), :, n0:n1].reshape(2 * rows, n1 - n0)
                ref[2 * t + r] += dot_tn(lhs, rhs)

    for big in range(5):
        for r in range(4):
            src = x_ref[big, r] if big < 4 else xn_ref[0, r]
            for j, blk in enumerate(shifted_blocks(src)):
                xs[big, j, :, 128 * r : 128 * r + 128] = blk

    for j, (n0, n1) in enumerate(((0, 256), (128, 512), (384, 640))):
        grads = []
        for pp in range(4):
            r = pp % 2
            at = 2 * i + pp // 2 + 1
            lhs = jnp.concatenate([g2[at, :, n0:n1], g2[at - 1, :, n0:n1]], axis=1)
            rhs = jnp.concatenate([b2_ref[r, 256 * j : 256 * j + 256, n0:n1], b2_ref[2 + r, 256 * j : 256 * j + 256, n0:n1]], axis=1)
            back = dot_nt(lhs, rhs) * s1_ref[pp // 2, r, :, 256 * j : 256 * j + 256].astype(F32)
            grads.append(back.astype(BF16))
        grad = jnp.concatenate(grads, axis=0)
        for t in range(2):
            lhs = xs[t : t + 4, j].reshape(4 * rows, 512)
            d1_ref[512 * t : 512 * t + 512, :] += dot_tn(lhs, grad)


def torso_backward(x, a1, s1, a2, s2, s3, fg, band2, band3):
    rows = x.shape[2]
    outs = [(1024, 256), (4, 384, 256), (4, 384, 256), (4, 256, 128), (3, 384, 256)]
    return pl.pallas_call(
        backward_kernel,
        grid=(5,),
        in_specs=[
            pl.BlockSpec((4, 4, rows, 336), lambda i: (i, 0, 0, 0)),
            pl.BlockSpec((1, 4, rows, 336), lambda i: (4 * i + 4, 0, 0, 0)),
            pl.BlockSpec((2, 2, rows, 768), lambda i: (i, 0, 0, 0)),
            pl.BlockSpec((2, 2, rows, 768), lambda i: (i, 0, 0, 0)),
            once(a2.shape),
            once(s2.shape),
            once(s3.shape),
            once(fg.shape),
            once(band2.shape),
            once(band3.shape),
        ],
        out_specs=[once(s) for s in outs],
        out_shape=[jax.ShapeDtypeStruct(s, F32) for s in outs],
        scratch_shapes=[
            pltpu.VMEM((5, 3, rows, 512), BF16),
            pltpu.VMEM((11, rows, 512), BF16),
            pltpu.VMEM((11, rows, 640), BF16),
        ],
        compiler_params=pltpu.CompilerParams(vmem_limit_bytes=VMEM_LIMIT),
        name="torso_backward",
    )(x, x, a1, s1, a2, s2, s3, fg, band2, band3)


def high_low(v):
    high = v.astype(BF16)
    return high, (v - high.astype(F32)).astype(BF16)


def heads_kernel(
    atoms, acts, f_ref, w_ref, bias_ref, tgt_ref, slot_ref, sel_ref, selt_ref, fold_ref, foldt_ref, dw_ref, fg_ref, prio_ref, stat_ref, bg_ref
):
    rows = f_ref.shape[0]
    slots = tgt_ref.shape[0]
    feats = f_ref[...]
    pre = [dot_nt(feats, w_ref[:, 3200 * k : 3200 * k + 3200]) for k in range(2)]
    hidden, slope = [], []
    for k in range(2):
        a, s = silu_and_slope(pre[k])
        hidden.append(a.astype(BF16))
        slope.append(s)
    out_w = w_ref[:, 6400:7424]
    wide = out_w.shape[1]
    lane = lax.broadcasted_iota(jnp.int32, (1, wide), 1)
    zero = jnp.zeros((), BF16)
    w_val = jnp.where(lane[:, :128] < atoms, out_w[:, :128].astype(F32), 0.0).astype(BF16)
    w_adv = jnp.where(lane >= atoms, out_w.astype(F32), 0.0).astype(BF16)
    logits = dot(hidden[1], w_adv) + bias_ref[...]
    logits = jnp.concatenate([logits[:, :128] + dot(hidden[0], w_val), logits[:, 128:]], axis=1)
    high, low = high_low(logits)
    per_slot = dot(sel_ref[...], high) + dot(sel_ref[...], low)
    action = slot_ref[:, 2:3]
    which = jnp.where(lane < atoms, -1, jnp.where(lane < atoms * (acts + 1), (lane - atoms) // atoms, -2)).astype(F32)
    coeff = jnp.where(which == -1.0, 1.0, 0.0) + jnp.where(which == action, 1.0, 0.0) - jnp.where(which >= 0.0, 1.0 / acts, 0.0)
    high, low = high_low(per_slot * coeff)
    q = dot(high, fold_ref[...]) + dot(low, fold_ref[...])
    lane_q = lax.broadcasted_iota(jnp.int32, (slots, 128), 1)
    used = lane_q < atoms
    top = jnp.max(jnp.where(used, q, -jnp.inf), axis=1, keepdims=True)
    shifted = jnp.where(used, jnp.exp(jnp.where(used, q - top, 0.0)), 0.0)
    total = jnp.sum(shifted, axis=1, keepdims=True)
    tgt = tgt_ref[...]
    cross = -jnp.sum(jnp.where(used, tgt * (q - top - jnp.log(total)), 0.0), axis=1, keepdims=True)
    coef = slot_ref[:, 0:1]
    valid = slot_ref[:, 1:2]
    prio_ref[...] = valid * cross
    q_grad = coef * (shifted * (jnp.sum(tgt, axis=1, keepdims=True) / total) - tgt)
    high, low = high_low(q_grad)
    lgrad = ((dot(high, foldt_ref[...]) + dot(low, foldt_ref[...])) * coeff).astype(BF16)
    bg_ref[...] = jnp.sum(lgrad.astype(F32), axis=0, keepdims=True)
    stat_ref[0:1, :] = jnp.broadcast_to(jnp.sum(coef * cross, axis=0, keepdims=True), (1, 128))
    stat_ref[1:2, :] = jnp.broadcast_to(jnp.sum(valid, axis=0, keepdims=True), (1, 128))
    grad = dot(selt_ref[...], lgrad).astype(BF16)
    d_adv = dot_tn(hidden[1], grad)
    d_val = dot_tn(hidden[0], grad[:, :128])
    dw_ref[:, 6528:7424] = d_adv[:, 128:].astype(BF16)
    dw_ref[:, 6400:6528] = jnp.where(lane[:, :128] < atoms, d_val, d_adv[:, :128]).astype(BF16)
    pre_grad = [
        (dot_nt(grad[:, :128], w_val) * slope[0]).astype(BF16),
        (dot_nt(grad, w_adv) * slope[1]).astype(BF16),
    ]
    for k in range(2):
        for lo, hi in ((0, 1024), (1024, 2048), (2048, 3200)):
            dw_ref[:, 3200 * k + lo : 3200 * k + hi] = dot_tn(pre_grad[k], f_ref[:, lo:hi]).astype(BF16)
    for lo, hi in ((0, 1024), (1024, 2048), (2048, 3200)):
        back = dot(pre_grad[0], w_ref[:, lo:hi]) + dot(pre_grad[1], w_ref[:, 3200 + lo : 3200 + hi])
        fg_ref[:, lo:hi] = back.astype(BF16)


def heads(atoms, acts, feats, weights, bias, tgt, slot, rows_of_slot):
    rows, slots, wide = feats.shape[0], tgt.shape[0], bias.shape[1]
    sel = (rows_of_slot[:, None] == jnp.arange(rows, dtype=jnp.int32)[None, :]).astype(BF16)
    selt = (jnp.arange(rows, dtype=jnp.int32)[:, None] == rows_of_slot[None, :]).astype(BF16)
    n = jnp.arange(wide, dtype=jnp.int32)
    z = jnp.where(n < atoms * (acts + 1), n % atoms, -1)
    fold = (z[:, None] == jnp.arange(128, dtype=jnp.int32)[None, :]).astype(BF16)
    foldt = (jnp.arange(128, dtype=jnp.int32)[:, None] == z[None, :]).astype(BF16)
    return pl.pallas_call(
        functools.partial(heads_kernel, atoms, acts),
        out_shape=[
            jax.ShapeDtypeStruct(weights.shape, BF16),
            jax.ShapeDtypeStruct(feats.shape, BF16),
            jax.ShapeDtypeStruct((slots, 1), F32),
            jax.ShapeDtypeStruct((8, 128), F32),
            jax.ShapeDtypeStruct((1, wide), F32),
        ],
        compiler_params=pltpu.CompilerParams(vmem_limit_bytes=VMEM_LIMIT),
        name="heads",
    )(feats, weights, bias, tgt, slot, sel, selt, fold, foldt)


def on_device(
    frames,
    send_rows,
    recv_counts,
    actions,
    target_dist,
    sample_weight,
    conv_first,
    conv_second,
    conv_third,
    hidden_mean,
    hidden_spread,
    hidden_bias,
    feature_noise,
    hidden_noise,
    value_mean,
    value_spread,
    advantage_mean,
    advantage_spread,
    output_noise,
    output_bias,
):
    dp_count = lax.axis_size("dp")
    slots = send_rows.shape[0]
    capacity = slots // dp_count
    atoms = value_mean.shape[1]
    acts = advantage_mean.shape[1] // atoms
    rows = frames.shape[0]
    feat, own = hidden_mean.shape[1:]
    outs = atoms * (acts + 1)

    flat = jnp.concatenate([w.astype(BF16).reshape(-1) for w in (conv_first, conv_second, conv_third)])
    flat = lax.all_gather(flat, "dp", axis=0, tiled=False)
    sizes = [w.size for w in (conv_first, conv_second, conv_third)]
    kern1 = flat[:, : sizes[0]].reshape(-1, conv_first.shape[1])
    kern2 = flat[:, sizes[0] : sizes[0] + sizes[1]].reshape(-1, conv_second.shape[1])
    kern3 = flat[:, sizes[0] + sizes[1] :].reshape(-1, conv_third.shape[1])
    band1, band2, band3 = band_one(kern1), band_two(kern2), band_three(kern3)

    mean_t = hidden_mean.transpose(0, 2, 1)
    spread_t = hidden_spread.transpose(0, 2, 1)
    wide_one = mean_t + spread_t * feature_noise[:, None, :] * hidden_noise[0][:, :, None]
    wide_one = jnp.concatenate([wide_one, hidden_bias[:, :, None], jnp.zeros((2, own, 63), F32)], axis=2)
    wide_val = value_mean + value_spread * hidden_noise[1, 0][:, None] * output_noise[None, :atoms]
    wide_adv = advantage_mean + advantage_spread * hidden_noise[1, 1][:, None] * output_noise[None, atoms:]
    shard = jnp.concatenate(
        [wide_one[0], wide_one[1], wide_val, wide_adv, jnp.zeros((own, 1024 - outs), F32)], axis=1
    ).astype(BF16)
    weights = lax.all_gather(shard, ("mp", "dp"), axis=0, tiled=True)

    is_valid = jnp.arange(capacity, dtype=jnp.int32)[None, :] < recv_counts[:, None]
    is_valid = is_valid.astype(F32).reshape(slots)
    per_slot = jnp.concatenate(
        [target_dist, (is_valid * sample_weight)[:, None], is_valid[:, None], actions.astype(F32)[:, None]], axis=1
    )
    per_slot = lax.all_to_all(per_slot, "dp", split_axis=0, concat_axis=0, tiled=True)
    tgt = jnp.pad(per_slot[:, :atoms], ((0, 0), (0, 128 - atoms)))
    slot = per_slot[:, atoms:]

    x = frames.transpose(1, 0, 2).reshape(21, 4, rows, 336)
    a1, s1, a2, s2, feats, s3 = torso_forward(x, band1, band2, band3)
    bias = jnp.pad(output_bias, (0, 1024 - outs))[None, :]
    dweights, feat_grad, prio, stat, bias_grad = heads(atoms, acts, feats, weights, bias, tgt, slot, send_rows)
    dshard = lax.psum_scatter(dweights, ("mp", "dp"), scatter_dimension=0, tiled=True).astype(F32)
    loss_sum, count, bias_sum = lax.psum((stat[0, 0], stat[1, 0], bias_grad[0, :outs]), ("dp", "mp"))
    inverse = 1.0 / count

    d1, d2a, d2b, d2c, d3 = torso_backward(x, a1, s1, a2, s2, s3, feat_grad, band2, band3)
    kgrads = (unband_one(d1), unband_two(d2a, d2b, d2c), unband_three(d3))
    kflat = jnp.concatenate([g.reshape(dp_count, -1) for g in kgrads], axis=1)
    kflat = lax.psum(lax.psum_scatter(kflat, "dp", scatter_dimension=0, tiled=True)[0], "mp") * inverse
    conv_grads = (
        kflat[: sizes[0]].reshape(conv_first.shape),
        kflat[sizes[0] : sizes[0] + sizes[1]].reshape(conv_second.shape),
        kflat[sizes[0] + sizes[1] :].reshape(conv_third.shape),
    )

    dshard = dshard * inverse
    mean_grad_t = jnp.stack([dshard[:, :feat], dshard[:, 3200 : 3200 + feat]])
    spread_grad_t = mean_grad_t * feature_noise[:, None, :] * hidden_noise[0][:, :, None]
    value_mean_grad = dshard[:, 6400 : 6400 + atoms]
    adv_mean_grad = dshard[:, 6400 + atoms : 6400 + outs]
    return (
        loss_sum * inverse,
        *conv_grads,
        mean_grad_t.transpose(0, 2, 1),
        spread_grad_t.transpose(0, 2, 1),
        jnp.stack([dshard[:, feat], dshard[:, 3200 + feat]]),
        value_mean_grad,
        value_mean_grad * hidden_noise[1, 0][:, None] * output_noise[None, :atoms],
        adv_mean_grad,
        adv_mean_grad * hidden_noise[1, 1][:, None] * output_noise[None, atoms:],
        bias_sum * inverse,
        prio[:, 0],
    )


def solution(mesh):
    both, heads_dim = P(("dp", "mp")), P(("mp", "dp"), None)
    return jax.shard_map(
        on_device,
        mesh=mesh,
        in_specs=(
            P(("dp", "mp"), None, None),
            both,
            both,
            both,
            P(("dp", "mp"), None),
            both,
            P("dp", None),
            P("dp", None),
            P("dp", None),
            P(None, None, ("mp", "dp")),
            P(None, None, ("mp", "dp")),
            P(None, ("mp", "dp")),
            P(),
            P(None, None, ("mp", "dp")),
            heads_dim,
            heads_dim,
            heads_dim,
            heads_dim,
            P(),
            P(),
        ),
        out_specs=(
            P(),
            P("dp", None),
            P("dp", None),
            P("dp", None),
            P(None, None, ("mp", "dp")),
            P(None, None, ("mp", "dp")),
            P(None, ("mp", "dp")),
            heads_dim,
            heads_dim,
            heads_dim,
            heads_dim,
            P(),
            both,
        ),
        check_vma=False,
    )
```

```python
import functools

import jax
import jax.numpy as jnp
from jax import lax
from jax.experimental import pallas as pl
from jax.experimental.pallas import tpu as pltpu
from jax.sharding import PartitionSpec as P

F32 = jnp.float32
BF16 = jnp.bfloat16
VMEM_LIMIT = 60 * 1024 * 1024


def sigmoid(v):
    return 0.5 * jnp.tanh(0.5 * v) + 0.5


def silu_and_slope(v):
    s = sigmoid(v)
    a = v * s
    return a, s + a * (1.0 - s)


def dot(a, b):
    return lax.dot_general(a, b, (((1,), (0,)), ((), ())), preferred_element_type=F32)


def dot_nt(a, b):
    return lax.dot_general(a, b, (((1,), (1,)), ((), ())), preferred_element_type=F32)


def dot_tn(a, b):
    return lax.dot_general(a, b, (((0,), (0,)), ((), ())), preferred_element_type=F32)


def columns_of_one():
    return [7 * (g // 8) + g % 8 if g % 8 < 7 and 7 * (g // 8) + g % 8 < 20 else -9 for g in range(24)]


def half_lanes(left, right, rows):
    lane = lax.broadcasted_iota(jnp.int32, (rows, 128), 1)
    zero = jnp.zeros((rows, 128), F32)
    return jnp.where(lane < 64, zero if left is None else left, zero if right is None else right)


def fill_band_one(k1_ref, band):
    lane = lax.broadcasted_iota(jnp.int32, (16, 128), 1) // 32
    for u in range(8):
        taps = [k1_ref[((u // 4) * 2 + v) * 64 + (u % 4) * 16 :][:16].astype(F32) for v in range(2)]
        for g in range(8):
            for h in range(2):
                col = lane + 4 * h
                here = jnp.where((col == g) & (col < 7), taps[0], 0.0) + jnp.where((col == g - 1) & (col < 7), taps[1], 0.0)
                band[128 * u + 16 * g : 128 * u + 16 * g + 16, 128 * h : 128 * h + 128] = here.astype(BF16)


def fill_band_two(k2_ref, band):
    band[...] = jnp.zeros_like(band)
    cols = columns_of_one()
    for u in range(4):

        def tap(v):
            at = ((u // 2) * 2 + v // 2) * 128 + ((u % 2) * 2 + v % 2) * 32
            return k2_ref[at : at + 32, :].astype(F32)

        for g, q in enumerate(cols):
            if q < 0:
                continue
            used = {(q - v) // 2: v for v in (q % 2, q % 2 + 2) if 0 <= (q - v) // 2 < 9}
            for m in sorted({c // 2 for c in used}):
                sides = [tap(used[2 * m + side]) if 2 * m + side in used else None for side in range(2)]
                band[u, 32 * g : 32 * g + 32, 128 * m : 128 * m + 128] = half_lanes(*sides, 32).astype(BF16)


def fill_band_three(k3_ref, band):
    band[...] = jnp.zeros_like(band)
    for u in range(3):

        def tap(v):
            return k3_ref[(u * 3 + v) * 64 : (u * 3 + v) * 64 + 64, :].astype(F32)

        for q in range(9):
            used = {q - v: v for v in range(3) if 0 <= q - v < 7}
            for m in sorted({c // 2 for c in used}):
                sides = [tap(used[2 * m + side]) if 2 * m + side in used else None for side in range(2)]
                band[u, 64 * q : 64 * q + 64, 128 * m : 128 * m + 128] = half_lanes(*sides, 64).astype(BF16)


def fold_lanes(v, width):
    step = 64
    while step >= width:
        v = v + pltpu.roll(v, step, 1)
        step //= 2
    return v


def take_band_one(d1, out):
    lane = lax.broadcasted_iota(jnp.int32, (16, 128), 1) // 32
    for u in range(8):
        for v in range(2):
            total = jnp.zeros((16, 128), F32)
            for col in range(7):
                at = 128 * u + 16 * (col + v)
                h = col // 4
                total = total + jnp.where(lane + 4 * h == col, d1[at : at + 16, 128 * h : 128 * h + 128], 0.0)
            at = ((u // 4) * 2 + v) * 64 + (u % 4) * 16
            out[at : at + 16, :] = fold_lanes(total, 32)


def take_band_two(blocks, out):
    cols = columns_of_one()
    lane = lax.broadcasted_iota(jnp.int32, (32, 128), 1)
    for u in range(4):
        for v in range(4):
            total = jnp.zeros((32, 128), F32)
            for ref, first, c0, count in blocks:
                for c in range(count):
                    at = 32 * (cols.index(2 * (c0 + c) + v) - first)
                    piece = ref[u, at : at + 32, 128 * (c // 2) : 128 * (c // 2) + 128]
                    total = total + jnp.where((lane < 64) == (c % 2 == 0), piece, 0.0)
            at = ((u // 2) * 2 + v // 2) * 128 + ((u % 2) * 2 + v % 2) * 32
            out[at : at + 32, :] = fold_lanes(total, 64)


def take_band_three(d3, out):
    lane = lax.broadcasted_iota(jnp.int32, (64, 128), 1)
    for u in range(3):
        for v in range(3):
            total = jnp.zeros((64, 128), F32)
            for c in range(4):
                piece = d3[u, 64 * (c + v) : 64 * (c + v) + 64, 128 * (c // 2) : 128 * (c // 2) + 128]
                total = total + jnp.where((lane < 64) == (c % 2 == 0), piece, 0.0)
            at = (u * 3 + v) * 64
            out[at : at + 64, :] = fold_lanes(total, 64)


def shifted_blocks(x):
    rows = x.shape[0]
    return (
        x[:, 0:128],
        x[:, 112:240],
        jnp.concatenate([x[:, 224:336], jnp.zeros((rows, 16), x.dtype)], axis=1),
    )


def forward_kernel(
    x_ref, xn_ref, k1_ref, k2_ref, k3_ref, a1_ref, s1_ref, a2_ref, s2_ref, f_ref, s3_ref, y_ref, y0_ref, carry, a1s, a2s, b1_ref, b2_ref, b3_ref
):
    i = pl.program_id(0)
    rows = x_ref.shape[2]

    @pl.when(i == 0)
    def _():
        fill_band_one(k1_ref, b1_ref)
        fill_band_two(k2_ref, b2_ref)
        fill_band_three(k3_ref, b3_ref)
        for r in range(4):
            for j, blk in enumerate(shifted_blocks(x_ref[0, r])):
                carry[j, :, 128 * r : 128 * r + 128] = blk
        y0_ref[...] = carry[...]

    for pp in range(4):
        for r in range(4):
            src = x_ref[pp + 1, r] if pp < 3 else xn_ref[0, r]
            for j, blk in enumerate(shifted_blocks(src)):
                y_ref[pp, j, :, 128 * r : 128 * r + 128] = blk
        for j in range(3):
            lhs = jnp.concatenate([carry[j] if pp == 0 else y_ref[pp - 1, j], y_ref[pp, j]], axis=1)
            act, slope = silu_and_slope(dot(lhs, b1_ref[...]))
            act = act.astype(BF16)
            a1_ref[pp // 2, pp % 2, :, 256 * j : 256 * j + 256] = act
            a1s[2 * i + pp // 2, pp % 2, :, 256 * j : 256 * j + 256] = act
            s1_ref[pp // 2, pp % 2, :, 256 * j : 256 * j + 256] = slope.astype(BF16)
    carry[...] = y_ref[3]

    def second(p):
        for lo, hi, n0, n1 in ((0, 384, 0, 256), (256, 640, 256, 512), (512, 768, 512, 640)):
            lhs = jnp.concatenate([a1s[p + u // 2, u % 2, :, lo:hi] for u in range(4)], axis=1)
            rhs = jnp.concatenate([b2_ref[u, lo:hi, n0:n1] for u in range(4)], axis=0)
            act, slope = silu_and_slope(dot(lhs, rhs))
            act = act.astype(BF16)
            a2_ref[p, :, n0:n1] = act
            a2s[p, :, n0:n1] = act
            s2_ref[p, :, n0:n1] = slope.astype(BF16)

    def third(p, odd):
        acts, slopes = [], []
        for lo, hi, n0, n1 in ((0, 384, 0, 256), (256, 640, 256, 512)):
            lhs = jnp.concatenate([a2s[p + u, :, lo:hi] for u in range(3)], axis=1)
            rhs = jnp.concatenate([b3_ref[u, lo:hi, n0:n1] for u in range(3)], axis=0)
            act, slope = silu_and_slope(dot(lhs, rhs))
            acts.append(act)
            slopes.append(slope)
        lane = lax.broadcasted_iota(jnp.int32, (rows, 512), 1)
        base = (p // 2) * 896
        for out, parts in ((f_ref, acts), (s3_ref, slopes)):
            whole = jnp.where(lane < 448, jnp.concatenate(parts, axis=1), 0.0)
            if not odd:
                out[:, pl.ds(pl.multiple_of(base, 128), 512)] = whole.astype(BF16)
            else:
                whole = pltpu.roll(whole, 64, 1)
                at = pl.ds(pl.multiple_of(base + 384, 128), 128)
                out[:, at] = (out[:, at].astype(F32) + whole[:, :128]).astype(BF16)
                out[:, pl.ds(pl.multiple_of(base + 512, 128), 384)] = whole[:, 128:].astype(BF16)

    @pl.when(i >= 1)
    def _():
        second(2 * i - 1)

    second(2 * i)

    @pl.when(i >= 2)
    def _():
        third(2 * i - 3, True)

    @pl.when(i >= 1)
    def _():
        third(2 * i - 2, False)

    @pl.when(i == 4)
    def _():
        lane = lax.broadcasted_iota(jnp.int32, (rows, 128), 1)
        last = f_ref[:, 3072:3200].astype(F32)
        f_ref[:, 3072:3200] = jnp.where(lane == 64, 1.0, last).astype(BF16)


def full(shape):
    return pl.BlockSpec(shape, lambda *_: (0,) * len(shape))


def once(shape):
    return pl.BlockSpec(shape, lambda *_: (0,) * len(shape), pipeline_mode=pl.Buffered(1))


BANDS = [(1024, 256), (4, 768, 640), (3, 640, 512)]


def torso_forward(x, kern1, kern2, kern3):
    rows = x.shape[2]
    shapes = [(10, 2, rows, 768)] * 2 + [(9, rows, 640)] * 2 + [(rows, 3200)] * 2 + [(20, 3, rows, 512), (3, rows, 512)]
    return pl.pallas_call(
        forward_kernel,
        grid=(5,),
        in_specs=[
            pl.BlockSpec((4, 4, rows, 336), lambda i: (i, 0, 0, 0)),
            pl.BlockSpec((1, 4, rows, 336), lambda i: (4 * i + 4, 0, 0, 0)),
            once(kern1.shape),
            once(kern2.shape),
            once(kern3.shape),
        ],
        out_specs=[pl.BlockSpec((2, 2, rows, 768), lambda i: (i, 0, 0, 0))] * 2
        + [once((9, rows, 640))] * 2
        + [once((rows, 3200))] * 2
        + [pl.BlockSpec((4, 3, rows, 512), lambda i: (i, 0, 0, 0)), once((3, rows, 512))],
        out_shape=[jax.ShapeDtypeStruct(s, BF16) for s in shapes],
        scratch_shapes=[
            pltpu.VMEM((3, rows, 512), BF16),
            pltpu.VMEM((10, 2, rows, 768), BF16),
            pltpu.VMEM((9, rows, 640), BF16),
            *[pltpu.VMEM(s, BF16) for s in BANDS],
        ],
        compiler_params=pltpu.CompilerParams(vmem_limit_bytes=VMEM_LIMIT),
        name="torso_forward",
    )(x, x, kern1, kern2, kern3)


def coordinates():
    d, m = lax.axis_index("dp"), lax.axis_index("mp")
    return {"z": d // 2, "y": d % 2, "x": m // 2, "c": m % 2}


def device_at(at):
    return dict(
        device_id={"dp": at["z"] * 2 + at["y"], "mp": at["x"] * 2 + at["c"]}, device_id_type=pl.DeviceIdType.MESH
    )


AXES = {"x": 2, "z": 4, "y": 2}
HALF = 3712
SUM_FLOWS = [(0, 0, HALF, "xzy"), (1, 0, HALF, "yxz")]


def flow_buffers(flows):
    shapes = []
    for _, lo, hi, order in flows:
        for s, axis in enumerate(order):
            rest = [AXES[a] for a in AXES if a in order[s + 1 :]]
            shapes.append((AXES[axis] - 1, *rest, 16, hi - lo))
    return shapes


def peers_of(axis):
    me = coordinates()
    n = AXES[axis]
    return [{**me, axis: lax.rem(me[axis] + k, n)} for k in range(1, n)]


def block_of(ref, half, lo, hi, at):
    return ref.at[(half, *[at.get(a, slice(None)) for a in AXES], slice(None), slice(lo, hi))]


def sum_copies(acc, flow, stage, buf, send, recv):
    half, lo, hi, order = flow
    me = coordinates()
    held = {a: me[a] for a in order[:stage]}
    copies = []
    for k, peer in enumerate(peers_of(order[stage])):
        src = block_of(acc, half, lo, hi, {**held, order[stage]: peer[order[stage]]})
        copies.append(pltpu.make_async_remote_copy(src, buf.at[k], send.at[k], recv.at[k], **device_at(peer)))
    return copies


def add_arrived(acc, flow, stage, buf, out=None):
    half, lo, hi, order = flow
    me = coordinates()
    own = block_of(acc, half, lo, hi, {a: me[a] for a in order[: stage + 1]})
    total = own[...].astype(F32)
    for k in range(AXES[order[stage]] - 1):
        total = total + buf[k].astype(F32)
    if out is None:
        own[...] = total.astype(BF16)
    else:
        out[half, :, lo:hi] = total


def everyone(axis, count):
    me = lax.axis_index(axis)
    return [dict(device_id={axis: lax.rem(me + k, count)}, device_id_type=pl.DeviceIdType.MESH) for k in range(1, count)]


def share(axis, count, src, buf, send, recv):
    me = lax.axis_index(axis)
    return [
        pltpu.make_async_remote_copy(src(k), buf.at[me], send.at[k], recv.at[k], **to)
        for k, to in enumerate(everyone(axis, count))
    ]


def in_order(buf, count):
    total = buf[0].astype(F32)
    for k in range(1, count):
        total = total + buf[k].astype(F32)
    return total


def pack_kernels(d, o1, o2, o3):
    lane = lax.broadcasted_iota(jnp.int32, (32, 128), 1)
    two = jnp.where(lane < 64, o2[64 * d : 64 * d + 32, :], o2[64 * d + 32 : 64 * d + 64, :])
    three = jnp.where(lane < 64, o3[72 * d : 72 * d + 32, :], o3[72 * d + 32 : 72 * d + 64, :])
    lane = lane[:8] // 32
    one = jnp.zeros((8, 128), F32)
    for k in range(4):
        one = jnp.where(lane == k, o1[32 * d + 8 * k : 32 * d + 8 * k + 8, :], one)
    return jnp.concatenate([two, three, o3[72 * d + 64 : 72 * d + 72, :], one], axis=0)


def unpack_kernels(v, c1, c2, c3):
    c2[0:32, :] = v[0:32, 0:64]
    c2[32:64, :] = pltpu.roll(v[0:32], 64, 1)[:, 0:64]
    c3[0:32, :] = v[32:64, 0:64]
    c3[32:64, :] = pltpu.roll(v[32:64], 64, 1)[:, 0:64]
    c3[64:72, :] = v[64:72, 0:64]
    for k in range(4):
        turned = v[72:80] if k == 0 else pltpu.roll(v[72:80], 128 - 32 * k, 1)
        c1[8 * k : 8 * k + 8, :] = turned[:, 0:32]


def backward_kernel(summed, *refs):
    (y_ref, y0_ref, a1_ref, s1_ref, a2_ref, s2_ref, s3_ref, fg_ref, k2_ref, k3_ref), refs = refs[:10], refs[10:]
    if summed:
        (dw_ref, stat_ref, dsum_ref, stat_out, c1_ref, c2_ref, c3_ref), refs = refs[:7], refs[7:]
    (o1_ref, o2_ref, o3_ref), refs = refs[:3], refs[3:]
    (carry, g3, g2, b2_ref, b3_ref, d1_ref, d2a_ref, d2b_ref, d2c_ref, d3_ref), refs = refs[:10], refs[10:]
    if summed:
        (acc, core_buf, stat_dp, stat_mp, kern_send, kern_dp, kern_mp, core_sems, load_sem, sems, send_s, recv_s), bufs = refs[:12], refs[12:]
        me = coordinates()
        stages = {}
        at = 0
        for f, flow in enumerate(SUM_FLOWS):
            for s in range(3):
                stages[f, s] = (acc, flow, s, bufs[at], sems.at[0, at], sems.at[1, at])
                at += 1

        def core_copies():
            other = {**me, "c": 1 - me["c"]}
            return [
                pltpu.make_async_remote_copy(
                    dw_ref.at[h, :, 1 - me["c"]], core_buf.at[h], core_sems.at[0, h], core_sems.at[1, h], **device_at(other)
                )
                for h in range(2)
            ]

        def loads():
            return [pltpu.make_async_copy(dw_ref.at[h, :, me["c"]], acc.at[h], load_sem.at[h]) for h in range(2)]

        def stat_copies(axis, count, k):
            src = stat_ref if k == 0 else stat_mp.at[lax.axis_index("mp")]
            return share(axis, count, lambda _: src, (stat_dp, stat_mp)[k], send_s.at[k], recv_s.at[k])

        def kern_copies(axis, count, k):
            ids = [lax.rem(lax.axis_index("dp") + j, 8) for j in range(1, 8)]
            src = (lambda j: kern_send.at[ids[j]]) if k == 0 else (lambda _: kern_mp.at[lax.axis_index("mp")])
            return share(axis, count, src, (kern_dp, kern_mp)[k], send_s.at[2 + k], recv_s.at[2 + k])

        def start(copies):
            for copy in copies:
                copy.start()

        def finish(copies):
            for copy in copies:
                copy.wait()

        def first():
            barrier = pltpu.get_barrier_semaphore()
            ids = everyone("dp", 8) + everyone("mp", 4)
            for to in ids:
                pl.semaphore_signal(barrier, inc=1, **to)
            pl.semaphore_wait(barrier, len(ids))
            start(core_copies())
            start(loads())
            start(stat_copies("dp", 8, 0))
            stat_dp[lax.axis_index("dp")] = stat_ref[...]

        def after_core():
            finish(loads())
            finish(core_copies())
            for h in range(2):

                def one(j, _):
                    at = (h, j // 8, (j // 2) % 4, j % 2)
                    acc[at] = (acc[at].astype(F32) + core_buf[at].astype(F32)).astype(BF16)
                    return 0

                lax.fori_loop(0, 16, one, 0)
            for f in range(2):
                start(sum_copies(*stages[f, 0]))
            finish(stat_copies("dp", 8, 0))
            stat_mp[lax.axis_index("mp")] = in_order(stat_dp, 8)
            start(stat_copies("mp", 4, 1))

        def next_stage(f, s):
            finish(sum_copies(*stages[f, s]))
            add_arrived(*stages[f, s][:4], out=dsum_ref if s == 2 else None)
            if s < 2:
                start(sum_copies(*stages[f, s + 1]))

        def stats_done():
            finish(stat_copies("mp", 4, 1))
            stat_out[...] = in_order(stat_mp, 4)

        def kernels_out():
            for d in range(8):
                kern_send[d] = pack_kernels(d, o1_ref, o2_ref, o3_ref).astype(BF16)
            kern_dp[lax.axis_index("dp")] = kern_send[lax.axis_index("dp")]
            start(kern_copies("dp", 8, 0))

        def kernels_over():
            finish(kern_copies("dp", 8, 0))
            kern_mp[lax.axis_index("mp")] = in_order(kern_dp, 8)
            start(kern_copies("mp", 4, 1))

        def kernels_done():
            finish(kern_copies("mp", 4, 1))
            total = in_order(kern_mp, 4) / stat_out[9:10, :]
            unpack_kernels(total, c1_ref, c2_ref, c3_ref)

    i = pl.program_id(0)
    rows = y_ref.shape[2]

    @pl.when(i == 0)
    def _():
        if summed:
            first()
        fill_band_two(k2_ref, b2_ref)
        fill_band_three(k3_ref, b3_ref)
        for at in (0, 1, 9, 10):
            g3[at] = jnp.zeros((rows, 512), BF16)
        for at in (0, 10):
            g2[at] = jnp.zeros((rows, 640), BF16)
        lane = lax.broadcasted_iota(jnp.int32, (rows, 512), 1)
        for p in range(7):
            base = (p // 2) * 896 + (384 if p % 2 else 0)
            both = fg_ref[:, base : base + 512].astype(F32) * s3_ref[:, base : base + 512].astype(F32)
            if p % 2:
                both = pltpu.roll(both, 448, 1)
            g3[p + 2] = jnp.where(lane < 448, both, 0.0).astype(BF16)
        for u in range(3):
            total = 0.0
            for m in range(2):
                lhs = a2_ref[u : u + 7, :, 256 * m : 256 * m + 384].reshape(7 * rows, 384)
                rhs = g3[2:9, :, 256 * m : 256 * m + 256].reshape(7 * rows, 256)
                total = total + dot_tn(lhs, rhs)
            d3_ref[u] = total
        if summed:
            after_core()
        d1_ref[...] = jnp.zeros_like(d1_ref)
        d2a_ref[...] = jnp.zeros_like(d2a_ref)
        d2b_ref[...] = jnp.zeros_like(d2b_ref)
        d2c_ref[...] = jnp.zeros_like(d2c_ref)
        for lo, hi, n0, n1 in ((0, 256, 0, 256), (256, 512, 128, 512), (512, 640, 384, 512)):
            rhs = jnp.concatenate([b3_ref[u, lo:hi, n0:n1] for u in range(3)], axis=1)

            def one(p, _):
                lhs = jnp.concatenate([g3[p + 2 - u, :, n0:n1] for u in range(3)], axis=1)
                back = dot_nt(lhs, rhs) * s2_ref[p, :, lo:hi].astype(F32)
                g2[p + 1, :, lo:hi] = back.astype(BF16)
                return 0

            lax.fori_loop(0, 9, one, 0)

    for r in range(2):
        for t in range(2):
            for ref, lo, hi, n0, n1 in ((d2a_ref, 0, 384, 0, 256), (d2b_ref, 256, 640, 256, 512), (d2c_ref, 512, 768, 512, 640)):
                lhs = a1_ref[:, r, :, lo:hi].reshape(2 * rows, hi - lo)
                rhs = g2[pl.ds(2 * i + 1 - t, 2), :, n0:n1].reshape(2 * rows, n1 - n0)
                ref[2 * t + r] += dot_tn(lhs, rhs)

    @pl.when(i == 0)
    def _():
        carry[...] = y0_ref[...]

    for j, (n0, n1) in enumerate(((0, 256), (128, 512), (384, 640))):
        grads = []
        for pp in range(4):
            r = pp % 2
            at = 2 * i + pp // 2 + 1
            lhs = jnp.concatenate([g2[at, :, n0:n1], g2[at - 1, :, n0:n1]], axis=1)
            rhs = jnp.concatenate([b2_ref[r, 256 * j : 256 * j + 256, n0:n1], b2_ref[2 + r, 256 * j : 256 * j + 256, n0:n1]], axis=1)
            back = dot_nt(lhs, rhs) * s1_ref[pp // 2, r, :, 256 * j : 256 * j + 256].astype(F32)
            grads.append(back.astype(BF16))
        grad = jnp.concatenate(grads, axis=0)
        for t in range(2):
            pieces = [y_ref[k - 1 + t, j] if k + t > 0 else carry[j] for k in range(4)]
            lhs = jnp.concatenate(pieces, axis=0)
            d1_ref[512 * t : 512 * t + 512, :] += dot_tn(lhs, grad)
    carry[...] = y_ref[3]

    if summed:

        @pl.when(i == 2)
        def _():
            stats_done()
            next_stage(0, 0)
            next_stage(1, 0)

        @pl.when(i == 3)
        def _():
            next_stage(1, 1)

    @pl.when(i == 4)
    def _():
        if summed:
            next_stage(0, 1)
        take_band_one(d1_ref, o1_ref)
        take_band_two(((d2a_ref, 0, 0, 4), (d2b_ref, 8, 4, 4), (d2c_ref, 16, 8, 1)), o2_ref)
        take_band_three(d3_ref, o3_ref)
        if summed:
            kernels_out()
            next_stage(1, 2)
            next_stage(0, 2)
            kernels_over()
            kernels_done()


def torso_backward(y, y0, a1, s1, a2, s2, s3, fg, kern2, kern3, summed=None):
    rows = y.shape[2]
    sums = [(1024, 256), (4, 384, 256), (4, 384, 256), (4, 256, 128), (3, 384, 256)]
    own = [(256, 128), (512, 128), (576, 128)]
    args = [y, y0, a1, s1, a2, s2, s3, fg, kern2, kern3]
    in_specs = [
        pl.BlockSpec((4, 3, rows, 512), lambda i: (i, 0, 0, 0)),
        once(y0.shape),
        pl.BlockSpec((2, 2, rows, 768), lambda i: (i, 0, 0, 0)),
        pl.BlockSpec((2, 2, rows, 768), lambda i: (i, 0, 0, 0)),
        *[once(v.shape) for v in args[4:]],
    ]
    scratch = [
        pltpu.VMEM((3, rows, 512), BF16),
        pltpu.VMEM((11, rows, 512), BF16),
        pltpu.VMEM((11, rows, 640), BF16),
        *[pltpu.VMEM(s, BF16) for s in BANDS[1:]],
        *[pltpu.VMEM(s, F32) for s in sums],
    ]
    outs = own
    params = {}
    if summed is not None:
        args += summed
        in_specs += [pl.BlockSpec(memory_space=pl.ANY), once((16, 128))]
        outs = [(2, 16, HALF), (16, 128), (32, 32), (64, 64), (72, 64)]
        buffers = flow_buffers(SUM_FLOWS)
        scratch = [pltpu.VMEM(s, F32) for s in own] + scratch
        scratch += [
            pltpu.VMEM((2, *AXES.values(), 16, HALF), BF16),
            pltpu.VMEM((2, *AXES.values(), 16, HALF), BF16),
            pltpu.VMEM((8, 16, 128), F32),
            pltpu.VMEM((4, 16, 128), F32),
            pltpu.VMEM((8, 80, 128), BF16),
            pltpu.VMEM((8, 80, 128), BF16),
            pltpu.VMEM((4, 80, 128), F32),
            pltpu.SemaphoreType.DMA((2, 2)),
            pltpu.SemaphoreType.DMA((2,)),
            pltpu.SemaphoreType.DMA((2, len(buffers), 3)),
            pltpu.SemaphoreType.DMA((4, 7)),
            pltpu.SemaphoreType.DMA((4, 7)),
            *[pltpu.VMEM(s, BF16) for s in buffers],
        ]
        params = dict(collective_id=1, has_side_effects=True)
    return pl.pallas_call(
        functools.partial(backward_kernel, summed is not None),
        grid=(5,),
        in_specs=in_specs,
        out_specs=[once(s) for s in outs],
        out_shape=[jax.ShapeDtypeStruct(s, F32) for s in outs],
        scratch_shapes=scratch,
        compiler_params=pltpu.CompilerParams(vmem_limit_bytes=VMEM_LIMIT, **params),
        name="torso_backward",
    )(*args)


def high_low(v):
    high = v.astype(BF16)
    return high, (v - high.astype(F32)).astype(BF16)


def heads_kernel(
    atoms, acts, f_ref, w_ref, bias_ref, slot_ref, col_ref, row_ref, dw_ref, fg_ref, prio_ref, stat_ref
):
    rows = f_ref.shape[0]
    slots = slot_ref.shape[0]
    feats = f_ref[...]
    pre = [dot_nt(feats, w_ref[k, :, :3200]) for k in range(2)]
    hidden, slope = [], []
    for k in range(2):
        a, s = silu_and_slope(pre[k])
        hidden.append(a.astype(BF16))
        slope.append(s)
    out_w = jnp.concatenate([w_ref[0, :, 3200:], w_ref[1, :, 3200:]], axis=1)
    wide = out_w.shape[1]
    lane = lax.broadcasted_iota(jnp.int32, (1, wide), 1)
    zero = jnp.zeros((), BF16)
    w_val = jnp.where(lane[:, :128] < atoms, out_w[:, :128].astype(F32), 0.0).astype(BF16)
    w_adv = jnp.where(lane >= atoms, out_w.astype(F32), 0.0).astype(BF16)
    logits = dot(hidden[1], w_adv) + bias_ref[...]
    logits = jnp.concatenate([logits[:, :128] + dot(hidden[0], w_val), logits[:, 128:]], axis=1)
    high, low = high_low(logits)
    sel = jnp.where(lax.broadcasted_iota(jnp.int32, (slots, rows), 1) == col_ref[...], 1.0, 0.0).astype(BF16)
    selt = jnp.where(lax.broadcasted_iota(jnp.int32, (rows, slots), 0) == row_ref[...], 1.0, 0.0).astype(BF16)
    per_slot = dot(sel, high) + dot(sel, low)
    action = slot_ref[:, atoms + 2 : atoms + 3]
    which = jnp.where(lane < atoms, -1, jnp.where(lane < atoms * (acts + 1), (lane - atoms) // atoms, -2)).astype(F32)
    coeff = jnp.where(which == -1.0, 1.0, 0.0) + jnp.where(which == action, 1.0, 0.0) - jnp.where(which >= 0.0, 1.0 / acts, 0.0)
    atom = jnp.where(which >= -1.0, lane - atoms * (which.astype(jnp.int32) + 1), -1)
    fold = jnp.where(lax.broadcasted_iota(jnp.int32, (128, wide), 0) == atom, 1.0, 0.0).astype(BF16)
    high, low = high_low(per_slot * coeff)
    q = dot_nt(high, fold) + dot_nt(low, fold)
    lane_q = lax.broadcasted_iota(jnp.int32, (slots, 128), 1)
    used = lane_q < atoms
    top = jnp.max(jnp.where(used, q, -jnp.inf), axis=1, keepdims=True)
    shifted = jnp.where(used, jnp.exp(jnp.where(used, q - top, 0.0)), 0.0)
    total = jnp.sum(shifted, axis=1, keepdims=True)
    tgt = jnp.where(used, slot_ref[...], 0.0)
    cross = -jnp.sum(jnp.where(used, tgt * (q - top - jnp.log(total)), 0.0), axis=1, keepdims=True)
    coef = slot_ref[:, atoms : atoms + 1]
    valid = slot_ref[:, atoms + 1 : atoms + 2]
    prio_ref[...] = valid * cross
    q_grad = coef * (shifted * (jnp.sum(tgt, axis=1, keepdims=True) / total) - tgt)
    high, low = high_low(q_grad)
    lgrad = ((dot(high, fold) + dot(low, fold)) * coeff).astype(BF16)
    bias_grad = jnp.sum(lgrad.astype(F32), axis=0, keepdims=True)
    for k in range(8):
        stat_ref[k : k + 1, :] = bias_grad[:, 128 * k : 128 * k + 128]
    stat_ref[8:9, :] = jnp.broadcast_to(jnp.sum(coef * cross, axis=0, keepdims=True), (1, 128))
    stat_ref[9:10, :] = jnp.broadcast_to(jnp.sum(valid, axis=0, keepdims=True), (1, 128))
    stat_ref[10:16, :] = jnp.zeros((6, 128), F32)
    grad = dot(selt, lgrad).astype(BF16)
    d_adv = dot_tn(hidden[1], grad)
    d_val = dot_tn(hidden[0], grad[:, :128])
    dw_ref[0, :, 3200:3328] = jnp.where(lane[:, :128] < atoms, d_val, d_adv[:, :128]).astype(BF16)
    dw_ref[0, :, 3328:] = d_adv[:, 128:512].astype(BF16)
    dw_ref[1, :, 3200:] = d_adv[:, 512:].astype(BF16)
    pre_grad = [
        (dot_nt(grad[:, :128], w_val) * slope[0]).astype(BF16),
        (dot_nt(grad, w_adv) * slope[1]).astype(BF16),
    ]
    for k in range(2):
        for lo, hi in ((0, 1024), (1024, 2048), (2048, 3200)):
            dw_ref[k, :, lo:hi] = dot_tn(pre_grad[k], f_ref[:, lo:hi]).astype(BF16)
    for lo, hi in ((0, 1024), (1024, 2048), (2048, 3200)):
        back = dot(pre_grad[0], w_ref[0, :, lo:hi]) + dot(pre_grad[1], w_ref[1, :, lo:hi])
        fg_ref[:, lo:hi] = back.astype(BF16)


def heads(atoms, acts, feats, weights, bias, per_slot, rows_of_slot):
    slots = per_slot.shape[0]
    return pl.pallas_call(
        functools.partial(heads_kernel, atoms, acts),
        out_shape=[
            jax.ShapeDtypeStruct(weights.shape, BF16),
            jax.ShapeDtypeStruct(feats.shape, BF16),
            jax.ShapeDtypeStruct((slots, 1), F32),
            jax.ShapeDtypeStruct((16, 128), F32),
        ],
        compiler_params=pltpu.CompilerParams(vmem_limit_bytes=VMEM_LIMIT),
        name="heads",
    )(feats, weights, bias, per_slot, rows_of_slot[:, None], rows_of_slot[None, :])


def exchange_kernel(count, kern_ref, slot_ref, kerns_out, slots_out, send_kern, recv_kern, send_slot, recv_slot, own):
    me = lax.axis_index("dp")
    peers = [lax.rem(me + k, count) for k in range(count)]
    barrier = pltpu.get_barrier_semaphore()
    for k in range(1, count):
        pl.semaphore_signal(barrier, inc=1, device_id={"dp": peers[k]}, device_id_type=pl.DeviceIdType.MESH)
    pl.semaphore_wait(barrier, count - 1)
    mine = [
        pltpu.make_async_copy(kern_ref, kerns_out.at[me], own.at[0]),
        pltpu.make_async_copy(slot_ref.at[me], slots_out.at[me], own.at[1]),
    ]
    sent = []
    for k in range(1, count):
        to = dict(device_id={"dp": peers[k]}, device_id_type=pl.DeviceIdType.MESH)
        sent.append(pltpu.make_async_remote_copy(kern_ref, kerns_out.at[me], send_kern.at[k], recv_kern.at[k], **to))
        sent.append(pltpu.make_async_remote_copy(slot_ref.at[peers[k]], slots_out.at[me], send_slot.at[k], recv_slot.at[k], **to))
    for copy in mine + sent:
        copy.start()
    for copy in mine + sent:
        copy.wait()


def exchange(kern, slot):
    count = slot.shape[0]
    return pl.pallas_call(
        functools.partial(exchange_kernel, count),
        in_specs=[pl.BlockSpec(memory_space=pltpu.VMEM)] * 2,
        out_specs=[pl.BlockSpec(memory_space=pltpu.VMEM)] * 2,
        out_shape=[jax.ShapeDtypeStruct((count, *kern.shape), kern.dtype), jax.ShapeDtypeStruct(slot.shape, slot.dtype)],
        scratch_shapes=[pltpu.SemaphoreType.DMA((count,))] * 4 + [pltpu.SemaphoreType.DMA((2,))],
        compiler_params=pltpu.CompilerParams(collective_id=0, has_side_effects=True, vmem_limit_bytes=VMEM_LIMIT),
        name="exchange",
    )(kern, slot)


def on_device(
    frames,
    send_rows,
    recv_counts,
    actions,
    target_dist,
    sample_weight,
    conv_first,
    conv_second,
    conv_third,
    hidden_mean,
    hidden_spread,
    hidden_bias,
    feature_noise,
    hidden_noise,
    value_mean,
    value_spread,
    advantage_mean,
    advantage_spread,
    output_noise,
    output_bias,
):
    dp_count = lax.axis_size("dp")
    slots = send_rows.shape[0]
    capacity = slots // dp_count
    atoms = value_mean.shape[1]
    acts = advantage_mean.shape[1] // atoms
    rows = frames.shape[0]
    feat, own = hidden_mean.shape[1:]
    outs = atoms * (acts + 1)

    sizes = [w.size for w in (conv_first, conv_second, conv_third)]
    flat = jnp.concatenate([w.astype(BF16).reshape(-1) for w in (conv_first, conv_second, conv_third)])
    tall = -(-flat.size // 2048) * 16
    flat = jnp.pad(flat, (0, tall * 128 - flat.size)).reshape(tall, 128)
    is_valid = jnp.arange(capacity, dtype=jnp.int32)[None, :] < recv_counts[:, None]
    is_valid = is_valid.astype(F32).reshape(slots)
    per_slot = jnp.stack([is_valid * sample_weight, is_valid, actions.astype(F32)], axis=1)
    per_slot = jnp.concatenate([target_dist, per_slot, jnp.zeros((slots, 125 - atoms), F32)], axis=1)
    flat, per_slot = exchange(flat, per_slot.reshape(dp_count, capacity, 128))
    per_slot = per_slot.reshape(slots, 128)
    flat = flat.reshape(dp_count, -1)
    kern1 = jnp.tile(flat[:, : sizes[0]].reshape(-1, 32), (1, 4))
    kern2 = jnp.tile(flat[:, sizes[0] : sizes[0] + sizes[1]].reshape(-1, 64), (1, 2))
    kern3 = jnp.tile(flat[:, sizes[0] + sizes[1] : sum(sizes)].reshape(-1, 64), (1, 2))

    mean_t = hidden_mean.transpose(0, 2, 1)
    spread_t = hidden_spread.transpose(0, 2, 1)
    wide_one = mean_t + spread_t * feature_noise[:, None, :] * hidden_noise[0][:, :, None]
    wide_one = jnp.concatenate([wide_one, hidden_bias[:, :, None], jnp.zeros((2, own, 63), F32)], axis=2)
    wide_val = value_mean + value_spread * hidden_noise[1, 0][:, None] * output_noise[None, :atoms]
    wide_adv = advantage_mean + advantage_spread * hidden_noise[1, 1][:, None] * output_noise[None, atoms:]
    wide_out = jnp.concatenate([wide_val, wide_adv, jnp.zeros((own, 1024 - outs), F32)], axis=1)
    wide_out = wide_out.reshape(own, 2, 512).transpose(1, 0, 2)
    shard = jnp.concatenate([wide_one, wide_out], axis=2).astype(BF16)
    weights = lax.all_gather(shard, ("mp", "dp"), axis=1, tiled=True)

    x = frames.transpose(1, 0, 2).reshape(21, 4, rows, 336)
    a1, s1, a2, s2, feats, s3, y, y0 = torso_forward(x, kern1, kern2, kern3)
    bias = jnp.pad(output_bias, (0, 1024 - outs))[None, :]
    dweights, feat_grad, prio, stat = heads(atoms, acts, feats, weights, bias, per_slot, send_rows)
    torso = (y, y0, a1, s1, a2, s2, s3, feat_grad, kern2, kern3)
    if (dp_count, lax.axis_size("mp"), own) == (8, 4, 16):
        summed = [dweights.reshape(2, 2, 2, 4, 2, own, HALF), stat]
        dshard, stat, *conv_grads = torso_backward(*torso, summed=summed)
        inverse = 1.0 / stat[9, 0]
    else:
        dshard = lax.psum_scatter(dweights, ("mp", "dp"), scatter_dimension=1, tiled=True).astype(F32)
        stat = lax.psum(stat, ("dp", "mp"))
        inverse = 1.0 / stat[9, 0]
        k1, k2, k3 = torso_backward(*torso)
        kflat = jnp.concatenate([g.reshape(dp_count, -1) for g in (k1[:, :32], k2[:, :64], k3[:, :64])], axis=1)
        kflat = lax.psum(lax.psum_scatter(kflat, "dp", scatter_dimension=0, tiled=True)[0], "mp") * inverse
        conv_grads = (
            kflat[: sizes[0]].reshape(conv_first.shape),
            kflat[sizes[0] : sizes[0] + sizes[1]].reshape(conv_second.shape),
            kflat[sizes[0] + sizes[1] :].reshape(conv_third.shape),
        )

    dshard = dshard * inverse
    mean_grad_t = dshard[:, :, :feat]
    spread_grad_t = mean_grad_t * feature_noise[:, None, :] * hidden_noise[0][:, :, None]
    out_grad = dshard[:, :, 3200:].transpose(1, 0, 2).reshape(own, 1024)
    value_mean_grad = out_grad[:, :atoms]
    adv_mean_grad = out_grad[:, atoms:outs]
    return (
        stat[8, 0] * inverse,
        *conv_grads,
        mean_grad_t.transpose(0, 2, 1),
        spread_grad_t.transpose(0, 2, 1),
        dshard[:, :, feat],
        value_mean_grad,
        value_mean_grad * hidden_noise[1, 0][:, None] * output_noise[None, :atoms],
        adv_mean_grad,
        adv_mean_grad * hidden_noise[1, 1][:, None] * output_noise[None, atoms:],
        stat[:8].reshape(-1)[:outs] * inverse,
        prio[:, 0],
    )


def solution(mesh):
    both, heads_dim = P(("dp", "mp")), P(("mp", "dp"), None)
    return jax.shard_map(
        on_device,
        mesh=mesh,
        in_specs=(
            P(("dp", "mp"), None, None),
            both,
            both,
            both,
            P(("dp", "mp"), None),
            both,
            P("dp", None),
            P("dp", None),
            P("dp", None),
            P(None, None, ("mp", "dp")),
            P(None, None, ("mp", "dp")),
            P(None, ("mp", "dp")),
            P(),
            P(None, None, ("mp", "dp")),
            heads_dim,
            heads_dim,
            heads_dim,
            heads_dim,
            P(),
            P(),
        ),
        out_specs=(
            P(),
            P("dp", None),
            P("dp", None),
            P("dp", None),
            P(None, None, ("mp", "dp")),
            P(None, None, ("mp", "dp")),
            P(None, ("mp", "dp")),
            heads_dim,
            heads_dim,
            heads_dim,
            heads_dim,
            P(),
            both,
        ),
        check_vma=False,
    )
```

```python
import functools

import jax
import jax.numpy as jnp
from jax import lax
from jax.experimental import pallas as pl
from jax.experimental.pallas import tpu as pltpu
from jax.sharding import PartitionSpec as P

F32 = jnp.float32
BF16 = jnp.bfloat16
VMEM_LIMIT = 60 * 1024 * 1024


def sigmoid(v):
    return 0.5 * jnp.tanh(0.5 * v) + 0.5


def silu_and_slope(v):
    s = sigmoid(v)
    a = v * s
    return a, s + a * (1.0 - s)


def dot(a, b):
    return lax.dot_general(a, b, (((1,), (0,)), ((), ())), preferred_element_type=F32)


def dot_nt(a, b):
    return lax.dot_general(a, b, (((1,), (1,)), ((), ())), preferred_element_type=F32)


def dot_tn(a, b):
    return lax.dot_general(a, b, (((0,), (0,)), ((), ())), preferred_element_type=F32)


def columns_of_one():
    return [7 * (g // 8) + g % 8 if g % 8 < 7 and 7 * (g // 8) + g % 8 < 20 else -9 for g in range(24)]


def half_lanes(left, right, rows):
    lane = lax.broadcasted_iota(jnp.int32, (rows, 128), 1)
    zero = jnp.zeros((rows, 128), F32)
    return jnp.where(lane < 64, zero if left is None else left, zero if right is None else right)


def fill_band_one(k1_ref, band):
    lane = lax.broadcasted_iota(jnp.int32, (16, 128), 1) // 32
    for u in range(8):
        taps = [k1_ref[((u // 4) * 2 + v) * 64 + (u % 4) * 16 :][:16].astype(F32) for v in range(2)]
        for g in range(8):
            for h in range(2):
                col = lane + 4 * h
                here = jnp.where((col == g) & (col < 7), taps[0], 0.0) + jnp.where((col == g - 1) & (col < 7), taps[1], 0.0)
                band[128 * u + 16 * g : 128 * u + 16 * g + 16, 128 * h : 128 * h + 128] = here.astype(BF16)


def fill_band_two(k2_ref, band):
    cols = columns_of_one()
    for u in range(4):

        def tap(v):
            at = ((u // 2) * 2 + v // 2) * 128 + ((u % 2) * 2 + v % 2) * 32
            return k2_ref[at : at + 32, :].astype(F32)

        for g, q in enumerate(cols):
            if q < 0:
                continue
            used = {(q - v) // 2: v for v in (q % 2, q % 2 + 2) if 0 <= (q - v) // 2 < 9}
            for m in sorted({c // 2 for c in used}):
                sides = [tap(used[2 * m + side]) if 2 * m + side in used else None for side in range(2)]
                band[u, 32 * g : 32 * g + 32, 128 * m : 128 * m + 128] = half_lanes(*sides, 32).astype(BF16)


def fill_band_three(k3_ref, band):
    for u in range(3):

        def tap(v):
            return k3_ref[(u * 3 + v) * 64 : (u * 3 + v) * 64 + 64, :].astype(F32)

        for q in range(9):
            used = {q - v: v for v in range(3) if 0 <= q - v < 7}
            for m in sorted({c // 2 for c in used}):
                sides = [tap(used[2 * m + side]) if 2 * m + side in used else None for side in range(2)]
                band[u, 64 * q : 64 * q + 64, 128 * m : 128 * m + 128] = half_lanes(*sides, 64).astype(BF16)


def fold_lanes(v, width):
    step = 64
    while step >= width:
        v = v + pltpu.roll(v, step, 1)
        step //= 2
    return v


def take_band_one(d1, out):
    lane = lax.broadcasted_iota(jnp.int32, (16, 128), 1) // 32
    for u in range(8):
        for v in range(2):
            total = jnp.zeros((16, 128), F32)
            for col in range(7):
                at = 128 * u + 16 * (col + v)
                h = col // 4
                total = total + jnp.where(lane + 4 * h == col, d1[at : at + 16, 128 * h : 128 * h + 128], 0.0)
            at = ((u // 4) * 2 + v) * 64 + (u % 4) * 16
            out[at : at + 16, :] = fold_lanes(total, 32)


def take_band_two(blocks, out):
    cols = columns_of_one()
    lane = lax.broadcasted_iota(jnp.int32, (32, 128), 1)
    for u in range(4):
        for v in range(4):
            total = jnp.zeros((32, 128), F32)
            for ref, first, c0, count in blocks:
                for c in range(count):
                    at = 32 * (cols.index(2 * (c0 + c) + v) - first)
                    piece = ref[u, at : at + 32, 128 * (c // 2) : 128 * (c // 2) + 128]
                    total = total + jnp.where((lane < 64) == (c % 2 == 0), piece, 0.0)
            at = ((u // 2) * 2 + v // 2) * 128 + ((u % 2) * 2 + v % 2) * 32
            out[at : at + 32, :] = fold_lanes(total, 64)


def take_band_three(d3, out):
    lane = lax.broadcasted_iota(jnp.int32, (64, 128), 1)
    for u in range(3):
        for v in range(3):
            total = jnp.zeros((64, 128), F32)
            for c in range(4):
                piece = d3[u, 64 * (c + v) : 64 * (c + v) + 64, 128 * (c // 2) : 128 * (c // 2) + 128]
                total = total + jnp.where((lane < 64) == (c % 2 == 0), piece, 0.0)
            at = (u * 3 + v) * 64
            out[at : at + 64, :] = fold_lanes(total, 64)


def coordinates():
    d, m = lax.axis_index("dp"), lax.axis_index("mp")
    return {"z": d // 2, "y": d % 2, "x": m // 2, "c": m % 2}


def device_at(at):
    return dict(
        device_id={"dp": at["z"] * 2 + at["y"], "mp": at["x"] * 2 + at["c"]}, device_id_type=pl.DeviceIdType.MESH
    )


AXES = {"x": 2, "z": 4, "y": 2}
HALF = 3712
CUT = 1536
SUM_FLOWS = [(0, 0, CUT, "xzy"), (1, 0, CUT, "yzx"), (0, CUT, HALF, "xyz"), (1, CUT, HALF, "yxz")]
GATHER_FLOWS = [(half, lo, hi, order[::-1]) for half, lo, hi, order in SUM_FLOWS]


def flow_buffers(flows):
    shapes = []
    for _, lo, hi, order in flows:
        for s, axis in enumerate(order):
            rest = [AXES[a] for a in AXES if a in order[s + 1 :]]
            shapes.append((AXES[axis] - 1, *rest, 16, hi - lo))
    return shapes


def peers_of(axis):
    me = coordinates()
    n = AXES[axis]
    return [{**me, axis: lax.rem(me[axis] + k, n)} for k in range(1, n)]


def block_of(ref, half, lo, hi, at):
    return ref.at[(half, *[at.get(a, slice(None)) for a in AXES], slice(None), slice(lo, hi))]


def sum_copies(acc, flow, stage, buf, send, recv):
    half, lo, hi, order = flow
    me = coordinates()
    held = {a: me[a] for a in order[:stage]}
    copies = []
    for k, peer in enumerate(peers_of(order[stage])):
        src = block_of(acc, half, lo, hi, {**held, order[stage]: peer[order[stage]]})
        copies.append(pltpu.make_async_remote_copy(src, buf.at[k], send.at[k], recv.at[k], **device_at(peer)))
    return copies


def add_arrived(acc, flow, stage, buf, out=None):
    half, lo, hi, order = flow
    me = coordinates()
    own = block_of(acc, half, lo, hi, {a: me[a] for a in order[: stage + 1]})
    total = own[...].astype(F32)
    for k in range(AXES[order[stage]] - 1):
        total = total + buf[k].astype(F32)
    if out is None:
        own[...] = total.astype(BF16)
    else:
        out[half, :, lo:hi] = total


def everyone(axis, count):
    me = lax.axis_index(axis)
    return [dict(device_id={axis: lax.rem(me + k, count)}, device_id_type=pl.DeviceIdType.MESH) for k in range(1, count)]


def share(axis, count, src, buf, send, recv):
    me = lax.axis_index(axis)
    return [
        pltpu.make_async_remote_copy(src(k), buf.at[me], send.at[k], recv.at[k], **to)
        for k, to in enumerate(everyone(axis, count))
    ]


def in_order(buf, count):
    total = buf[0].astype(F32)
    for k in range(1, count):
        total = total + buf[k].astype(F32)
    return total


def gathered_block(ref, half, lo, hi, core, at):
    x, z, y = (at.get(a, slice(None)) for a in AXES)
    return ref.at[half, x, core, z, y, :, lo:hi]


def gather_copies(shard, out, flow, stage, send, recv):
    half, lo, hi, order = flow
    me = coordinates()
    at = {a: me[a] for a in order[stage:]}
    dst = gathered_block(out, half, lo, hi, me["c"], at)
    src = shard.at[half, :, lo:hi] if stage == 0 else dst
    return [
        pltpu.make_async_remote_copy(src, dst, send.at[k], recv.at[k], **device_at(peer))
        for k, peer in enumerate(peers_of(order[stage]))
    ]


def core_copy(out, flow, last, send, recv):
    half, lo, hi, order = flow
    me = coordinates()
    axis = order[2]
    block = gathered_block(out, half, lo, hi, me["c"], {axis: 1 - me[axis] if last else me[axis]})
    other = {**me, "c": 1 - me["c"]}
    return pltpu.make_async_remote_copy(block, block, send, recv, **device_at(other))


def start(copies):
    for copy in copies:
        copy.start()


def finish(copies):
    for copy in copies:
        copy.wait()


def greet():
    for to in everyone("dp", 8) + everyone("mp", 4):
        pl.semaphore_signal(pltpu.get_barrier_semaphore(), inc=1, **to)


def greeted():
    pl.semaphore_wait(pltpu.get_barrier_semaphore(), 10)


def as_column(row):
    n = row.shape[1]
    eye = lax.broadcasted_iota(jnp.int32, (n, n), 0) == lax.broadcasted_iota(jnp.int32, (n, n), 1)
    return jnp.sum(jnp.where(eye, row, 0.0), axis=1, keepdims=True)


def as_row(column):
    n = column.shape[0]
    eye = lax.broadcasted_iota(jnp.int32, (n, n), 0) == lax.broadcasted_iota(jnp.int32, (n, n), 1)
    return jnp.sum(jnp.where(eye, column, 0.0), axis=0, keepdims=True)


def pack_shards(c1, c2, c3t):
    c3 = jnp.transpose(jnp.concatenate([c3t, jnp.zeros((64, 56), F32)], axis=1))
    blank = jnp.zeros((8, 64), F32)
    return jnp.concatenate(
        [
            jnp.concatenate([c2[0:32], c2[32:64]], axis=1),
            jnp.concatenate([c3[0:32], c3[32:64]], axis=1),
            jnp.concatenate([c3[64:72], blank], axis=1),
            jnp.concatenate([c1[8 * k : 8 * k + 8] for k in range(4)], axis=1),
        ],
        axis=0,
    )


def unpack_shards(d, v, k1, k2, k3):
    lane = lax.broadcasted_iota(jnp.int32, (32, 128), 1)

    def sides(w):
        turned = pltpu.roll(w, 64, 1)
        low = lane[: w.shape[0]] < 64
        return jnp.where(low, w, turned), jnp.where(low, turned, w)

    k2[64 * d : 64 * d + 32, :], k2[64 * d + 32 : 64 * d + 64, :] = sides(v[0:32])
    k3[72 * d : 72 * d + 32, :], k3[72 * d + 32 : 72 * d + 64, :] = sides(v[32:64])
    k3[72 * d + 64 : 72 * d + 72, :] = sides(v[64:72])[0]
    for k in range(4):
        part = jnp.where(lane[:8] // 32 == k, v[72:80], 0.0)
        k1[32 * d + 8 * k : 32 * d + 8 * k + 8, :] = fold_lanes(part, 32)


def noisy_weights(shard, hm, hs, hb, fn, hn, vm, vs, am, adv_s, on):
    atoms, outs = vm.shape[1], on.shape[1]
    lane = lax.broadcasted_iota(jnp.int32, (16, 128), 1)
    for h in range(2):
        wide = hm[h] + hs[h] * fn[h : h + 1, :] * as_column(hn[0, h : h + 1, :])
        shard[h, :, 0:3072] = wide[:, 0:3072].astype(BF16)
        last = jnp.concatenate([wide[:, 3072:], jnp.zeros((16, 64), F32)], axis=1)
        last = jnp.where(lane == 64, as_column(hb[h : h + 1, :]), last)
        shard[h, :, 3072:3200] = last.astype(BF16)
    val = vm[...] + vs[...] * as_column(hn[1, 0:1, :]) * on[:, :atoms]
    adv = am[...] + adv_s[...] * as_column(hn[1, 1:2, :]) * on[:, atoms:]
    out = jnp.concatenate([val, adv, jnp.zeros((16, 1024 - outs), F32)], axis=1).astype(BF16)
    shard[0, :, 3200:] = out[:, :512]
    shard[1, :, 3200:] = out[:, 512:]


def slot_rows(staged, tt, cnt, act, sw):
    atoms, slots = tt.shape
    lane = lax.broadcasted_iota(jnp.int32, (8, slots), 1)
    source = lax.broadcasted_iota(jnp.int32, (8, slots), 0)
    cap = slots // 8
    used = jnp.sum(jnp.where(lane // cap == source, as_column(cnt[...].astype(F32)), 0.0), axis=0, keepdims=True)
    valid = jnp.where((lane[0:1] % cap).astype(F32) < used, 1.0, 0.0)
    staged[...] = jnp.zeros_like(staged)
    staged[0:atoms, :] = tt[...]
    staged[atoms : atoms + 1, :] = valid * sw[...]
    staged[atoms + 1 : atoms + 2, :] = valid
    staged[atoms + 2 : atoms + 3, :] = act[...].astype(F32)
    return jnp.transpose(staged[...])


def shifted_blocks(x):
    rows = x.shape[0]
    return (
        x[:, 0:128],
        x[:, 112:240],
        jnp.concatenate([x[:, 224:336], jnp.zeros((rows, 16), x.dtype)], axis=1),
    )


def forward_kernel(shared, *refs):
    if shared:
        ins, refs = refs[:18], refs[18:]
        (x_ref, xn_ref, c1, c2, c3t, hm, hs, hb, fn, hn, vm, vs, am, adv_s, on, tt, cnt, act), refs = ins, refs
        (sw,), refs = refs[:1], refs[1:]
    else:
        (x_ref, xn_ref, k1_ref, k2_ref, k3_ref), refs = refs[:5], refs[5:]
    (a1_ref, s1_ref, a2_ref, s2_ref, f_ref, s3_ref, y_ref, y0_ref), refs = refs[:8], refs[8:]
    if shared:
        (w_out, slot_out, k2_ref, k3_ref), refs = refs[:4], refs[4:]
    (carry, a1s, b1_ref, b2_ref, b3_ref), refs = refs[:5], refs[5:]
    i = pl.program_id(0)
    rows = x_ref.shape[2]
    if shared:
        k1_ref, shard, kern_own, kern_buf, staged, slot_src, slot_buf, kern_s, kern_r, slot_s, slot_r, own_sem, sems, core_sems = refs
        flow_stage = {
            (f, s): (shard, w_out, flow, s, sems.at[0, f, s], sems.at[1, f, s])
            for f, flow in enumerate(GATHER_FLOWS)
            for s in range(3)
        }

        def kern_copies():
            return share("dp", 8, lambda _: kern_own, kern_buf, kern_s, kern_r)

        def slot_copies():
            ids = [lax.rem(lax.axis_index("dp") + j, 8) for j in range(1, 8)]
            return share("dp", 8, lambda j: slot_src.at[ids[j]], slot_buf, slot_s, slot_r)

        def own_copies():
            me = coordinates()
            return [
                pltpu.make_async_copy(shard.at[h], w_out.at[h, me["x"], me["c"], me["z"], me["y"]], own_sem.at[h])
                for h in range(2)
            ]

        def to_core(f, last):
            return core_copy(w_out, GATHER_FLOWS[f], last, core_sems.at[0, f, last], core_sems.at[1, f, last])

        def begin():
            greet()
            kern_own[...] = pack_shards(c1[...], c2[...], c3t[...]).astype(BF16)
            kern_buf[lax.axis_index("dp")] = kern_own[...]
            noisy_weights(shard, hm, hs, hb, fn, hn, vm, vs, am, adv_s, on)
            packed = slot_rows(staged, tt, cnt, act, sw).reshape(8, 2, 32, 128)
            lane = lax.broadcasted_iota(jnp.int32, (8, 32, 128), 2)
            slot_src[...] = jnp.where(lane < 64, packed[:, 0], pltpu.roll(packed[:, 1].reshape(256, 128), 64, 1).reshape(8, 32, 128))
            slot_buf[lax.axis_index("dp")] = slot_src[lax.axis_index("dp")]
            greeted()
            start(kern_copies())
            for f in range(4):
                start(gather_copies(*flow_stage[f, 0]))
            start(own_copies())
            prepare()
            finish(kern_copies())
            for d in range(8):
                unpack_shards(d, kern_buf[d].astype(F32), k1_ref, k2_ref, k3_ref)

        def advance(f, s):
            finish(gather_copies(*flow_stage[f, s]))
            start(gather_copies(*flow_stage[f, s + 1]))

        def point(step, k):
            todo = []
            if k == 1:
                todo = [
                    (1, lambda: (finish(own_copies()), [advance(f, 0) for f in (2, 3, 0, 1)])),
                    (3, lambda: [(advance(f, 1), to_core(f, 0).start()) for f in (2, 3)]),
                ]
            elif k == 2:
                todo = [
                    (4, lambda: ([(advance(f, 1), to_core(f, 0).start()) for f in (0, 1)], start(slot_copies()))),
                ]
            for at, what in todo:

                @pl.when(step == at)
                def _():
                    what()

        def end():
            for f in (2, 3, 0, 1):
                finish(gather_copies(*flow_stage[f, 2]))
                to_core(f, 1).start()
            finish(slot_copies())
            slot_out[:, 0:32] = slot_buf[...]
            slot_out[:, 32:64] = pltpu.roll(slot_buf[...].reshape(256, 128), 64, 1).reshape(8, 32, 128)
            for f in range(4):
                for last in range(2):
                    to_core(f, last).wait()

    def prepare():
        b2_ref[...] = jnp.zeros_like(b2_ref)
        b3_ref[...] = jnp.zeros_like(b3_ref)
        for r in range(4):
            for j, blk in enumerate(shifted_blocks(x_ref[0, r])):
                carry[j, :, 128 * r : 128 * r + 128] = blk
        y0_ref[...] = carry[...]

    @pl.when(i == 0)
    def _():
        if shared:
            begin()
        else:
            prepare()
        fill_band_one(k1_ref, b1_ref)
        fill_band_two(k2_ref, b2_ref)
        fill_band_three(k3_ref, b3_ref)

    for pp in range(4):
        for r in range(4):
            src = x_ref[pp + 1, r] if pp < 3 else xn_ref[0, r]
            for j, blk in enumerate(shifted_blocks(src)):
                y_ref[pp, j, :, 128 * r : 128 * r + 128] = blk
        for j in range(3):
            lhs = jnp.concatenate([carry[j] if pp == 0 else y_ref[pp - 1, j], y_ref[pp, j]], axis=1)
            act, slope = silu_and_slope(dot(lhs, b1_ref[...]))
            act = act.astype(BF16)
            a1_ref[pp // 2, pp % 2, :, 256 * j : 256 * j + 256] = act
            a1s[2 * i + pp // 2, pp % 2, :, 256 * j : 256 * j + 256] = act
            s1_ref[pp // 2, pp % 2, :, 256 * j : 256 * j + 256] = slope.astype(BF16)
        if shared and pp == 1:
            point(i, 1)
    carry[...] = y_ref[3]
    if shared:
        point(i, 2)

    def second(p):
        for lo, hi, n0, n1 in ((0, 384, 0, 256), (256, 640, 256, 512), (512, 768, 512, 640)):
            lhs = jnp.concatenate([a1s[p + u // 2, u % 2, :, lo:hi] for u in range(4)], axis=1)
            rhs = jnp.concatenate([b2_ref[u, lo:hi, n0:n1] for u in range(4)], axis=0)
            act, slope = silu_and_slope(dot(lhs, rhs))
            act = act.astype(BF16)
            a2_ref[p, :, n0:n1] = act
            s2_ref[p, :, n0:n1] = slope.astype(BF16)

    def third(p, odd):
        acts, slopes = [], []
        for lo, hi, n0, n1 in ((0, 384, 0, 256), (256, 640, 256, 512)):
            lhs = jnp.concatenate([a2_ref[p + u, :, lo:hi] for u in range(3)], axis=1)
            rhs = jnp.concatenate([b3_ref[u, lo:hi, n0:n1] for u in range(3)], axis=0)
            act, slope = silu_and_slope(dot(lhs, rhs))
            acts.append(act)
            slopes.append(slope)
        lane = lax.broadcasted_iota(jnp.int32, (rows, 512), 1)
        base = (p // 2) * 896
        for out, parts in ((f_ref, acts), (s3_ref, slopes)):
            whole = jnp.where(lane < 448, jnp.concatenate(parts, axis=1), 0.0)
            if not odd:
                out[:, pl.ds(pl.multiple_of(base, 128), 512)] = whole.astype(BF16)
            else:
                whole = pltpu.roll(whole, 64, 1)
                at = pl.ds(pl.multiple_of(base + 384, 128), 128)
                out[:, at] = (out[:, at].astype(F32) + whole[:, :128]).astype(BF16)
                out[:, pl.ds(pl.multiple_of(base + 512, 128), 384)] = whole[:, 128:].astype(BF16)

    @pl.when(i >= 1)
    def _():
        second(2 * i - 1)

    second(2 * i)

    @pl.when(i >= 2)
    def _():
        third(2 * i - 3, True)

    @pl.when(i >= 1)
    def _():
        third(2 * i - 2, False)

    @pl.when(i == 4)
    def _():
        lane = lax.broadcasted_iota(jnp.int32, (rows, 128), 1)
        last = f_ref[:, 3072:3200].astype(F32)
        f_ref[:, 3072:3200] = jnp.where(lane == 64, 1.0, last).astype(BF16)
        if shared:
            end()


def full(shape):
    return pl.BlockSpec(shape, lambda *_: (0,) * len(shape))


def once(shape):
    return pl.BlockSpec(shape, lambda *_: (0,) * len(shape), pipeline_mode=pl.Buffered(1))


BANDS = [(1024, 256), (4, 768, 640), (3, 640, 512)]


def torso_forward(x, kernels, shared=None):
    rows = x.shape[2]
    shapes = [(10, 2, rows, 768)] * 2 + [(9, rows, 640)] * 2 + [(rows, 3200)] * 2 + [(20, 3, rows, 512), (3, rows, 512)]
    args = [x, x, *kernels]
    out_specs = (
        [pl.BlockSpec((2, 2, rows, 768), lambda i: (i, 0, 0, 0))] * 2
        + [once((9, rows, 640))] * 2
        + [once((rows, 3200))] * 2
        + [pl.BlockSpec((4, 3, rows, 512), lambda i: (i, 0, 0, 0)), once((3, rows, 512))]
    )
    out_shape = [jax.ShapeDtypeStruct(s, BF16) for s in shapes]
    scratch = [
        pltpu.VMEM((3, rows, 512), BF16),
        pltpu.VMEM((10, 2, rows, 768), BF16),
        *[pltpu.VMEM(s, BF16) for s in BANDS],
    ]
    params = {}
    if shared is not None:
        args += shared
        out_specs += [pl.BlockSpec(memory_space=pl.ANY), once((8, 64, 128)), once((512, 128)), once((576, 128))]
        out_shape += [
            jax.ShapeDtypeStruct((2, 2, 2, 4, 2, 16, HALF), BF16),
            jax.ShapeDtypeStruct((8, 64, 128), F32),
            jax.ShapeDtypeStruct((512, 128), F32),
            jax.ShapeDtypeStruct((576, 128), F32),
        ]
        scratch += [
            pltpu.VMEM((256, 128), F32),
            pltpu.VMEM((2, 16, HALF), BF16),
            pltpu.VMEM((80, 128), BF16),
            pltpu.VMEM((8, 80, 128), BF16),
            pltpu.VMEM((128, 512), F32),
            pltpu.VMEM((8, 32, 128), F32),
            pltpu.VMEM((8, 32, 128), F32),
            *[pltpu.SemaphoreType.DMA((7,))] * 4,
            pltpu.SemaphoreType.DMA((2,)),
            pltpu.SemaphoreType.DMA((2, 4, 3, 3)),
            pltpu.SemaphoreType.DMA((2, 4, 2)),
        ]
        params = dict(collective_id=0, has_side_effects=True)
    return pl.pallas_call(
        functools.partial(forward_kernel, shared is not None),
        grid=(5,),
        in_specs=[
            pl.BlockSpec((4, 4, rows, 336), lambda i: (i, 0, 0, 0)),
            pl.BlockSpec((1, 4, rows, 336), lambda i: (4 * i + 4, 0, 0, 0)),
            *[once(v.shape) for v in args[2:]],
        ],
        out_specs=out_specs,
        out_shape=out_shape,
        scratch_shapes=scratch,
        compiler_params=pltpu.CompilerParams(vmem_limit_bytes=VMEM_LIMIT, **params),
        name="torso_forward",
    )(*args)


def pack_kernels(d, o1, o2, o3):
    lane = lax.broadcasted_iota(jnp.int32, (32, 128), 1)
    two = jnp.where(lane < 64, o2[64 * d : 64 * d + 32, :], o2[64 * d + 32 : 64 * d + 64, :])
    three = jnp.where(lane < 64, o3[72 * d : 72 * d + 32, :], o3[72 * d + 32 : 72 * d + 64, :])
    lane = lane[:8] // 32
    one = jnp.zeros((8, 128), F32)
    for k in range(4):
        one = jnp.where(lane == k, o1[32 * d + 8 * k : 32 * d + 8 * k + 8, :], one)
    return jnp.concatenate([two, three, o3[72 * d + 64 : 72 * d + 72, :], one], axis=0)


def backward_kernel(summed, *refs):
    (y_ref, y0_ref, a1_ref, s1_ref, a2_ref, s2_ref, s3_ref, fg_ref, k2_ref, k3_ref), refs = refs[:10], refs[10:]
    if summed:
        (dw_ref, stat_ref, dsum_ref, stat_out, kern_out), refs = refs[:5], refs[5:]
    (o1_ref, o2_ref, o3_ref), refs = refs[:3], refs[3:]
    (carry, g3, g2, b2_ref, b3_ref, d1_ref, d2a_ref, d2b_ref, d2c_ref, d3_ref), refs = refs[:10], refs[10:]
    if summed:
        (acc, stat_dp, stat_mp, kern_send, kern_dp, kern_mp, load_sem, sems, send_s, recv_s), bufs = refs[:10], refs[10:]
        me = coordinates()
        stages = {}
        at = 0
        for f, flow in enumerate(SUM_FLOWS):
            for s in range(3):
                stages[f, s] = (dw_ref if s == 0 else acc, flow, s, bufs[at], sems.at[0, at], sems.at[1, at])
                at += 1

        def loads():
            return [pltpu.make_async_copy(dw_ref.at[h], acc.at[h], load_sem.at[h]) for h in range(2)]

        def stat_copies(axis, count, k):
            src = stat_ref if k == 0 else stat_mp.at[lax.axis_index("mp")]
            return share(axis, count, lambda _: src, (stat_dp, stat_mp)[k], send_s.at[k], recv_s.at[k])

        def kern_copies(axis, count, k):
            ids = [lax.rem(lax.axis_index("dp") + j, 8) for j in range(1, 8)]
            src = (lambda j: kern_send.at[ids[j]]) if k == 0 else (lambda _: kern_mp.at[lax.axis_index("mp")])
            return share(axis, count, src, (kern_dp, kern_mp)[k], send_s.at[2 + k], recv_s.at[2 + k])

        def first():
            start(loads())
            greeted()
            for f in (0, 1):
                start(sum_copies(*stages[f, 0]))
            start(stat_copies("dp", 8, 0))
            stat_dp[lax.axis_index("dp")] = stat_ref[...]

        def stats_over():
            finish(loads())
            finish(stat_copies("dp", 8, 0))
            stat_mp[lax.axis_index("mp")] = in_order(stat_dp, 8)
            start(stat_copies("mp", 4, 1))

        def point(step, k):
            todo = {
                (0, 4): stats_over,
                (1, 1): lambda: (next_stage(0, 0), next_stage(1, 0), [start(sum_copies(*stages[f, 0])) for f in (2, 3)]),
                (2, 0): stats_done,
                (2, 3): lambda: (next_stage(2, 0), next_stage(3, 0)),
                (3, 3): lambda: (next_stage(2, 1), next_stage(3, 1)),
                (4, 1): lambda: (next_stage(0, 1), next_stage(1, 1)),
            }
            todo = [(at, what) for (at, where), what in todo.items() if where == k]
            for at, what in todo:

                @pl.when(step == at)
                def _():
                    what()

        def next_stage(f, s):
            finish(sum_copies(*stages[f, s]))
            add_arrived(acc, *stages[f, s][1:4], out=dsum_ref if s == 2 else None)
            if s < 2:
                start(sum_copies(*stages[f, s + 1]))

        def stats_done():
            finish(stat_copies("mp", 4, 1))
            stat_out[...] = in_order(stat_mp, 4)

        def kernels_out():
            for d in range(8):
                kern_send[d] = pack_kernels(d, o1_ref, o2_ref, o3_ref).astype(BF16)
            kern_dp[lax.axis_index("dp")] = kern_send[lax.axis_index("dp")]
            start(kern_copies("dp", 8, 0))

        def kernels_over():
            finish(kern_copies("dp", 8, 0))
            kern_mp[lax.axis_index("mp")] = in_order(kern_dp, 8)
            start(kern_copies("mp", 4, 1))

        def kernels_done():
            finish(kern_copies("mp", 4, 1))
            kern_out[...] = in_order(kern_mp, 4) / stat_out[9:10, :]

    i = pl.program_id(0)
    rows = y_ref.shape[2]

    @pl.when(i == 0)
    def _():
        if summed:
            greet()
        b2_ref[...] = jnp.zeros_like(b2_ref)
        b3_ref[...] = jnp.zeros_like(b3_ref)
        fill_band_two(k2_ref, b2_ref)
        fill_band_three(k3_ref, b3_ref)
        for at in (0, 1, 9, 10):
            g3[at] = jnp.zeros((rows, 512), BF16)
        for at in (0, 10):
            g2[at] = jnp.zeros((rows, 640), BF16)
        lane = lax.broadcasted_iota(jnp.int32, (rows, 512), 1)
        for p in range(7):
            base = (p // 2) * 896 + (384 if p % 2 else 0)
            both = fg_ref[:, base : base + 512].astype(F32) * s3_ref[:, base : base + 512].astype(F32)
            if p % 2:
                both = pltpu.roll(both, 448, 1)
            g3[p + 2] = jnp.where(lane < 448, both, 0.0).astype(BF16)
        if summed:
            first()
        for u in range(3):
            total = 0.0
            for m in range(2):
                lhs = a2_ref[u : u + 7, :, 256 * m : 256 * m + 384].reshape(7 * rows, 384)
                rhs = g3[2:9, :, 256 * m : 256 * m + 256].reshape(7 * rows, 256)
                total = total + dot_tn(lhs, rhs)
            d3_ref[u] = total
        d1_ref[...] = jnp.zeros_like(d1_ref)
        d2a_ref[...] = jnp.zeros_like(d2a_ref)
        d2b_ref[...] = jnp.zeros_like(d2b_ref)
        d2c_ref[...] = jnp.zeros_like(d2c_ref)
        for lo, hi, n0, n1 in ((0, 256, 0, 256), (256, 512, 128, 512), (512, 640, 384, 512)):
            rhs = jnp.concatenate([b3_ref[u, lo:hi, n0:n1] for u in range(3)], axis=1)

            def one(p, _):
                lhs = jnp.concatenate([g3[p + 2 - u, :, n0:n1] for u in range(3)], axis=1)
                back = dot_nt(lhs, rhs) * s2_ref[p, :, lo:hi].astype(F32)
                g2[p + 1, :, lo:hi] = back.astype(BF16)
                return 0

            lax.fori_loop(0, 9, one, 0)

    if summed:
        point(i, 0)
    for r in range(2):
        for t in range(2):
            for ref, lo, hi, n0, n1 in ((d2a_ref, 0, 384, 0, 256), (d2b_ref, 256, 640, 256, 512), (d2c_ref, 512, 768, 512, 640)):
                lhs = a1_ref[:, r, :, lo:hi].reshape(2 * rows, hi - lo)
                rhs = g2[pl.ds(2 * i + 1 - t, 2), :, n0:n1].reshape(2 * rows, n1 - n0)
                ref[2 * t + r] += dot_tn(lhs, rhs)

    @pl.when(i == 0)
    def _():
        carry[...] = y0_ref[...]

    for j, (n0, n1) in enumerate(((0, 256), (128, 512), (384, 640))):
        if summed:
            point(i, 1 + j)
        grads = []
        for pp in range(4):
            r = pp % 2
            at = 2 * i + pp // 2 + 1
            lhs = jnp.concatenate([g2[at, :, n0:n1], g2[at - 1, :, n0:n1]], axis=1)
            rhs = jnp.concatenate([b2_ref[r, 256 * j : 256 * j + 256, n0:n1], b2_ref[2 + r, 256 * j : 256 * j + 256, n0:n1]], axis=1)
            back = dot_nt(lhs, rhs) * s1_ref[pp // 2, r, :, 256 * j : 256 * j + 256].astype(F32)
            grads.append(back.astype(BF16))
        grad = jnp.concatenate(grads, axis=0)
        for t in range(2):
            pieces = [y_ref[k - 1 + t, j] if k + t > 0 else carry[j] for k in range(4)]
            lhs = jnp.concatenate(pieces, axis=0)
            d1_ref[512 * t : 512 * t + 512, :] += dot_tn(lhs, grad)
    carry[...] = y_ref[3]
    if summed:
        point(i, 4)

    @pl.when(i == 4)
    def _():
        take_band_one(d1_ref, o1_ref)
        take_band_two(((d2a_ref, 0, 0, 4), (d2b_ref, 8, 4, 4), (d2c_ref, 16, 8, 1)), o2_ref)
        take_band_three(d3_ref, o3_ref)
        if summed:
            kernels_out()
            for f in range(4):
                next_stage(f, 2)
            kernels_over()
            kernels_done()


def torso_backward(y, y0, a1, s1, a2, s2, s3, fg, kern2, kern3, summed=None):
    rows = y.shape[2]
    sums = [(1024, 256), (4, 384, 256), (4, 384, 256), (4, 256, 128), (3, 384, 256)]
    own = [(256, 128), (512, 128), (576, 128)]
    args = [y, y0, a1, s1, a2, s2, s3, fg, kern2, kern3]
    in_specs = [
        pl.BlockSpec((4, 3, rows, 512), lambda i: (i, 0, 0, 0)),
        once(y0.shape),
        pl.BlockSpec((2, 2, rows, 768), lambda i: (i, 0, 0, 0)),
        pl.BlockSpec((2, 2, rows, 768), lambda i: (i, 0, 0, 0)),
        *[once(v.shape) for v in args[4:]],
    ]
    scratch = [
        pltpu.VMEM((3, rows, 512), BF16),
        pltpu.VMEM((11, rows, 512), BF16),
        pltpu.VMEM((11, rows, 640), BF16),
        *[pltpu.VMEM(s, BF16) for s in BANDS[1:]],
        *[pltpu.VMEM(s, F32) for s in sums],
    ]
    outs = own
    params = {}
    if summed is not None:
        args += summed
        block = (2, *AXES.values(), 16, HALF)
        in_specs += [pl.BlockSpec(memory_space=pl.ANY), once((16, 128))]
        outs = [(2, 16, HALF), (16, 128), (80, 128)]
        buffers = flow_buffers(SUM_FLOWS)
        scratch = [pltpu.VMEM(s, F32) for s in own] + scratch
        scratch += [
            pltpu.VMEM(block, BF16),
            pltpu.VMEM((8, 16, 128), F32),
            pltpu.VMEM((4, 16, 128), F32),
            pltpu.VMEM((8, 80, 128), BF16),
            pltpu.VMEM((8, 80, 128), BF16),
            pltpu.VMEM((4, 80, 128), F32),
            pltpu.SemaphoreType.DMA((2,)),
            pltpu.SemaphoreType.DMA((2, len(buffers), 3)),
            pltpu.SemaphoreType.DMA((4, 7)),
            pltpu.SemaphoreType.DMA((4, 7)),
            *[pltpu.VMEM(s, BF16) for s in buffers],
        ]
        params = dict(collective_id=1, has_side_effects=True)
    return pl.pallas_call(
        functools.partial(backward_kernel, summed is not None),
        grid=(5,),
        in_specs=in_specs,
        out_specs=[once(s) for s in outs],
        out_shape=[jax.ShapeDtypeStruct(s, F32) for s in outs],
        scratch_shapes=scratch,
        compiler_params=pltpu.CompilerParams(vmem_limit_bytes=VMEM_LIMIT, **params),
        name="torso_backward",
    )(*args)


def high_low(v):
    high = v.astype(BF16)
    return high, (v - high.astype(F32)).astype(BF16)


def heads_kernel(atoms, acts, paired, f_ref, w_ref, bias_ref, slot_ref, row_ref, dw_out, fg_ref, prio_ref, stat_ref, *refs):
    if paired:
        dw_ref, arrived, send, recv = refs
        me = coordinates()
        other = device_at({**me, "c": 1 - me["c"]})
        barrier = pltpu.get_barrier_semaphore()
        pl.semaphore_signal(barrier, inc=1, **other)
        pl.semaphore_wait(barrier, 1)
        to_core = [
            pltpu.make_async_remote_copy(dw_ref.at[h, :, 1 - me["c"]], arrived.at[h], send.at[h], recv.at[h], **other)
            for h in range(2)
        ]

    def put(h, lo, hi, v):
        v = v.astype(BF16)
        if paired:
            dw_ref[h, :, :, :, :, :, lo:hi] = v.reshape(2, 2, 4, 2, 16, hi - lo)
        else:
            dw_out[h, :, lo:hi] = v

    rows = f_ref.shape[0]
    slots = slot_ref.shape[0]
    feats = f_ref[...]
    pre = [dot_nt(feats, w_ref[k, :, :3200]) for k in range(2)]
    hidden, slope = [], []
    for k in range(2):
        a, s = silu_and_slope(pre[k])
        hidden.append(a.astype(BF16))
        slope.append(s)
    out_w = jnp.concatenate([w_ref[0, :, 3200:], w_ref[1, :, 3200:]], axis=1)
    wide = out_w.shape[1]
    lane = lax.broadcasted_iota(jnp.int32, (1, wide), 1)
    zero = jnp.zeros((), BF16)
    w_val = jnp.where(lane[:, :128] < atoms, out_w[:, :128].astype(F32), 0.0).astype(BF16)
    w_adv = jnp.where(lane >= atoms, out_w.astype(F32), 0.0).astype(BF16)
    outs = bias_ref.shape[1]
    bias = jnp.concatenate([bias_ref[...], jnp.zeros((1, wide - outs), F32)], axis=1)
    logits = dot(hidden[1], w_adv) + bias
    logits = jnp.concatenate([logits[:, :128] + dot(hidden[0], w_val), logits[:, 128:]], axis=1)
    high, low = high_low(logits)
    selt = jnp.where(lax.broadcasted_iota(jnp.int32, (rows, slots), 0) == row_ref[...], 1.0, 0.0).astype(BF16)
    per_slot = dot_tn(selt, high) + dot_tn(selt, low)
    action = slot_ref[:, atoms + 2 : atoms + 3]
    which = jnp.where(lane < atoms, -1, jnp.where(lane < atoms * (acts + 1), (lane - atoms) // atoms, -2)).astype(F32)
    coeff = jnp.where(which == -1.0, 1.0, 0.0) + jnp.where(which == action, 1.0, 0.0) - jnp.where(which >= 0.0, 1.0 / acts, 0.0)
    atom = jnp.where(which >= -1.0, lane - atoms * (which.astype(jnp.int32) + 1), -1)
    fold = jnp.where(lax.broadcasted_iota(jnp.int32, (128, wide), 0) == atom, 1.0, 0.0).astype(BF16)
    high, low = high_low(per_slot * coeff)
    q = dot_nt(high, fold) + dot_nt(low, fold)
    lane_q = lax.broadcasted_iota(jnp.int32, (slots, 128), 1)
    used = lane_q < atoms
    top = jnp.max(jnp.where(used, q, -jnp.inf), axis=1, keepdims=True)
    shifted = jnp.where(used, jnp.exp(jnp.where(used, q - top, 0.0)), 0.0)
    total = jnp.sum(shifted, axis=1, keepdims=True)
    tgt = jnp.where(used, slot_ref[...], 0.0)
    cross = -jnp.sum(jnp.where(used, tgt * (q - top - jnp.log(total)), 0.0), axis=1, keepdims=True)
    coef = slot_ref[:, atoms : atoms + 1]
    valid = slot_ref[:, atoms + 1 : atoms + 2]
    prio_ref[...] = jnp.transpose(jnp.broadcast_to(valid * cross, (slots, 128)))[0:1]
    q_grad = coef * (shifted * (jnp.sum(tgt, axis=1, keepdims=True) / total) - tgt)
    high, low = high_low(q_grad)
    lgrad = ((dot(high, fold) + dot(low, fold)) * coeff).astype(BF16)
    bias_grad = jnp.sum(lgrad.astype(F32), axis=0, keepdims=True)
    for k in range(8):
        stat_ref[k : k + 1, :] = bias_grad[:, 128 * k : 128 * k + 128]
    stat_ref[8:9, :] = jnp.broadcast_to(jnp.sum(coef * cross, axis=0, keepdims=True), (1, 128))
    stat_ref[9:10, :] = jnp.broadcast_to(jnp.sum(valid, axis=0, keepdims=True), (1, 128))
    stat_ref[10:16, :] = jnp.zeros((6, 128), F32)
    grad = dot(selt, lgrad).astype(BF16)
    d_adv = dot_tn(hidden[1], grad)
    d_val = dot_tn(hidden[0], grad[:, :128])
    put(0, 3200, 3328, jnp.where(lane[:, :128] < atoms, d_val, d_adv[:, :128]))
    put(0, 3328, HALF, d_adv[:, 128:512])
    put(1, 3200, HALF, d_adv[:, 512:])
    pre_grad = [
        (dot_nt(grad[:, :128], w_val) * slope[0]).astype(BF16),
        (dot_nt(grad, w_adv) * slope[1]).astype(BF16),
    ]
    for k in range(2):
        for lo, hi in ((0, 1024), (1024, 2048), (2048, 3200)):
            put(k, lo, hi, dot_tn(pre_grad[k], f_ref[:, lo:hi]))
        if paired:
            to_core[k].start()
    for lo, hi in ((0, 1024), (1024, 2048), (2048, 3200)):
        back = dot(pre_grad[0], w_ref[0, :, lo:hi]) + dot(pre_grad[1], w_ref[1, :, lo:hi])
        fg_ref[:, lo:hi] = back.astype(BF16)
    if paired:
        for h in range(2):
            to_core[h].wait()

            def one(j, _):
                x, z, y = j // 8, (j // 2) % 4, j % 2
                dw_out[h, x, z, y] = (dw_ref[h, x, me["c"], z, y].astype(F32) + arrived[h, x, z, y].astype(F32)).astype(BF16)
                return 0

            lax.fori_loop(0, 16, one, 0)


def heads(atoms, acts, feats, weights, bias, per_slot, rows_of_slot, paired=False):
    slots = per_slot.shape[0]
    block = (2, 2, 4, 2, 16, HALF)
    scratch, params = [], {}
    if paired:
        scratch = [
            pltpu.VMEM((2, 2, 2, 4, 2, 16, HALF), BF16),
            pltpu.VMEM(block, BF16),
            pltpu.SemaphoreType.DMA((2,)),
            pltpu.SemaphoreType.DMA((2,)),
        ]
        params = dict(collective_id=3, has_side_effects=True)
    return pl.pallas_call(
        functools.partial(heads_kernel, atoms, acts, paired),
        out_shape=[
            jax.ShapeDtypeStruct(block if paired else weights.shape, BF16),
            jax.ShapeDtypeStruct(feats.shape, BF16),
            jax.ShapeDtypeStruct((1, slots), F32),
            jax.ShapeDtypeStruct((16, 128), F32),
        ],
        scratch_shapes=scratch,
        compiler_params=pltpu.CompilerParams(vmem_limit_bytes=VMEM_LIMIT, **params),
        name="heads",
    )(feats, weights, bias, per_slot, rows_of_slot[None, :])


def finish_kernel(
    dsum, stat, kern, fn, hn, on, loss, g1, g2, g3t, mean_g, spread_g, bias_g, val_g, val_s, adv_g, adv_s, out_g
):
    feat, atoms, outs = fn.shape[1], val_g.shape[1], on.shape[1]
    inverse = 1.0 / stat[9:10, 0:1]
    loss[...] = stat[8:9, 0:1] * inverse
    v = kern[...]
    turned = pltpu.roll(v, 64, 1)
    g2[0:32, :] = v[0:32, 0:64]
    g2[32:64, :] = turned[0:32, 0:64]
    third = jnp.concatenate([v[32:64], turned[32:64], v[64:72], jnp.zeros((56, 128), F32)], axis=0)
    g3t[...] = jnp.transpose(third)[0:64, 0:72]
    for k in range(4):
        g1[8 * k : 8 * k + 8, :] = v[72:80, 32 * k : 32 * k + 32]
    for h in range(2):
        mean = dsum[h, :, 0:feat] * inverse
        mean_g[h] = mean
        spread_g[h] = mean * fn[h : h + 1, :] * as_column(hn[0, h : h + 1, :])
        bias_g[h : h + 1, :] = as_row(dsum[h, :, feat : feat + 1] * inverse)
    out = jnp.concatenate([dsum[0, :, 3200:], dsum[1, :, 3200:]], axis=1) * inverse
    val, adv = out[:, :atoms], out[:, atoms:outs]
    val_g[...] = val
    val_s[...] = val * as_column(hn[1, 0:1, :]) * on[:, :atoms]
    adv_g[...] = adv
    adv_s[...] = adv * as_column(hn[1, 1:2, :]) * on[:, atoms:]
    out_g[...] = jnp.concatenate([stat[k : k + 1, :] for k in range(8)], axis=1)[:, :outs] * inverse


def outputs(dsum, stat, kern, fn, hn, on, atoms):
    feat, outs = fn.shape[1], on.shape[1]
    shapes = [(1, 1), (32, 32), (64, 64), (64, 72), (2, 16, feat), (2, 16, feat), (2, 16)]
    shapes += [(16, atoms)] * 2 + [(16, outs - atoms)] * 2 + [(1, outs)]
    return pl.pallas_call(
        finish_kernel,
        out_shape=[jax.ShapeDtypeStruct(s, F32) for s in shapes],
        compiler_params=pltpu.CompilerParams(vmem_limit_bytes=VMEM_LIMIT),
        name="outputs",
    )(dsum, stat, kern, fn, hn, on)


def exchange_kernel(count, kern_ref, slot_ref, kerns_out, slots_out, send_kern, recv_kern, send_slot, recv_slot, own):
    me = lax.axis_index("dp")
    peers = [lax.rem(me + k, count) for k in range(count)]
    barrier = pltpu.get_barrier_semaphore()
    for k in range(1, count):
        pl.semaphore_signal(barrier, inc=1, device_id={"dp": peers[k]}, device_id_type=pl.DeviceIdType.MESH)
    pl.semaphore_wait(barrier, count - 1)
    mine = [
        pltpu.make_async_copy(kern_ref, kerns_out.at[me], own.at[0]),
        pltpu.make_async_copy(slot_ref.at[me], slots_out.at[me], own.at[1]),
    ]
    sent = []
    for k in range(1, count):
        to = dict(device_id={"dp": peers[k]}, device_id_type=pl.DeviceIdType.MESH)
        sent.append(pltpu.make_async_remote_copy(kern_ref, kerns_out.at[me], send_kern.at[k], recv_kern.at[k], **to))
        sent.append(pltpu.make_async_remote_copy(slot_ref.at[peers[k]], slots_out.at[me], send_slot.at[k], recv_slot.at[k], **to))
    for copy in mine + sent:
        copy.start()
    for copy in mine + sent:
        copy.wait()


def exchange(kern, slot):
    count = slot.shape[0]
    return pl.pallas_call(
        functools.partial(exchange_kernel, count),
        in_specs=[pl.BlockSpec(memory_space=pltpu.VMEM)] * 2,
        out_specs=[pl.BlockSpec(memory_space=pltpu.VMEM)] * 2,
        out_shape=[jax.ShapeDtypeStruct((count, *kern.shape), kern.dtype), jax.ShapeDtypeStruct(slot.shape, slot.dtype)],
        scratch_shapes=[pltpu.SemaphoreType.DMA((count,))] * 4 + [pltpu.SemaphoreType.DMA((2,))],
        compiler_params=pltpu.CompilerParams(collective_id=2, has_side_effects=True, vmem_limit_bytes=VMEM_LIMIT),
        name="exchange",
    )(kern, slot)


def on_device(
    frames,
    send_rows,
    recv_counts,
    actions,
    target_dist,
    sample_weight,
    conv_first,
    conv_second,
    conv_third,
    hidden_mean,
    hidden_spread,
    hidden_bias,
    feature_noise,
    hidden_noise,
    value_mean,
    value_spread,
    advantage_mean,
    advantage_spread,
    output_noise,
    output_bias,
):
    dp_count = lax.axis_size("dp")
    slots = send_rows.shape[0]
    capacity = slots // dp_count
    atoms = value_mean.shape[1]
    acts = advantage_mean.shape[1] // atoms
    rows = frames.shape[0]
    feat, own = hidden_mean.shape[1:]
    outs = atoms * (acts + 1)

    x = frames.transpose(1, 0, 2).reshape(21, 4, rows, 336)
    bias = output_bias[None, :]
    mean_t = hidden_mean.transpose(0, 2, 1)
    spread_t = hidden_spread.transpose(0, 2, 1)

    if (dp_count, lax.axis_size("mp"), own, slots) == (8, 4, 16, 512):
        noise = output_noise[None, :]
        shared = [mean_t, spread_t, hidden_bias, feature_noise, hidden_noise]
        shared += [value_mean, value_spread, advantage_mean, advantage_spread, noise]
        shared += [target_dist.T, recv_counts[None, :], actions[None, :], sample_weight[None, :]]
        kernels = [conv_first, conv_second, conv_third.T]
        a1, s1, a2, s2, feats, s3, y, y0, weights, per_slot, kern2, kern3 = torso_forward(x, kernels, shared)
        weights, per_slot = weights.reshape(2, 512, HALF), per_slot.reshape(slots, 128)
        dweights, feat_grad, prio, stat = heads(atoms, acts, feats, weights, bias, per_slot, send_rows, paired=True)
        summed = [dweights, stat]
        summed = torso_backward(y, y0, a1, s1, a2, s2, s3, feat_grad, kern2, kern3, summed=summed)
        loss, g1, g2, g3t, mean_g, spread_g, bias_g, *outer, out_g = outputs(
            *summed, feature_noise, hidden_noise, noise, atoms
        )
        return (
            loss[0, 0],
            g1,
            g2,
            g3t.T,
            mean_g.transpose(0, 2, 1),
            spread_g.transpose(0, 2, 1),
            bias_g,
            *outer,
            out_g[0],
            prio[0],
        )

    sizes = [w.size for w in (conv_first, conv_second, conv_third)]
    flat = jnp.concatenate([w.astype(BF16).reshape(-1) for w in (conv_first, conv_second, conv_third)])
    tall = -(-flat.size // 2048) * 16
    flat = jnp.pad(flat, (0, tall * 128 - flat.size)).reshape(tall, 128)
    is_valid = jnp.arange(capacity, dtype=jnp.int32)[None, :] < recv_counts[:, None]
    is_valid = is_valid.astype(F32).reshape(slots)
    per_slot = jnp.stack([is_valid * sample_weight, is_valid, actions.astype(F32)], axis=1)
    per_slot = jnp.concatenate([target_dist, per_slot, jnp.zeros((slots, 125 - atoms), F32)], axis=1)
    flat, per_slot = exchange(flat, per_slot.reshape(dp_count, capacity, 128))
    per_slot = per_slot.reshape(slots, 128)
    flat = flat.reshape(dp_count, -1)
    kern1 = jnp.tile(flat[:, : sizes[0]].reshape(-1, 32), (1, 4))
    kern2 = jnp.tile(flat[:, sizes[0] : sizes[0] + sizes[1]].reshape(-1, 64), (1, 2))
    kern3 = jnp.tile(flat[:, sizes[0] + sizes[1] : sum(sizes)].reshape(-1, 64), (1, 2))

    wide_one = mean_t + spread_t * feature_noise[:, None, :] * hidden_noise[0][:, :, None]
    wide_one = jnp.concatenate([wide_one, hidden_bias[:, :, None], jnp.zeros((2, own, 63), F32)], axis=2)
    wide_val = value_mean + value_spread * hidden_noise[1, 0][:, None] * output_noise[None, :atoms]
    wide_adv = advantage_mean + advantage_spread * hidden_noise[1, 1][:, None] * output_noise[None, atoms:]
    wide_out = jnp.concatenate([wide_val, wide_adv, jnp.zeros((own, 1024 - outs), F32)], axis=1)
    wide_out = wide_out.reshape(own, 2, 512).transpose(1, 0, 2)
    shard = jnp.concatenate([wide_one, wide_out], axis=2).astype(BF16)
    weights = lax.all_gather(shard, ("mp", "dp"), axis=1, tiled=True)

    a1, s1, a2, s2, feats, s3, y, y0 = torso_forward(x, [kern1, kern2, kern3])
    dweights, feat_grad, prio, stat = heads(atoms, acts, feats, weights, bias, per_slot, send_rows)
    dshard = lax.psum_scatter(dweights, ("mp", "dp"), scatter_dimension=1, tiled=True).astype(F32)
    stat = lax.psum(stat, ("dp", "mp"))
    inverse = 1.0 / stat[9, 0]
    k1, k2, k3 = torso_backward(y, y0, a1, s1, a2, s2, s3, feat_grad, kern2, kern3)
    kflat = jnp.concatenate([g.reshape(dp_count, -1) for g in (k1[:, :32], k2[:, :64], k3[:, :64])], axis=1)
    kflat = lax.psum(lax.psum_scatter(kflat, "dp", scatter_dimension=0, tiled=True)[0], "mp") * inverse
    conv_grads = (
        kflat[: sizes[0]].reshape(conv_first.shape),
        kflat[sizes[0] : sizes[0] + sizes[1]].reshape(conv_second.shape),
        kflat[sizes[0] + sizes[1] :].reshape(conv_third.shape),
    )
    dshard = dshard * inverse
    mean_grad_t = dshard[:, :, :feat]
    spread_grad_t = mean_grad_t * feature_noise[:, None, :] * hidden_noise[0][:, :, None]
    out_grad = dshard[:, :, 3200:].transpose(1, 0, 2).reshape(own, 1024)
    value_mean_grad = out_grad[:, :atoms]
    adv_mean_grad = out_grad[:, atoms:outs]
    return (
        stat[8, 0] * inverse,
        *conv_grads,
        mean_grad_t.transpose(0, 2, 1),
        spread_grad_t.transpose(0, 2, 1),
        dshard[:, :, feat],
        value_mean_grad,
        value_mean_grad * hidden_noise[1, 0][:, None] * output_noise[None, :atoms],
        adv_mean_grad,
        adv_mean_grad * hidden_noise[1, 1][:, None] * output_noise[None, atoms:],
        stat[:8].reshape(-1)[:outs] * inverse,
        prio[0],
    )


def solution(mesh):
    both, heads_dim = P(("dp", "mp")), P(("mp", "dp"), None)
    return jax.shard_map(
        on_device,
        mesh=mesh,
        in_specs=(
            P(("dp", "mp"), None, None),
            both,
            both,
            both,
            P(("dp", "mp"), None),
            both,
            P("dp", None),
            P("dp", None),
            P("dp", None),
            P(None, None, ("mp", "dp")),
            P(None, None, ("mp", "dp")),
            P(None, ("mp", "dp")),
            P(),
            P(None, None, ("mp", "dp")),
            heads_dim,
            heads_dim,
            heads_dim,
            heads_dim,
            P(),
            P(),
        ),
        out_specs=(
            P(),
            P("dp", None),
            P("dp", None),
            P("dp", None),
            P(None, None, ("mp", "dp")),
            P(None, None, ("mp", "dp")),
            P(None, ("mp", "dp")),
            heads_dim,
            heads_dim,
            heads_dim,
            heads_dim,
            P(),
            both,
        ),
        check_vma=False,
    )
```

```python
import functools

import jax
import jax.numpy as jnp
from jax import lax
from jax.experimental import pallas as pl
from jax.experimental.pallas import tpu as pltpu
from jax.sharding import PartitionSpec as P

F32 = jnp.float32
BF16 = jnp.bfloat16
VMEM_LIMIT = 60 * 1024 * 1024


def sigmoid(v):
    return 0.5 * jnp.tanh(0.5 * v) + 0.5


def silu_and_slope(v):
    s = sigmoid(v)
    a = v * s
    return a, s + a * (1.0 - s)


def dot(a, b):
    return lax.dot_general(a, b, (((1,), (0,)), ((), ())), preferred_element_type=F32)


def dot_nt(a, b):
    return lax.dot_general(a, b, (((1,), (1,)), ((), ())), preferred_element_type=F32)


def dot_tn(a, b):
    return lax.dot_general(a, b, (((0,), (0,)), ((), ())), preferred_element_type=F32)


def columns_of_one():
    return [7 * (g // 8) + g % 8 if g % 8 < 7 and 7 * (g // 8) + g % 8 < 20 else -9 for g in range(24)]


def half_lanes(left, right, rows):
    lane = lax.broadcasted_iota(jnp.int32, (rows, 128), 1)
    zero = jnp.zeros((rows, 128), F32)
    return jnp.where(lane < 64, zero if left is None else left, zero if right is None else right)


def fill_band_one(k1_ref, band):
    lane = lax.broadcasted_iota(jnp.int32, (16, 128), 1) // 32
    for u in range(8):
        taps = [k1_ref[((u // 4) * 2 + v) * 64 + (u % 4) * 16 :][:16].astype(F32) for v in range(2)]
        for g in range(8):
            for h in range(2):
                col = lane + 4 * h
                here = jnp.where((col == g) & (col < 7), taps[0], 0.0) + jnp.where((col == g - 1) & (col < 7), taps[1], 0.0)
                band[128 * u + 16 * g : 128 * u + 16 * g + 16, 128 * h : 128 * h + 128] = here.astype(BF16)


def fill_band_two(k2_ref, band):
    cols = columns_of_one()
    for u in range(4):

        def tap(v):
            at = ((u // 2) * 2 + v // 2) * 128 + ((u % 2) * 2 + v % 2) * 32
            return k2_ref[at : at + 32, :].astype(F32)

        for g, q in enumerate(cols):
            if q < 0:
                continue
            used = {(q - v) // 2: v for v in (q % 2, q % 2 + 2) if 0 <= (q - v) // 2 < 9}
            for m in sorted({c // 2 for c in used}):
                sides = [tap(used[2 * m + side]) if 2 * m + side in used else None for side in range(2)]
                band[u, 32 * g : 32 * g + 32, 128 * m : 128 * m + 128] = half_lanes(*sides, 32).astype(BF16)


def fill_band_three(k3_ref, band):
    for u in range(3):

        def tap(v):
            return k3_ref[(u * 3 + v) * 64 : (u * 3 + v) * 64 + 64, :].astype(F32)

        for q in range(9):
            used = {q - v: v for v in range(3) if 0 <= q - v < 7}
            for m in sorted({c // 2 for c in used}):
                sides = [tap(used[2 * m + side]) if 2 * m + side in used else None for side in range(2)]
                band[u, 64 * q : 64 * q + 64, 128 * m : 128 * m + 128] = half_lanes(*sides, 64).astype(BF16)


def fold_lanes(v, width):
    step = 64
    while step >= width:
        v = v + pltpu.roll(v, step, 1)
        step //= 2
    return v


def take_band_one(d1, out):
    lane = lax.broadcasted_iota(jnp.int32, (16, 128), 1) // 32
    for u in range(8):
        for v in range(2):
            total = jnp.zeros((16, 128), F32)
            for col in range(7):
                at = 128 * u + 16 * (col + v)
                h = col // 4
                total = total + jnp.where(lane + 4 * h == col, d1[at : at + 16, 128 * h : 128 * h + 128], 0.0)
            at = ((u // 4) * 2 + v) * 64 + (u % 4) * 16
            out[at : at + 16, :] = fold_lanes(total, 32)


def take_band_two(blocks, out):
    cols = columns_of_one()
    lane = lax.broadcasted_iota(jnp.int32, (32, 128), 1)
    for u in range(4):
        for v in range(4):
            total = jnp.zeros((32, 128), F32)
            for ref, first, c0, count in blocks:
                for c in range(count):
                    at = 32 * (cols.index(2 * (c0 + c) + v) - first)
                    piece = ref[u, at : at + 32, 128 * (c // 2) : 128 * (c // 2) + 128]
                    total = total + jnp.where((lane < 64) == (c % 2 == 0), piece, 0.0)
            at = ((u // 2) * 2 + v // 2) * 128 + ((u % 2) * 2 + v % 2) * 32
            out[at : at + 32, :] = fold_lanes(total, 64)


def take_band_three(d3, out):
    lane = lax.broadcasted_iota(jnp.int32, (64, 128), 1)
    for u in range(3):
        for v in range(3):
            total = jnp.zeros((64, 128), F32)
            for c in range(4):
                piece = d3[u, 64 * (c + v) : 64 * (c + v) + 64, 128 * (c // 2) : 128 * (c // 2) + 128]
                total = total + jnp.where((lane < 64) == (c % 2 == 0), piece, 0.0)
            at = (u * 3 + v) * 64
            out[at : at + 64, :] = fold_lanes(total, 64)


def coordinates():
    d, m = lax.axis_index("dp"), lax.axis_index("mp")
    return {"z": d // 2, "y": d % 2, "x": m // 2, "c": m % 2}


def device_at(at):
    return dict(
        device_id={"dp": at["z"] * 2 + at["y"], "mp": at["x"] * 2 + at["c"]}, device_id_type=pl.DeviceIdType.MESH
    )


AXES = {"x": 2, "z": 4, "y": 2}
HALF = 3712
CUTS = [(0, 1408, "zyx", "zxy"), (1408, 2816, "zyx", "zxy"), (2816, HALF, "xyz", "yxz")]
GATHER_FLOWS = [(half, lo, hi, orders[half]) for lo, hi, *orders in CUTS for half in range(2)]
SUM_FLOWS = [(half, lo, hi, order[::-1]) for half, lo, hi, order in GATHER_FLOWS]
GATHER_FIRST = [(4, 0), (5, 0), (0, 0)]
GATHER_PLAN = {(0, 0): [(4, 1), (5, 1), (1, 0), (0, 1)], (0, 1): [(2, 0)], (0, 3): [(1, 1)], (1, 0): [(3, 0)], (1, 3): [(2, 1), (0, 2)], (1, 5): [(4, 2)], (2, 1): [(1, 2)], (3, 0): [(3, 1)], (3, 4): [(5, 2)], (3, 5): [(2, 2)], (4, 1): [(3, 2)]}
GATHER_LAST = []
GATHER_DONE = [0, 4, 1, 2, 5, 3]
SUM_FIRST = [(0, 0), (1, 0), (4, 0)]
SUM_PLAN = {(0, 2): [(2, 0), (3, 0)], (0, 4): [(5, 0)], (1, 4): [(0, 1), (1, 1)], (2, 0): [(2, 1), (3, 1)], (2, 4): [(0, 2)], (2, 5): [(4, 1), (5, 1)], (2, 6): [(1, 2)], (3, 2): [(4, 2), (5, 2)], (3, 5): [(2, 2)], (4, 2): [(3, 2)]}
SUM_LAST = []
SUM_DONE = [0, 4, 5, 1, 2, 3]

def flow_buffers(flows):
    shapes = []
    for _, lo, hi, order in flows:
        for s, axis in enumerate(order):
            rest = [AXES[a] for a in AXES if a in order[s + 1 :]]
            shapes.append((AXES[axis] - 1, *rest, 16, hi - lo))
    return shapes


def peers_of(axis):
    me = coordinates()
    n = AXES[axis]
    return [{**me, axis: lax.rem(me[axis] + k, n)} for k in range(1, n)]


def block_of(ref, half, lo, hi, at):
    return ref.at[(half, *[at.get(a, slice(None)) for a in AXES], slice(None), slice(lo, hi))]


def sum_copies(acc, flow, stage, buf, send, recv):
    half, lo, hi, order = flow
    me = coordinates()
    held = {a: me[a] for a in order[:stage]}
    copies = []
    for k, peer in enumerate(peers_of(order[stage])):
        src = block_of(acc, half, lo, hi, {**held, order[stage]: peer[order[stage]]})
        copies.append(pltpu.make_async_remote_copy(src, buf.at[k], send.at[k], recv.at[k], **device_at(peer)))
    return copies


def add_arrived(acc, flow, stage, buf, out=None):
    half, lo, hi, order = flow
    me = coordinates()
    own = block_of(acc, half, lo, hi, {a: me[a] for a in order[: stage + 1]})
    if out is None and AXES[order[stage]] == 2:
        own[...] = own[...] + buf[0]
        return
    total = own[...].astype(F32)
    for k in range(AXES[order[stage]] - 1):
        total = total + buf[k].astype(F32)
    if out is None:
        own[...] = total.astype(BF16)
    else:
        out[half, :, lo:hi] = total


def everyone(axis, count):
    me = lax.axis_index(axis)
    return [dict(device_id={axis: lax.rem(me + k, count)}, device_id_type=pl.DeviceIdType.MESH) for k in range(1, count)]


def share(axis, count, src, buf, send, recv):
    me = lax.axis_index(axis)
    return [
        pltpu.make_async_remote_copy(src(k), buf.at[me], send.at[k], recv.at[k], **to)
        for k, to in enumerate(everyone(axis, count))
    ]


def in_order(buf, count):
    total = buf[0].astype(F32)
    for k in range(1, count):
        total = total + buf[k].astype(F32)
    return total


def gathered_block(ref, half, lo, hi, core, at):
    x, z, y = (at.get(a, slice(None)) for a in AXES)
    return ref.at[half, x, core, z, y, :, lo:hi]


def gather_copies(shard, out, flow, stage, send, recv):
    half, lo, hi, order = flow
    me = coordinates()
    at = {a: me[a] for a in order[stage:]}
    dst = gathered_block(out, half, lo, hi, me["c"], at)
    src = shard.at[half, :, lo:hi] if stage == 0 else dst
    return [
        pltpu.make_async_remote_copy(src, dst, send.at[k], recv.at[k], **device_at(peer))
        for k, peer in enumerate(peers_of(order[stage]))
    ]


def core_copies(out, flow, last, send, recv):
    half, lo, hi, order = flow
    me = coordinates()
    other = {**me, "c": 1 - me["c"]}
    copies = []
    for k, at in enumerate([peer[order[2]] for peer in peers_of(order[2])] if last else [me[order[2]]]):
        block = gathered_block(out, half, lo, hi, me["c"], {order[2]: at})
        copies.append(pltpu.make_async_remote_copy(block, block, send.at[k], recv.at[k], **device_at(other)))
    return copies


def start(copies):
    for copy in copies:
        copy.start()


def finish(copies):
    for copy in copies:
        copy.wait()


def greet():
    for to in everyone("dp", 8) + everyone("mp", 4):
        pl.semaphore_signal(pltpu.get_barrier_semaphore(), inc=1, **to)


def greeted():
    pl.semaphore_wait(pltpu.get_barrier_semaphore(), 10)


def as_column(row):
    n = row.shape[1]
    eye = lax.broadcasted_iota(jnp.int32, (n, n), 0) == lax.broadcasted_iota(jnp.int32, (n, n), 1)
    return jnp.sum(jnp.where(eye, row, 0.0), axis=1, keepdims=True)


def as_row(column):
    n = column.shape[0]
    eye = lax.broadcasted_iota(jnp.int32, (n, n), 0) == lax.broadcasted_iota(jnp.int32, (n, n), 1)
    return jnp.sum(jnp.where(eye, column, 0.0), axis=0, keepdims=True)


def pack_shards(c1, c2, c3t):
    c3 = jnp.transpose(jnp.concatenate([c3t, jnp.zeros((64, 56), F32)], axis=1))
    blank = jnp.zeros((8, 64), F32)
    return jnp.concatenate(
        [
            jnp.concatenate([c2[0:32], c2[32:64]], axis=1),
            jnp.concatenate([c3[0:32], c3[32:64]], axis=1),
            jnp.concatenate([c3[64:72], blank], axis=1),
            jnp.concatenate([c1[8 * k : 8 * k + 8] for k in range(4)], axis=1),
        ],
        axis=0,
    )


def unpack_shards(d, v, k1, k2, k3):
    lane = lax.broadcasted_iota(jnp.int32, (32, 128), 1)

    def sides(w):
        turned = pltpu.roll(w, 64, 1)
        low = lane[: w.shape[0]] < 64
        return jnp.where(low, w, turned), jnp.where(low, turned, w)

    k2[64 * d : 64 * d + 32, :], k2[64 * d + 32 : 64 * d + 64, :] = sides(v[0:32])
    k3[72 * d : 72 * d + 32, :], k3[72 * d + 32 : 72 * d + 64, :] = sides(v[32:64])
    k3[72 * d + 64 : 72 * d + 72, :] = sides(v[64:72])[0]
    for k in range(4):
        part = jnp.where(lane[:8] // 32 == k, v[72:80], 0.0)
        k1[32 * d + 8 * k : 32 * d + 8 * k + 8, :] = fold_lanes(part, 32)


def noisy_weights(shard, hm, hs, hb, fn, hn, vm, vs, am, adv_s, on):
    atoms, outs = vm.shape[1], on.shape[1]
    lane = lax.broadcasted_iota(jnp.int32, (16, 128), 1)
    for h in range(2):
        wide = hm[h] + hs[h] * fn[h : h + 1, :] * as_column(hn[0, h : h + 1, :])
        shard[h, :, 0:3072] = wide[:, 0:3072].astype(BF16)
        last = jnp.concatenate([wide[:, 3072:], jnp.zeros((16, 64), F32)], axis=1)
        last = jnp.where(lane == 64, as_column(hb[h : h + 1, :]), last)
        shard[h, :, 3072:3200] = last.astype(BF16)
    val = vm[...] + vs[...] * as_column(hn[1, 0:1, :]) * on[:, :atoms]
    adv = am[...] + adv_s[...] * as_column(hn[1, 1:2, :]) * on[:, atoms:]
    out = jnp.concatenate([val, adv, jnp.zeros((16, 1024 - outs), F32)], axis=1).astype(BF16)
    shard[0, :, 3200:] = out[:, :512]
    shard[1, :, 3200:] = out[:, 512:]


def slot_rows(staged, tt, cnt, act, sw):
    atoms, slots = tt.shape
    lane = lax.broadcasted_iota(jnp.int32, (8, slots), 1)
    source = lax.broadcasted_iota(jnp.int32, (8, slots), 0)
    cap = slots // 8
    used = jnp.sum(jnp.where(lane // cap == source, as_column(cnt[...].astype(F32)), 0.0), axis=0, keepdims=True)
    valid = jnp.where((lane[0:1] % cap).astype(F32) < used, 1.0, 0.0)
    staged[...] = jnp.zeros_like(staged)
    staged[0:atoms, :] = tt[...]
    staged[atoms : atoms + 1, :] = valid * sw[...]
    staged[atoms + 1 : atoms + 2, :] = valid
    staged[atoms + 2 : atoms + 3, :] = act[...].astype(F32)
    return jnp.transpose(staged[...])


def shifted_blocks(x):
    rows = x.shape[0]
    return (
        x[:, 0:128],
        x[:, 112:240],
        jnp.concatenate([x[:, 224:336], jnp.zeros((rows, 16), x.dtype)], axis=1),
    )


def forward_kernel(shared, *refs):
    if shared:
        ins, refs = refs[:18], refs[18:]
        (x_ref, xn_ref, c1, c2, c3t, hm, hs, hb, fn, hn, vm, vs, am, adv_s, on, tt, cnt, act), refs = ins, refs
        (sw,), refs = refs[:1], refs[1:]
    else:
        (x_ref, xn_ref, k1_ref, k2_ref, k3_ref), refs = refs[:5], refs[5:]
    (a1_ref, s1_ref, *whole_out, y_ref, y0_ref), refs = refs[:8], refs[8:]
    if shared:
        (w_out, slot_out, k2_ref, k3_ref), refs = refs[:4], refs[4:]
    (carry, a1s, b1_ref, b2_ref, b3_ref, *whole, whole_sem), refs = refs[:10], refs[10:]
    a2_ref, s2_ref, f_ref, s3_ref = whole
    i = pl.program_id(0)
    rows = x_ref.shape[2]
    if shared:
        k1_ref, shard, kern_own, kern_buf, staged, slot_src, slot_buf, kern_s, kern_r, slot_s, slot_r, own_sem, sems, core_sems = refs
        flow_stage = {
            (f, s): (shard, w_out, flow, s, sems.at[0, f, s], sems.at[1, f, s])
            for f, flow in enumerate(GATHER_FLOWS)
            for s in range(3)
        }

        def kern_copies():
            return share("dp", 8, lambda _: kern_own, kern_buf, kern_s, kern_r)

        def slot_copies():
            ids = [lax.rem(lax.axis_index("dp") + j, 8) for j in range(1, 8)]
            return share("dp", 8, lambda j: slot_src.at[ids[j]], slot_buf, slot_s, slot_r)

        def own_copies():
            me = coordinates()
            return [
                pltpu.make_async_copy(shard.at[h], w_out.at[h, me["x"], me["c"], me["z"], me["y"]], own_sem.at[h])
                for h in range(2)
            ]

        def to_core(f, last):
            return core_copies(w_out, GATHER_FLOWS[f], last, core_sems.at[0, f, last], core_sems.at[1, f, last])

        def begin():
            greet()
            kern_own[...] = pack_shards(c1[...], c2[...], c3t[...]).astype(BF16)
            kern_buf[lax.axis_index("dp")] = kern_own[...]
            noisy_weights(shard, hm, hs, hb, fn, hn, vm, vs, am, adv_s, on)
            packed = slot_rows(staged, tt, cnt, act, sw).reshape(8, 2, 32, 128)
            lane = lax.broadcasted_iota(jnp.int32, (8, 32, 128), 2)
            slot_src[...] = jnp.where(lane < 64, packed[:, 0], pltpu.roll(packed[:, 1].reshape(256, 128), 64, 1).reshape(8, 32, 128))
            slot_buf[lax.axis_index("dp")] = slot_src[lax.axis_index("dp")]
            greeted()
            start(kern_copies())
            for f, s in GATHER_FIRST:
                enter(f, s)
            start(own_copies())
            prepare()
            finish(own_copies())
            finish(kern_copies())
            for d in range(8):
                unpack_shards(d, kern_buf[d].astype(F32), k1_ref, k2_ref, k3_ref)

        def enter(f, s):
            if s > 0:
                finish(gather_copies(*flow_stage[f, s - 1]))
            start(gather_copies(*flow_stage[f, s]))
            if s == 2:
                start(to_core(f, 0))

        def point(step, k):
            for (at, where), entries in GATHER_PLAN.items():
                if where == k:

                    @pl.when(step == at)
                    def _():
                        for f, s in entries:
                            enter(f, s)

            if k == 0:

                @pl.when(step == 4)
                def _():
                    start(slot_copies())

        def end():
            for f, s in GATHER_LAST:
                enter(f, s)
            for f in GATHER_DONE:
                finish(gather_copies(*flow_stage[f, 2]))
                start(to_core(f, 1))
            finish(slot_copies())
            slot_out[:, 0:32] = slot_buf[...]
            slot_out[:, 32:64] = pltpu.roll(slot_buf[...].reshape(256, 128), 64, 1).reshape(8, 32, 128)
            for f in GATHER_DONE:
                for last in range(2):
                    finish(to_core(f, last))

    def prepare():
        b2_ref[...] = jnp.zeros_like(b2_ref)
        b3_ref[...] = jnp.zeros_like(b3_ref)
        for r in range(4):
            for j, blk in enumerate(shifted_blocks(x_ref[0, r])):
                carry[j, :, 128 * r : 128 * r + 128] = blk
        y0_ref[...] = carry[...]

    @pl.when(i == 0)
    def _():
        if shared:
            begin()
        else:
            prepare()
        fill_band_one(k1_ref, b1_ref)
        fill_band_two(k2_ref, b2_ref)
        fill_band_three(k3_ref, b3_ref)

    for pp in range(4):
        for r in range(4):
            src = x_ref[pp + 1, r] if pp < 3 else xn_ref[0, r]
            for j, blk in enumerate(shifted_blocks(src)):
                y_ref[pp, j, :, 128 * r : 128 * r + 128] = blk
        for j in range(3):
            lhs = jnp.concatenate([carry[j] if pp == 0 else y_ref[pp - 1, j], y_ref[pp, j]], axis=1)
            act, slope = silu_and_slope(dot(lhs, b1_ref[...]))
            act = act.astype(BF16)
            a1_ref[pp // 2, pp % 2, :, 256 * j : 256 * j + 256] = act
            a1s[2 * i + pp // 2, pp % 2, :, 256 * j : 256 * j + 256] = act
            s1_ref[pp // 2, pp % 2, :, 256 * j : 256 * j + 256] = slope.astype(BF16)
        if shared:
            point(i, pp)
    carry[...] = y_ref[3]

    def second(p):
        for lo, hi, n0, n1 in ((0, 384, 0, 256), (256, 640, 256, 512), (512, 768, 512, 640)):
            lhs = jnp.concatenate([a1s[p + u // 2, u % 2, :, lo:hi] for u in range(4)], axis=1)
            rhs = jnp.concatenate([b2_ref[u, lo:hi, n0:n1] for u in range(4)], axis=0)
            act, slope = silu_and_slope(dot(lhs, rhs))
            act = act.astype(BF16)
            a2_ref[p, :, n0:n1] = act
            s2_ref[p, :, n0:n1] = slope.astype(BF16)

    def third(p, odd):
        acts, slopes = [], []
        for lo, hi, n0, n1 in ((0, 384, 0, 256), (256, 640, 256, 512)):
            lhs = jnp.concatenate([a2_ref[p + u, :, lo:hi] for u in range(3)], axis=1)
            rhs = jnp.concatenate([b3_ref[u, lo:hi, n0:n1] for u in range(3)], axis=0)
            act, slope = silu_and_slope(dot(lhs, rhs))
            acts.append(act)
            slopes.append(slope)
        lane = lax.broadcasted_iota(jnp.int32, (rows, 512), 1)
        base = (p // 2) * 896
        for out, parts in ((f_ref, acts), (s3_ref, slopes)):
            whole = jnp.where(lane < 448, jnp.concatenate(parts, axis=1), 0.0)
            if not odd:
                out[:, pl.ds(pl.multiple_of(base, 128), 512)] = whole.astype(BF16)
            else:
                whole = pltpu.roll(whole, 64, 1)
                at = pl.ds(pl.multiple_of(base + 384, 128), 128)
                out[:, at] = (out[:, at].astype(F32) + whole[:, :128]).astype(BF16)
                out[:, pl.ds(pl.multiple_of(base + 512, 128), 384)] = whole[:, 128:].astype(BF16)

    @pl.when(i >= 1)
    def _():
        second(2 * i - 1)

    if shared:
        point(i, 4)
    second(2 * i)
    if shared:
        point(i, 5)

    @pl.when(i >= 2)
    def _():
        third(2 * i - 3, True)

    if shared:
        point(i, 6)

    @pl.when(i >= 1)
    def _():
        third(2 * i - 2, False)

    @pl.when(i == 4)
    def _():
        lane = lax.broadcasted_iota(jnp.int32, (rows, 128), 1)
        last = f_ref[:, 3072:3200].astype(F32)
        f_ref[:, 3072:3200] = jnp.where(lane == 64, 1.0, last).astype(BF16)
        leaving = [pltpu.make_async_copy(whole[k], whole_out[k], whole_sem.at[k]) for k in range(4)]
        start(leaving)
        if shared:
            end()
        finish(leaving)


def full(shape):
    return pl.BlockSpec(shape, lambda *_: (0,) * len(shape))


def once(shape):
    return pl.BlockSpec(shape, lambda *_: (0,) * len(shape), pipeline_mode=pl.Buffered(1))


BANDS = [(1024, 256), (4, 768, 640), (3, 640, 512)]


def torso_forward(x, kernels, shared=None):
    rows = x.shape[2]
    shapes = [(10, 2, rows, 768)] * 2 + [(9, rows, 640)] * 2 + [(rows, 3200)] * 2 + [(20, 3, rows, 512), (3, rows, 512)]
    args = [x, x, *kernels]
    out_specs = (
        [pl.BlockSpec((2, 2, rows, 768), lambda i: (i, 0, 0, 0))] * 2
        + [pl.BlockSpec(memory_space=pl.ANY)] * 4
        + [pl.BlockSpec((4, 3, rows, 512), lambda i: (i, 0, 0, 0)), once((3, rows, 512))]
    )
    out_shape = [jax.ShapeDtypeStruct(s, BF16) for s in shapes]
    scratch = [
        pltpu.VMEM((3, rows, 512), BF16),
        pltpu.VMEM((10, 2, rows, 768), BF16),
        *[pltpu.VMEM(s, BF16) for s in BANDS],
        *[pltpu.VMEM(s, BF16) for s in shapes[2:6]],
        pltpu.SemaphoreType.DMA((4,)),
    ]
    params = {}
    if shared is not None:
        args += shared
        out_specs += [pl.BlockSpec(memory_space=pl.ANY), once((8, 64, 128)), once((512, 128)), once((576, 128))]
        out_shape += [
            jax.ShapeDtypeStruct((2, 2, 2, 4, 2, 16, HALF), BF16),
            jax.ShapeDtypeStruct((8, 64, 128), F32),
            jax.ShapeDtypeStruct((512, 128), F32),
            jax.ShapeDtypeStruct((576, 128), F32),
        ]
        scratch += [
            pltpu.VMEM((256, 128), F32),
            pltpu.VMEM((2, 16, HALF), BF16),
            pltpu.VMEM((80, 128), BF16),
            pltpu.VMEM((8, 80, 128), BF16),
            pltpu.VMEM((128, 512), F32),
            pltpu.VMEM((8, 32, 128), F32),
            pltpu.VMEM((8, 32, 128), F32),
            *[pltpu.SemaphoreType.DMA((7,))] * 4,
            pltpu.SemaphoreType.DMA((2,)),
            pltpu.SemaphoreType.DMA((2, len(GATHER_FLOWS), 3, 3)),
            pltpu.SemaphoreType.DMA((2, len(GATHER_FLOWS), 2, 3)),
        ]
        params = dict(collective_id=0, has_side_effects=True)
    return pl.pallas_call(
        functools.partial(forward_kernel, shared is not None),
        grid=(5,),
        in_specs=[
            pl.BlockSpec((4, 4, rows, 336), lambda i: (i, 0, 0, 0)),
            pl.BlockSpec((1, 4, rows, 336), lambda i: (4 * i + 4, 0, 0, 0)),
            *[once(v.shape) for v in args[2:]],
        ],
        out_specs=out_specs,
        out_shape=out_shape,
        scratch_shapes=scratch,
        compiler_params=pltpu.CompilerParams(vmem_limit_bytes=VMEM_LIMIT, **params),
        name="torso_forward",
    )(*args)


def pack_kernels(d, o1, o2, o3):
    lane = lax.broadcasted_iota(jnp.int32, (32, 128), 1)
    two = jnp.where(lane < 64, o2[64 * d : 64 * d + 32, :], o2[64 * d + 32 : 64 * d + 64, :])
    three = jnp.where(lane < 64, o3[72 * d : 72 * d + 32, :], o3[72 * d + 32 : 72 * d + 64, :])
    lane = lane[:8] // 32
    one = jnp.zeros((8, 128), F32)
    for k in range(4):
        one = jnp.where(lane == k, o1[32 * d + 8 * k : 32 * d + 8 * k + 8, :], one)
    return jnp.concatenate([two, three, o3[72 * d + 64 : 72 * d + 72, :], one], axis=0)


BACK_LANES = ((0, 256), (128, 512), (384, 640))


def backward_kernel(summed, *refs):
    (y_ref, a1_ref, s1_ref, *whole_in, k2_ref, k3_ref), refs = refs[:10], refs[10:]
    if summed:
        (dw_ref, stat_ref, dsum_ref, stat_out, kern_out), refs = refs[:5], refs[5:]
    (o1_ref, o2_ref, o3_ref), refs = refs[:3], refs[3:]
    (carry, *whole, whole_sem, back, grad, g3, g2, b2_ref, b3_ref, d1_ref, d2a_ref, d2b_ref, d2c_ref, d3_ref), refs = refs[:17], refs[17:]
    a2_ref, s2_ref, s3_ref, fg_ref = whole
    coming = [pltpu.make_async_copy(whole_in[k], (carry, *whole)[k], whole_sem.at[k]) for k in range(5)]
    if summed:
        (acc, stat_dp, stat_mp, kern_send, kern_dp, kern_mp, load_sem, sems, send_s, recv_s), bufs = refs[:10], refs[10:]
        me = coordinates()
        stages = {}
        at = 0
        for f, flow in enumerate(SUM_FLOWS):
            for s in range(3):
                stages[f, s] = (dw_ref if s == 0 else acc, flow, s, bufs[at], sems.at[0, at], sems.at[1, at])
                at += 1

        loaded = {
            f: pltpu.make_async_copy(
                dw_ref.at[half, :, :, :, :, lo:hi], acc.at[half, :, :, :, :, lo:hi], load_sem.at[f]
            )
            for f, (half, lo, hi, _) in enumerate(SUM_FLOWS)
        }

        def stat_copies(axis, count, k):
            src = stat_ref if k == 0 else stat_mp.at[lax.axis_index("mp")]
            return share(axis, count, lambda _: src, (stat_dp, stat_mp)[k], send_s.at[k], recv_s.at[k])

        def kern_copies(axis, count, k):
            ids = [lax.rem(lax.axis_index("dp") + j, 8) for j in range(1, 8)]
            src = (lambda j: kern_send.at[ids[j]]) if k == 0 else (lambda _: kern_mp.at[lax.axis_index("mp")])
            return share(axis, count, src, (kern_dp, kern_mp)[k], send_s.at[2 + k], recv_s.at[2 + k])

        def first():
            start(list(loaded.values()))
            greeted()
            for f, s in SUM_FIRST:
                enter(f, s)
            start(stat_copies("dp", 8, 0))
            stat_dp[lax.axis_index("dp")] = stat_ref[...]

        def stats_over():
            finish(stat_copies("dp", 8, 0))
            stat_mp[lax.axis_index("mp")] = in_order(stat_dp, 8)
            start(stat_copies("mp", 4, 1))

        def enter(f, s):
            if s > 0:
                leave(f, s - 1)
            start(sum_copies(*stages[f, s]))

        def leave(f, s):
            if s == 0:
                finish([loaded[f]])
            finish(sum_copies(*stages[f, s]))
            add_arrived(acc, *stages[f, s][1:4], out=dsum_ref if s == 2 else None)

        def point(step, k):
            for (at, where), entries in SUM_PLAN.items():
                if where == k:

                    @pl.when(step == at)
                    def _():
                        for f, s in entries:
                            enter(f, s)

            for at, where, what in ((0, 5, stats_over), (1, 6, stats_done)):
                if where == k:

                    @pl.when(step == at)
                    def _():
                        what()

        def stats_done():
            finish(stat_copies("mp", 4, 1))
            stat_out[...] = in_order(stat_mp, 4)

        def kernels_out():
            for d in range(8):
                kern_send[d] = pack_kernels(d, o1_ref, o2_ref, o3_ref).astype(BF16)
            kern_dp[lax.axis_index("dp")] = kern_send[lax.axis_index("dp")]
            start(kern_copies("dp", 8, 0))

        def kernels_over():
            finish(kern_copies("dp", 8, 0))
            kern_mp[lax.axis_index("mp")] = in_order(kern_dp, 8)
            start(kern_copies("mp", 4, 1))

        def kernels_done():
            finish(kern_copies("mp", 4, 1))
            kern_out[...] = in_order(kern_mp, 4) / stat_out[9:10, :]

    i = pl.program_id(0)
    rows = y_ref.shape[2]

    @pl.when(i == 0)
    def _():
        if summed:
            greet()
        start(coming[::-1])
        b2_ref[...] = jnp.zeros_like(b2_ref)
        b3_ref[...] = jnp.zeros_like(b3_ref)
        fill_band_two(k2_ref, b2_ref)
        fill_band_three(k3_ref, b3_ref)
        for r in range(2):
            for j, (n0, n1) in enumerate(BACK_LANES):
                for t in range(2):
                    turned = jnp.transpose(b2_ref[2 * t + r, 256 * j : 256 * j + 256, n0:n1].astype(F32))
                    back[j, r, t * (n1 - n0) : (t + 1) * (n1 - n0), :] = turned.astype(BF16)
        grad[3] = jnp.zeros(grad.shape[1:], BF16)
        finish(coming[3:])
        for at in (0, 1, 9, 10):
            g3[at] = jnp.zeros((rows, 512), BF16)
        for at in (0, 10):
            g2[at] = jnp.zeros((rows, 640), BF16)
        lane = lax.broadcasted_iota(jnp.int32, (rows, 512), 1)
        for p in range(7):
            base = (p // 2) * 896 + (384 if p % 2 else 0)
            both = fg_ref[:, base : base + 512].astype(F32) * s3_ref[:, base : base + 512].astype(F32)
            if p % 2:
                both = pltpu.roll(both, 448, 1)
            g3[p + 2] = jnp.where(lane < 448, both, 0.0).astype(BF16)
        if summed:
            first()
            point(i, "a0")
        finish([coming[1]])
        for u in range(3):
            total = 0.0
            for m in range(2):
                lhs = a2_ref[u : u + 7, :, 256 * m : 256 * m + 384].reshape(7 * rows, 384)
                rhs = g3[2:9, :, 256 * m : 256 * m + 256].reshape(7 * rows, 256)
                total = total + dot_tn(lhs, rhs)
            d3_ref[u] = total
            if summed:
                point(i, "a%d" % (1 + u))
        d1_ref[...] = jnp.zeros_like(d1_ref)
        d2a_ref[...] = jnp.zeros_like(d2a_ref)
        d2b_ref[...] = jnp.zeros_like(d2b_ref)
        d2c_ref[...] = jnp.zeros_like(d2c_ref)
        for at, (lo, hi, n0, n1) in enumerate(((0, 256, 0, 256), (256, 512, 128, 512), (512, 640, 384, 512))):
            rhs = jnp.concatenate([b3_ref[u, lo:hi, n0:n1] for u in range(3)], axis=1)
            if at == 0:
                finish([coming[0], coming[2]])
            for p in (0, 3, 6):
                lhs = jnp.concatenate([g3[p + 2 - u : p + 5 - u, :, n0:n1].reshape(3 * rows, n1 - n0) for u in range(3)], axis=1)
                product = dot_nt(lhs, rhs) * s2_ref[p : p + 3, :, lo:hi].reshape(3 * rows, hi - lo).astype(F32)
                g2[p + 1 : p + 4, :, lo:hi] = product.astype(BF16).reshape(3, rows, hi - lo)
            if summed:
                point(i, "a%d" % (4 + at))

    for r in range(2):
        for ref, lo, hi, n0, n1 in ((d2a_ref, 0, 384, 0, 256), (d2b_ref, 256, 640, 256, 512), (d2c_ref, 512, 768, 512, 640)):
            lhs = a1_ref[:, r, :, lo:hi].reshape(2 * rows, hi - lo)
            rhs = [g2[pl.ds(2 * i + 1 - t, 2), :, n0:n1].reshape(2 * rows, n1 - n0) for t in range(2)]
            both = dot_tn(lhs, jnp.concatenate(rhs, axis=1))
            for t in range(2):
                ref[2 * t + r] += both[:, t * (n1 - n0) : (t + 1) * (n1 - n0)]
        if summed:
            point(i, 2 * r)
            point(i, 2 * r + 1)

    for j, (n0, n1) in enumerate(BACK_LANES):
        lanes = slice(256 * j, 256 * j + 256)
        before = grad[3, :, lanes]
        for r in range(2):
            lhs = [g2[pl.ds(2 * i + 1 - t, 2), :, n0:n1].reshape(2 * rows, n1 - n0) for t in range(2)]
            product = dot(jnp.concatenate(lhs, axis=1), back[j, r, : 2 * (n1 - n0), :])
            for k in range(2):
                slope = s1_ref[k, r, :, lanes].astype(F32)
                grad[2 * k + r, :, lanes] = (product[k * rows : (k + 1) * rows] * slope).astype(BF16)
        now = [grad[k, :, lanes] for k in range(4)]
        rhs = jnp.concatenate([jnp.concatenate(now, axis=0), jnp.concatenate([before, *now[:3]], axis=0)], axis=1)
        lhs = jnp.concatenate([carry[j], *[y_ref[k, j] for k in range(3)]], axis=0)
        both = dot_tn(lhs, rhs)
        d1_ref[0:512, :] += both[:, 0:256]
        d1_ref[512:1024, :] += both[:, 256:512]
        if summed:
            point(i, 4 + j)
    carry[...] = y_ref[3]

    @pl.when(i == 4)
    def _():
        for j in range(3):
            d1_ref[512:1024, :] += dot_tn(y_ref[3, j], grad[3, :, 256 * j : 256 * j + 256])

    @pl.when(i == 4)
    def _():
        take_band_one(d1_ref, o1_ref)
        take_band_two(((d2a_ref, 0, 0, 4), (d2b_ref, 8, 4, 4), (d2c_ref, 16, 8, 1)), o2_ref)
        take_band_three(d3_ref, o3_ref)
        if summed:
            kernels_out()
            for f, s in SUM_LAST:
                enter(f, s)
            kernels_over()
            for f in SUM_DONE:
                leave(f, 2)
            kernels_done()


def torso_backward(y, y0, a1, s1, a2, s2, s3, fg, kern2, kern3, summed=None):
    rows = y.shape[2]
    sums = [(1024, 256), (4, 384, 256), (4, 384, 256), (4, 256, 128), (3, 384, 256)]
    own = [(256, 128), (512, 128), (576, 128)]
    args = [y, a1, s1, y0, a2, s2, s3, fg, kern2, kern3]
    in_specs = [
        pl.BlockSpec((4, 3, rows, 512), lambda i: (i, 0, 0, 0)),
        pl.BlockSpec((2, 2, rows, 768), lambda i: (i, 0, 0, 0)),
        pl.BlockSpec((2, 2, rows, 768), lambda i: (i, 0, 0, 0)),
        *[pl.BlockSpec(memory_space=pl.ANY)] * 5,
        *[once(v.shape) for v in args[8:]],
    ]
    scratch = [
        *[pltpu.VMEM(v.shape, BF16) for v in args[3:8]],
        pltpu.SemaphoreType.DMA((5,)),
        pltpu.VMEM((3, 2, 768, 256), BF16),
        pltpu.VMEM((4, rows, 768), BF16),
        pltpu.VMEM((11, rows, 512), BF16),
        pltpu.VMEM((11, rows, 640), BF16),
        *[pltpu.VMEM(s, BF16) for s in BANDS[1:]],
        *[pltpu.VMEM(s, F32) for s in sums],
    ]
    outs = own
    params = {}
    if summed is not None:
        args += summed
        block = (2, *AXES.values(), 16, HALF)
        in_specs += [pl.BlockSpec(memory_space=pl.ANY), once((16, 128))]
        outs = [(2, 16, HALF), (16, 128), (80, 128)]
        buffers = flow_buffers(SUM_FLOWS)
        scratch = [pltpu.VMEM(s, F32) for s in own] + scratch
        scratch += [
            pltpu.VMEM(block, BF16),
            pltpu.VMEM((8, 16, 128), F32),
            pltpu.VMEM((4, 16, 128), F32),
            pltpu.VMEM((8, 80, 128), BF16),
            pltpu.VMEM((8, 80, 128), BF16),
            pltpu.VMEM((4, 80, 128), F32),
            pltpu.SemaphoreType.DMA((len(SUM_FLOWS),)),
            pltpu.SemaphoreType.DMA((2, len(buffers), 3)),
            pltpu.SemaphoreType.DMA((4, 7)),
            pltpu.SemaphoreType.DMA((4, 7)),
            *[pltpu.VMEM(s, BF16) for s in buffers],
        ]
        params = dict(collective_id=1, has_side_effects=True)
    return pl.pallas_call(
        functools.partial(backward_kernel, summed is not None),
        grid=(5,),
        in_specs=in_specs,
        out_specs=[once(s) for s in outs],
        out_shape=[jax.ShapeDtypeStruct(s, F32) for s in outs],
        scratch_shapes=scratch,
        compiler_params=pltpu.CompilerParams(vmem_limit_bytes=VMEM_LIMIT, **params),
        name="torso_backward",
    )(*args)


def high_low(v):
    high = v.astype(BF16)
    return high, (v - high.astype(F32)).astype(BF16)


HEAD_COLUMNS = [(0, 1024), (1024, 2048), (2048, HALF)]


def heads_kernel(atoms, acts, paired, f_ref, w_ref, bias_ref, slot_ref, row_ref, dw_out, fg_ref, prio_ref, stat_ref, *refs):
    if paired:
        dw_ref, arrived, w_hbm, w_ref, summed, dw_hbm = *refs[:2], w_ref, refs[2], refs[3], dw_out
        send, recv, load, save = refs[4:]
        loads = [pltpu.make_async_copy(w_hbm.at[h], w_ref.at[h], load.at[h]) for h in range(2)]
        start(loads)
        me = coordinates()
        other = device_at({**me, "c": 1 - me["c"]})
        barrier = pltpu.get_barrier_semaphore()
        pl.semaphore_signal(barrier, inc=1, **other)

        def to_core(h, k):
            lo, hi = HEAD_COLUMNS[k]
            src = dw_ref.at[h, :, 1 - me["c"], :, :, :, lo:hi]
            return pltpu.make_async_remote_copy(src, arrived.at[h, :, :, :, :, lo:hi], send.at[h, k], recv.at[h, k], **other)

        def saving(h, k):
            lo, hi = HEAD_COLUMNS[k]
            return pltpu.make_async_copy(summed.at[h, :, :, :, :, lo:hi], dw_hbm.at[h, :, :, :, :, lo:hi], save.at[h, k])

        def add_core(h, k):
            lo, hi = HEAD_COLUMNS[k]
            to_core(h, k).wait()

            def one(j, _):
                x, z, y = j // 8, (j // 2) % 4, j % 2
                own = dw_ref[h, x, me["c"], z, y, :, lo:hi]
                summed[h, x, z, y, :, lo:hi] = own + arrived[h, x, z, y, :, lo:hi]
                return 0

            lax.fori_loop(0, 16, one, 0)
            saving(h, k).start()


    def put(h, lo, hi, v):
        v = v.astype(BF16)
        if paired:
            dw_ref[h, :, :, :, :, :, lo:hi] = v.reshape(2, 2, 4, 2, 16, hi - lo)
        else:
            dw_out[h, :, lo:hi] = v

    rows = f_ref.shape[0]
    slots = slot_ref.shape[0]
    wide = 1024
    lane = lax.broadcasted_iota(jnp.int32, (1, wide), 1)
    selt = jnp.where(lax.broadcasted_iota(jnp.int32, (rows, slots), 0) == row_ref[...], 1.0, 0.0).astype(BF16)
    action = slot_ref[:, atoms + 2 : atoms + 3]
    which = jnp.where(lane < atoms, -1, jnp.where(lane < atoms * (acts + 1), (lane - atoms) // atoms, -2)).astype(F32)
    coeff = jnp.where(which == -1.0, 1.0, 0.0) + jnp.where(which == action, 1.0, 0.0) - jnp.where(which >= 0.0, 1.0 / acts, 0.0)
    atom = jnp.where(which >= -1.0, lane - atoms * (which.astype(jnp.int32) + 1), -1)
    fold = jnp.where(lax.broadcasted_iota(jnp.int32, (128, wide), 0) == atom, 1.0, 0.0).astype(BF16)
    feats = f_ref[...]
    pre = []
    for k in range(2):
        if paired:
            loads[k].wait()
        pre.append(dot_nt(feats, w_ref[k, :, :3200]))
    hidden, slope = [], []
    for k in range(2):
        a, s = silu_and_slope(pre[k])
        hidden.append(a.astype(BF16))
        slope.append(s)
    out_w = jnp.concatenate([w_ref[0, :, 3200:], w_ref[1, :, 3200:]], axis=1)
    zero = jnp.zeros((), BF16)
    w_val = jnp.where(lane[:, :128] < atoms, out_w[:, :128].astype(F32), 0.0).astype(BF16)
    w_adv = jnp.where(lane >= atoms, out_w.astype(F32), 0.0).astype(BF16)
    outs = bias_ref.shape[1]
    bias = jnp.concatenate([bias_ref[...], jnp.zeros((1, wide - outs), F32)], axis=1)
    logits = dot(hidden[1], w_adv) + bias
    logits = jnp.concatenate([logits[:, :128] + dot(hidden[0], w_val), logits[:, 128:]], axis=1)
    high, low = high_low(logits)
    per_slot = dot_tn(selt, high) + dot_tn(selt, low)
    high, low = high_low(per_slot * coeff)
    q = dot_nt(high, fold) + dot_nt(low, fold)
    lane_q = lax.broadcasted_iota(jnp.int32, (slots, 128), 1)
    used = lane_q < atoms
    top = jnp.max(jnp.where(used, q, -jnp.inf), axis=1, keepdims=True)
    shifted = jnp.where(used, jnp.exp(jnp.where(used, q - top, 0.0)), 0.0)
    total = jnp.sum(shifted, axis=1, keepdims=True)
    tgt = jnp.where(used, slot_ref[...], 0.0)
    cross = -jnp.sum(jnp.where(used, tgt * (q - top - jnp.log(total)), 0.0), axis=1, keepdims=True)
    coef = slot_ref[:, atoms : atoms + 1]
    valid = slot_ref[:, atoms + 1 : atoms + 2]
    prio_ref[...] = jnp.transpose(jnp.broadcast_to(valid * cross, (slots, 128)))[0:1]
    q_grad = coef * (shifted * (jnp.sum(tgt, axis=1, keepdims=True) / total) - tgt)
    high, low = high_low(q_grad)
    lgrad = ((dot(high, fold) + dot(low, fold)) * coeff).astype(BF16)
    bias_grad = jnp.sum(lgrad.astype(F32), axis=0, keepdims=True)
    for k in range(8):
        stat_ref[k : k + 1, :] = bias_grad[:, 128 * k : 128 * k + 128]
    stat_ref[8:9, :] = jnp.broadcast_to(jnp.sum(coef * cross, axis=0, keepdims=True), (1, 128))
    stat_ref[9:10, :] = jnp.broadcast_to(jnp.sum(valid, axis=0, keepdims=True), (1, 128))
    stat_ref[10:16, :] = jnp.zeros((6, 128), F32)
    grad = dot(selt, lgrad).astype(BF16)
    d_adv = dot_tn(hidden[1], grad)
    d_val = dot_tn(hidden[0], grad[:, :128])
    put(0, 3200, 3328, jnp.where(lane[:, :128] < atoms, d_val, d_adv[:, :128]))
    put(0, 3328, HALF, d_adv[:, 128:512])
    put(1, 3200, HALF, d_adv[:, 512:])
    pre_grad = [
        (dot_nt(grad[:, :128], w_val) * slope[0]).astype(BF16),
        (dot_nt(grad, w_adv) * slope[1]).astype(BF16),
    ]
    for k in range(2):
        for part, (lo, hi) in enumerate(((0, 1024), (1024, 2048), (2048, 3200))):
            put(k, lo, hi, dot_tn(pre_grad[k], f_ref[:, lo:hi]))
            if paired:
                if (k, part) == (0, 0):
                    pl.semaphore_wait(barrier, 1)
                to_core(k, part).start()
    for part, (lo, hi) in enumerate(((0, 1024), (1024, 2048), (2048, 3200))):
        back = dot(pre_grad[0], w_ref[0, :, lo:hi]) + dot(pre_grad[1], w_ref[1, :, lo:hi])
        fg_ref[:, lo:hi] = back.astype(BF16)
        if paired:
            add_core(0, part)
    if paired:
        for part in range(3):
            add_core(1, part)
        for h in range(2):
            for part in range(3):
                saving(h, part).wait()


def heads(atoms, acts, feats, weights, bias, per_slot, rows_of_slot, paired=False):
    slots = per_slot.shape[0]
    block = (2, 2, 4, 2, 16, HALF)
    scratch, params = [], {}
    if paired:
        scratch = [
            pltpu.VMEM((2, 2, 2, 4, 2, 16, HALF), BF16),
            pltpu.VMEM(block, BF16),
            pltpu.VMEM(weights.shape, BF16),
            pltpu.VMEM(block, BF16),
            *[pltpu.SemaphoreType.DMA((2, 3)) for _ in range(2)],
            pltpu.SemaphoreType.DMA((2,)),
            pltpu.SemaphoreType.DMA((2, 3)),
        ]
        params = dict(collective_id=3, has_side_effects=True)
    vmem = pl.BlockSpec(memory_space=pltpu.VMEM)
    large = pl.BlockSpec(memory_space=pl.ANY) if paired else vmem
    return pl.pallas_call(
        functools.partial(heads_kernel, atoms, acts, paired),
        in_specs=[vmem, large, vmem, vmem, vmem],
        out_specs=[large, vmem, vmem, vmem],
        out_shape=[
            jax.ShapeDtypeStruct(block if paired else weights.shape, BF16),
            jax.ShapeDtypeStruct(feats.shape, BF16),
            jax.ShapeDtypeStruct((1, slots), F32),
            jax.ShapeDtypeStruct((16, 128), F32),
        ],
        scratch_shapes=scratch,
        compiler_params=pltpu.CompilerParams(vmem_limit_bytes=VMEM_LIMIT, **params),
        name="heads",
    )(feats, weights, bias, per_slot, rows_of_slot[None, :])


def finish_kernel(
    dsum, stat, kern, fn, hn, on, loss, g1, g2, g3t, mean_g, spread_g, bias_g, val_g, val_s, adv_g, adv_s, out_g
):
    feat, atoms, outs = fn.shape[1], val_g.shape[1], on.shape[1]
    inverse = 1.0 / stat[9:10, 0:1]
    loss[...] = stat[8:9, 0:1] * inverse
    v = kern[...]
    turned = pltpu.roll(v, 64, 1)
    g2[0:32, :] = v[0:32, 0:64]
    g2[32:64, :] = turned[0:32, 0:64]
    third = jnp.concatenate([v[32:64], turned[32:64], v[64:72], jnp.zeros((56, 128), F32)], axis=0)
    g3t[...] = jnp.transpose(third)[0:64, 0:72]
    for k in range(4):
        g1[8 * k : 8 * k + 8, :] = v[72:80, 32 * k : 32 * k + 32]
    for h in range(2):
        mean = dsum[h, :, 0:feat] * inverse
        mean_g[h] = mean
        spread_g[h] = mean * fn[h : h + 1, :] * as_column(hn[0, h : h + 1, :])
        bias_g[h : h + 1, :] = as_row(dsum[h, :, feat : feat + 1] * inverse)
    out = jnp.concatenate([dsum[0, :, 3200:], dsum[1, :, 3200:]], axis=1) * inverse
    val, adv = out[:, :atoms], out[:, atoms:outs]
    val_g[...] = val
    val_s[...] = val * as_column(hn[1, 0:1, :]) * on[:, :atoms]
    adv_g[...] = adv
    adv_s[...] = adv * as_column(hn[1, 1:2, :]) * on[:, atoms:]
    out_g[...] = jnp.concatenate([stat[k : k + 1, :] for k in range(8)], axis=1)[:, :outs] * inverse


def outputs(dsum, stat, kern, fn, hn, on, atoms):
    feat, outs = fn.shape[1], on.shape[1]
    shapes = [(1, 1), (32, 32), (64, 64), (64, 72), (2, 16, feat), (2, 16, feat), (2, 16)]
    shapes += [(16, atoms)] * 2 + [(16, outs - atoms)] * 2 + [(1, outs)]
    return pl.pallas_call(
        finish_kernel,
        out_shape=[jax.ShapeDtypeStruct(s, F32) for s in shapes],
        compiler_params=pltpu.CompilerParams(vmem_limit_bytes=VMEM_LIMIT),
        name="outputs",
    )(dsum, stat, kern, fn, hn, on)


def exchange_kernel(count, kern_ref, slot_ref, kerns_out, slots_out, send_kern, recv_kern, send_slot, recv_slot, own):
    me = lax.axis_index("dp")
    peers = [lax.rem(me + k, count) for k in range(count)]
    barrier = pltpu.get_barrier_semaphore()
    for k in range(1, count):
        pl.semaphore_signal(barrier, inc=1, device_id={"dp": peers[k]}, device_id_type=pl.DeviceIdType.MESH)
    pl.semaphore_wait(barrier, count - 1)
    mine = [
        pltpu.make_async_copy(kern_ref, kerns_out.at[me], own.at[0]),
        pltpu.make_async_copy(slot_ref.at[me], slots_out.at[me], own.at[1]),
    ]
    sent = []
    for k in range(1, count):
        to = dict(device_id={"dp": peers[k]}, device_id_type=pl.DeviceIdType.MESH)
        sent.append(pltpu.make_async_remote_copy(kern_ref, kerns_out.at[me], send_kern.at[k], recv_kern.at[k], **to))
        sent.append(pltpu.make_async_remote_copy(slot_ref.at[peers[k]], slots_out.at[me], send_slot.at[k], recv_slot.at[k], **to))
    for copy in mine + sent:
        copy.start()
    for copy in mine + sent:
        copy.wait()


def exchange(kern, slot):
    count = slot.shape[0]
    return pl.pallas_call(
        functools.partial(exchange_kernel, count),
        in_specs=[pl.BlockSpec(memory_space=pltpu.VMEM)] * 2,
        out_specs=[pl.BlockSpec(memory_space=pltpu.VMEM)] * 2,
        out_shape=[jax.ShapeDtypeStruct((count, *kern.shape), kern.dtype), jax.ShapeDtypeStruct(slot.shape, slot.dtype)],
        scratch_shapes=[pltpu.SemaphoreType.DMA((count,))] * 4 + [pltpu.SemaphoreType.DMA((2,))],
        compiler_params=pltpu.CompilerParams(collective_id=2, has_side_effects=True, vmem_limit_bytes=VMEM_LIMIT),
        name="exchange",
    )(kern, slot)


def on_device(
    frames,
    send_rows,
    recv_counts,
    actions,
    target_dist,
    sample_weight,
    conv_first,
    conv_second,
    conv_third,
    hidden_mean,
    hidden_spread,
    hidden_bias,
    feature_noise,
    hidden_noise,
    value_mean,
    value_spread,
    advantage_mean,
    advantage_spread,
    output_noise,
    output_bias,
):
    dp_count = lax.axis_size("dp")
    slots = send_rows.shape[0]
    capacity = slots // dp_count
    atoms = value_mean.shape[1]
    acts = advantage_mean.shape[1] // atoms
    rows = frames.shape[0]
    feat, own = hidden_mean.shape[1:]
    outs = atoms * (acts + 1)

    x = frames.transpose(1, 0, 2).reshape(21, 4, rows, 336)
    bias = output_bias[None, :]
    mean_t = hidden_mean.transpose(0, 2, 1)
    spread_t = hidden_spread.transpose(0, 2, 1)

    if (dp_count, lax.axis_size("mp"), own, slots) == (8, 4, 16, 512):
        noise = output_noise[None, :]
        shared = [mean_t, spread_t, hidden_bias, feature_noise, hidden_noise]
        shared += [value_mean, value_spread, advantage_mean, advantage_spread, noise]
        shared += [target_dist.T, recv_counts[None, :], actions[None, :], sample_weight[None, :]]
        kernels = [conv_first, conv_second, conv_third.T]
        a1, s1, a2, s2, feats, s3, y, y0, weights, per_slot, kern2, kern3 = torso_forward(x, kernels, shared)
        weights, per_slot = weights.reshape(2, 512, HALF), per_slot.reshape(slots, 128)
        dweights, feat_grad, prio, stat = heads(atoms, acts, feats, weights, bias, per_slot, send_rows, paired=True)
        summed = [dweights, stat]
        summed = torso_backward(y, y0, a1, s1, a2, s2, s3, feat_grad, kern2, kern3, summed=summed)
        loss, g1, g2, g3t, mean_g, spread_g, bias_g, *outer, out_g = outputs(
            *summed, feature_noise, hidden_noise, noise, atoms
        )
        return (
            loss[0, 0],
            g1,
            g2,
            g3t.T,
            mean_g.transpose(0, 2, 1),
            spread_g.transpose(0, 2, 1),
            bias_g,
            *outer,
            out_g[0],
            prio[0],
        )

    sizes = [w.size for w in (conv_first, conv_second, conv_third)]
    flat = jnp.concatenate([w.astype(BF16).reshape(-1) for w in (conv_first, conv_second, conv_third)])
    tall = -(-flat.size // 2048) * 16
    flat = jnp.pad(flat, (0, tall * 128 - flat.size)).reshape(tall, 128)
    is_valid = jnp.arange(capacity, dtype=jnp.int32)[None, :] < recv_counts[:, None]
    is_valid = is_valid.astype(F32).reshape(slots)
    per_slot = jnp.stack([is_valid * sample_weight, is_valid, actions.astype(F32)], axis=1)
    per_slot = jnp.concatenate([target_dist, per_slot, jnp.zeros((slots, 125 - atoms), F32)], axis=1)
    flat, per_slot = exchange(flat, per_slot.reshape(dp_count, capacity, 128))
    per_slot = per_slot.reshape(slots, 128)
    flat = flat.reshape(dp_count, -1)
    kern1 = jnp.tile(flat[:, : sizes[0]].reshape(-1, 32), (1, 4))
    kern2 = jnp.tile(flat[:, sizes[0] : sizes[0] + sizes[1]].reshape(-1, 64), (1, 2))
    kern3 = jnp.tile(flat[:, sizes[0] + sizes[1] : sum(sizes)].reshape(-1, 64), (1, 2))

    wide_one = mean_t + spread_t * feature_noise[:, None, :] * hidden_noise[0][:, :, None]
    wide_one = jnp.concatenate([wide_one, hidden_bias[:, :, None], jnp.zeros((2, own, 63), F32)], axis=2)
    wide_val = value_mean + value_spread * hidden_noise[1, 0][:, None] * output_noise[None, :atoms]
    wide_adv = advantage_mean + advantage_spread * hidden_noise[1, 1][:, None] * output_noise[None, atoms:]
    wide_out = jnp.concatenate([wide_val, wide_adv, jnp.zeros((own, 1024 - outs), F32)], axis=1)
    wide_out = wide_out.reshape(own, 2, 512).transpose(1, 0, 2)
    shard = jnp.concatenate([wide_one, wide_out], axis=2).astype(BF16)
    weights = lax.all_gather(shard, ("mp", "dp"), axis=1, tiled=True)

    a1, s1, a2, s2, feats, s3, y, y0 = torso_forward(x, [kern1, kern2, kern3])
    dweights, feat_grad, prio, stat = heads(atoms, acts, feats, weights, bias, per_slot, send_rows)
    dshard = lax.psum_scatter(dweights, ("mp", "dp"), scatter_dimension=1, tiled=True).astype(F32)
    stat = lax.psum(stat, ("dp", "mp"))
    inverse = 1.0 / stat[9, 0]
    k1, k2, k3 = torso_backward(y, y0, a1, s1, a2, s2, s3, feat_grad, kern2, kern3)
    kflat = jnp.concatenate([g.reshape(dp_count, -1) for g in (k1[:, :32], k2[:, :64], k3[:, :64])], axis=1)
    kflat = lax.psum(lax.psum_scatter(kflat, "dp", scatter_dimension=0, tiled=True)[0], "mp") * inverse
    conv_grads = (
        kflat[: sizes[0]].reshape(conv_first.shape),
        kflat[sizes[0] : sizes[0] + sizes[1]].reshape(conv_second.shape),
        kflat[sizes[0] + sizes[1] :].reshape(conv_third.shape),
    )
    dshard = dshard * inverse
    mean_grad_t = dshard[:, :, :feat]
    spread_grad_t = mean_grad_t * feature_noise[:, None, :] * hidden_noise[0][:, :, None]
    out_grad = dshard[:, :, 3200:].transpose(1, 0, 2).reshape(own, 1024)
    value_mean_grad = out_grad[:, :atoms]
    adv_mean_grad = out_grad[:, atoms:outs]
    return (
        stat[8, 0] * inverse,
        *conv_grads,
        mean_grad_t.transpose(0, 2, 1),
        spread_grad_t.transpose(0, 2, 1),
        dshard[:, :, feat],
        value_mean_grad,
        value_mean_grad * hidden_noise[1, 0][:, None] * output_noise[None, :atoms],
        adv_mean_grad,
        adv_mean_grad * hidden_noise[1, 1][:, None] * output_noise[None, atoms:],
        stat[:8].reshape(-1)[:outs] * inverse,
        prio[0],
    )


def solution(mesh):
    both, heads_dim = P(("dp", "mp")), P(("mp", "dp"), None)
    return jax.shard_map(
        on_device,
        mesh=mesh,
        in_specs=(
            P(("dp", "mp"), None, None),
            both,
            both,
            both,
            P(("dp", "mp"), None),
            both,
            P("dp", None),
            P("dp", None),
            P("dp", None),
            P(None, None, ("mp", "dp")),
            P(None, None, ("mp", "dp")),
            P(None, ("mp", "dp")),
            P(),
            P(None, None, ("mp", "dp")),
            heads_dim,
            heads_dim,
            heads_dim,
            heads_dim,
            P(),
            P(),
        ),
        out_specs=(
            P(),
            P("dp", None),
            P("dp", None),
            P("dp", None),
            P(None, None, ("mp", "dp")),
            P(None, None, ("mp", "dp")),
            P(None, ("mp", "dp")),
            heads_dim,
            heads_dim,
            heads_dim,
            heads_dim,
            P(),
            both,
        ),
        check_vma=False,
    )
```

```python
import functools

import jax
import jax.numpy as jnp
from jax import lax
from jax.experimental import pallas as pl
from jax.experimental.pallas import tpu as pltpu
from jax.sharding import PartitionSpec as P

F32 = jnp.float32
BF16 = jnp.bfloat16
VMEM_LIMIT = 60 * 1024 * 1024


def sigmoid(v):
    return 0.5 * jnp.tanh(0.5 * v) + 0.5


def silu_and_slope(v):
    s = sigmoid(v)
    a = v * s
    return a, s + a * (1.0 - s)


def dot(a, b):
    return lax.dot_general(a, b, (((1,), (0,)), ((), ())), preferred_element_type=F32)


def dot_nt(a, b):
    return lax.dot_general(a, b, (((1,), (1,)), ((), ())), preferred_element_type=F32)


def dot_tn(a, b):
    return lax.dot_general(a, b, (((0,), (0,)), ((), ())), preferred_element_type=F32)


def columns_of_one():
    return [7 * (g // 8) + g % 8 if g % 8 < 7 and 7 * (g // 8) + g % 8 < 20 else -9 for g in range(24)]


def half_lanes(left, right, rows):
    lane = lax.broadcasted_iota(jnp.int32, (rows, 128), 1)
    zero = jnp.zeros((rows, 128), F32)
    return jnp.where(lane < 64, zero if left is None else left, zero if right is None else right)


def fill_band_one(k1_ref, band):
    lane = lax.broadcasted_iota(jnp.int32, (16, 128), 1) // 32
    for u in range(8):
        taps = [k1_ref[((u // 4) * 2 + v) * 64 + (u % 4) * 16 :][:16].astype(F32) for v in range(2)]
        for g in range(8):
            for h in range(2):
                col = lane + 4 * h
                here = jnp.where((col == g) & (col < 7), taps[0], 0.0) + jnp.where((col == g - 1) & (col < 7), taps[1], 0.0)
                band[128 * u + 16 * g : 128 * u + 16 * g + 16, 128 * h : 128 * h + 128] = here.astype(BF16)


def fill_band_two(k2_ref, band):
    cols = columns_of_one()
    for u in range(4):

        def tap(v):
            at = ((u // 2) * 2 + v // 2) * 128 + ((u % 2) * 2 + v % 2) * 32
            return k2_ref[at : at + 32, :].astype(F32)

        for g, q in enumerate(cols):
            if q < 0:
                continue
            used = {(q - v) // 2: v for v in (q % 2, q % 2 + 2) if 0 <= (q - v) // 2 < 9}
            for m in sorted({c // 2 for c in used}):
                sides = [tap(used[2 * m + side]) if 2 * m + side in used else None for side in range(2)]
                band[u, 32 * g : 32 * g + 32, 128 * m : 128 * m + 128] = half_lanes(*sides, 32).astype(BF16)


def fill_band_three(k3_ref, band):
    for u in range(3):

        def tap(v):
            return k3_ref[(u * 3 + v) * 64 : (u * 3 + v) * 64 + 64, :].astype(F32)

        for q in range(9):
            used = {q - v: v for v in range(3) if 0 <= q - v < 7}
            for m in sorted({c // 2 for c in used}):
                sides = [tap(used[2 * m + side]) if 2 * m + side in used else None for side in range(2)]
                band[u, 64 * q : 64 * q + 64, 128 * m : 128 * m + 128] = half_lanes(*sides, 64).astype(BF16)


def fold_lanes(v, width):
    step = 64
    while step >= width:
        v = v + pltpu.roll(v, step, 1)
        step //= 2
    return v


def take_band_one(d1, out):
    lane = lax.broadcasted_iota(jnp.int32, (16, 128), 1) // 32
    for u in range(8):
        for v in range(2):
            total = jnp.zeros((16, 128), F32)
            for col in range(7):
                at = 128 * u + 16 * (col + v)
                h = col // 4
                total = total + jnp.where(lane + 4 * h == col, d1[at : at + 16, 128 * h : 128 * h + 128], 0.0)
            at = ((u // 4) * 2 + v) * 64 + (u % 4) * 16
            out[at : at + 16, :] = total
    out[...] = fold_lanes(out[...], 32)


def take_band_two(blocks, out):
    cols = columns_of_one()
    lane = lax.broadcasted_iota(jnp.int32, (32, 128), 1)
    for u in range(4):
        for v in range(4):
            total = jnp.zeros((32, 128), F32)
            for ref, first, c0, count in blocks:
                for c in range(count):
                    at = 32 * (cols.index(2 * (c0 + c) + v) - first)
                    piece = ref[u, at : at + 32, 128 * (c // 2) : 128 * (c // 2) + 128]
                    total = total + jnp.where((lane < 64) == (c % 2 == 0), piece, 0.0)
            at = ((u // 2) * 2 + v // 2) * 128 + ((u % 2) * 2 + v % 2) * 32
            out[at : at + 32, :] = total
    out[...] = fold_lanes(out[...], 64)


def take_band_three(d3, out):
    lane = lax.broadcasted_iota(jnp.int32, (64, 128), 1)
    for u in range(3):
        for v in range(3):
            total = jnp.zeros((64, 128), F32)
            for c in range(4):
                piece = d3[u, 64 * (c + v) : 64 * (c + v) + 64, 128 * (c // 2) : 128 * (c // 2) + 128]
                total = total + jnp.where((lane < 64) == (c % 2 == 0), piece, 0.0)
            at = (u * 3 + v) * 64
            out[at : at + 64, :] = total
    out[...] = fold_lanes(out[...], 64)


def coordinates():
    d, m = lax.axis_index("dp"), lax.axis_index("mp")
    return {"z": d // 2, "y": d % 2, "x": m // 2, "c": m % 2}


def device_at(at):
    return dict(
        device_id={"dp": at["z"] * 2 + at["y"], "mp": at["x"] * 2 + at["c"]}, device_id_type=pl.DeviceIdType.MESH
    )


AXES = {"x": 2, "z": 4, "y": 2}
HALF = 3712
CUTS = [(0, 1408, "zyx", "zxy"), (1408, 2816, "zyx", "zxy"), (2816, HALF, "xyz", "yxz")]
GATHER_FLOWS = [(half, lo, hi, orders[half]) for lo, hi, *orders in CUTS for half in range(2)]
SUM_FLOWS = [(half, lo, hi, order[::-1]) for half, lo, hi, order in GATHER_FLOWS]
GATHER_FIRST = [(4, 0), (5, 0), (0, 0)]
GATHER_PLAN = {(0, 0): [(4, 1), (5, 1), (1, 0), (0, 1)], (0, 1): [(2, 0)], (0, 3): [(1, 1)], (1, 0): [(3, 0)], (1, 3): [(2, 1), (0, 2)], (1, 5): [(4, 2)], (2, 1): [(1, 2)], (3, 0): [(3, 1)], (3, 4): [(5, 2)], (3, 5): [(2, 2)], (4, 1): [(3, 2)]}
GATHER_LAST = []
GATHER_DONE = [0, 4, 1, 2, 5, 3]
SUM_FIRST = [(0, 0), (1, 0), (4, 0)]
SUM_PLAN = {(0, 2): [(2, 0), (3, 0)], (0, 4): [(5, 0)], (1, 4): [(0, 1), (1, 1)], (2, 0): [(2, 1), (3, 1)], (2, 4): [(0, 2)], (2, 5): [(4, 1), (5, 1)], (2, 6): [(1, 2)], (3, 2): [(4, 2), (5, 2)], (3, 5): [(2, 2)], (4, 2): [(3, 2)]}
SUM_LAST = []
SUM_DONE = [0, 4, 5, 1, 2, 3]

def flow_buffers(flows):
    shapes = []
    for _, lo, hi, order in flows:
        for s, axis in enumerate(order):
            rest = [AXES[a] for a in AXES if a in order[s + 1 :]]
            shapes.append((AXES[axis] - 1, *rest, 16, hi - lo))
    return shapes


def peers_of(axis):
    me = coordinates()
    n = AXES[axis]
    return [{**me, axis: lax.rem(me[axis] + k, n)} for k in range(1, n)]


def block_of(ref, half, lo, hi, at):
    return ref.at[(half, *[at.get(a, slice(None)) for a in AXES], slice(None), slice(lo, hi))]


def sum_copies(acc, flow, stage, buf, send, recv):
    half, lo, hi, order = flow
    me = coordinates()
    held = {a: me[a] for a in order[:stage]}
    copies = []
    for k, peer in enumerate(peers_of(order[stage])):
        src = block_of(acc, half, lo, hi, {**held, order[stage]: peer[order[stage]]})
        copies.append(pltpu.make_async_remote_copy(src, buf.at[k], send.at[k], recv.at[k], **device_at(peer)))
    return copies


def add_arrived(acc, flow, stage, buf, out=None):
    half, lo, hi, order = flow
    me = coordinates()
    own = block_of(acc, half, lo, hi, {a: me[a] for a in order[: stage + 1]})
    if out is None and AXES[order[stage]] == 2:
        own[...] = own[...] + buf[0]
        return
    total = own[...].astype(F32)
    for k in range(AXES[order[stage]] - 1):
        total = total + buf[k].astype(F32)
    if out is None:
        own[...] = total.astype(BF16)
    else:
        out[half, :, lo:hi] = total


def everyone(axis, count):
    me = lax.axis_index(axis)
    return [dict(device_id={axis: lax.rem(me + k, count)}, device_id_type=pl.DeviceIdType.MESH) for k in range(1, count)]


def share(axis, count, src, buf, send, recv):
    me = lax.axis_index(axis)
    return [
        pltpu.make_async_remote_copy(src(k), buf.at[me], send.at[k], recv.at[k], **to)
        for k, to in enumerate(everyone(axis, count))
    ]


def in_order(buf, count):
    total = buf[0].astype(F32)
    for k in range(1, count):
        total = total + buf[k].astype(F32)
    return total


def gathered_block(ref, half, lo, hi, core, at):
    x, z, y = (at.get(a, slice(None)) for a in AXES)
    return ref.at[half, x, core, z, y, :, lo:hi]


def gather_copies(shard, out, flow, stage, send, recv):
    half, lo, hi, order = flow
    me = coordinates()
    at = {a: me[a] for a in order[stage:]}
    dst = gathered_block(out, half, lo, hi, me["c"], at)
    src = shard.at[half, :, lo:hi] if stage == 0 else dst
    return [
        pltpu.make_async_remote_copy(src, dst, send.at[k], recv.at[k], **device_at(peer))
        for k, peer in enumerate(peers_of(order[stage]))
    ]


def core_copies(out, flow, last, send, recv):
    half, lo, hi, order = flow
    me = coordinates()
    other = {**me, "c": 1 - me["c"]}
    copies = []
    for k, at in enumerate([peer[order[2]] for peer in peers_of(order[2])] if last else [me[order[2]]]):
        block = gathered_block(out, half, lo, hi, me["c"], {order[2]: at})
        copies.append(pltpu.make_async_remote_copy(block, block, send.at[k], recv.at[k], **device_at(other)))
    return copies


def start(copies):
    for copy in copies:
        copy.start()


def finish(copies):
    for copy in copies:
        copy.wait()


def greet():
    for to in everyone("dp", 8) + everyone("mp", 4):
        pl.semaphore_signal(pltpu.get_barrier_semaphore(), inc=1, **to)


def greeted():
    pl.semaphore_wait(pltpu.get_barrier_semaphore(), 10)


def as_column(row):
    n = row.shape[1]
    eye = lax.broadcasted_iota(jnp.int32, (n, n), 0) == lax.broadcasted_iota(jnp.int32, (n, n), 1)
    return jnp.sum(jnp.where(eye, row, 0.0), axis=1, keepdims=True)


def as_row(column):
    n = column.shape[0]
    eye = lax.broadcasted_iota(jnp.int32, (n, n), 0) == lax.broadcasted_iota(jnp.int32, (n, n), 1)
    return jnp.sum(jnp.where(eye, column, 0.0), axis=0, keepdims=True)


def pack_shards(c1, c2, c3t):
    c3 = jnp.transpose(jnp.concatenate([c3t, jnp.zeros((64, 56), F32)], axis=1))
    blank = jnp.zeros((8, 64), F32)
    return jnp.concatenate(
        [
            jnp.concatenate([c2[0:32], c2[32:64]], axis=1),
            jnp.concatenate([c3[0:32], c3[32:64]], axis=1),
            jnp.concatenate([c3[64:72], blank], axis=1),
            jnp.concatenate([c1[8 * k : 8 * k + 8] for k in range(4)], axis=1),
        ],
        axis=0,
    )


def unpack_shards(d, v, k1, k2, k3):
    lane = lax.broadcasted_iota(jnp.int32, (32, 128), 1)

    def sides(w):
        turned = pltpu.roll(w, 64, 1)
        low = lane[: w.shape[0]] < 64
        return jnp.where(low, w, turned), jnp.where(low, turned, w)

    k2[64 * d : 64 * d + 32, :], k2[64 * d + 32 : 64 * d + 64, :] = sides(v[0:32])
    k3[72 * d : 72 * d + 32, :], k3[72 * d + 32 : 72 * d + 64, :] = sides(v[32:64])
    k3[72 * d + 64 : 72 * d + 72, :] = sides(v[64:72])[0]
    for k in range(4):
        part = jnp.where(lane[:8] // 32 == k, v[72:80], 0.0)
        k1[32 * d + 8 * k : 32 * d + 8 * k + 8, :] = fold_lanes(part, 32)


def noisy_weights(shard, hm, hs, hb, fn, hn, vm, vs, am, adv_s, on):
    atoms, outs = vm.shape[1], on.shape[1]
    lane = lax.broadcasted_iota(jnp.int32, (16, 128), 1)
    for h in range(2):
        wide = hm[h] + hs[h] * fn[h : h + 1, :] * as_column(hn[0, h : h + 1, :])
        shard[h, :, 0:3072] = wide[:, 0:3072].astype(BF16)
        last = jnp.concatenate([wide[:, 3072:], jnp.zeros((16, 64), F32)], axis=1)
        last = jnp.where(lane == 64, as_column(hb[h : h + 1, :]), last)
        shard[h, :, 3072:3200] = last.astype(BF16)
    val = vm[...] + vs[...] * as_column(hn[1, 0:1, :]) * on[:, :atoms]
    adv = am[...] + adv_s[...] * as_column(hn[1, 1:2, :]) * on[:, atoms:]
    out = jnp.concatenate([val, adv, jnp.zeros((16, 1024 - outs), F32)], axis=1).astype(BF16)
    shard[0, :, 3200:] = out[:, :512]
    shard[1, :, 3200:] = out[:, 512:]


def slot_rows(staged, tt, cnt, act, sw):
    atoms, slots = tt.shape
    lane = lax.broadcasted_iota(jnp.int32, (8, slots), 1)
    source = lax.broadcasted_iota(jnp.int32, (8, slots), 0)
    cap = slots // 8
    used = jnp.sum(jnp.where(lane // cap == source, as_column(cnt[...].astype(F32)), 0.0), axis=0, keepdims=True)
    valid = jnp.where((lane[0:1] % cap).astype(F32) < used, 1.0, 0.0)
    staged[...] = jnp.zeros_like(staged)
    staged[0:atoms, :] = tt[...]
    staged[atoms : atoms + 1, :] = valid * sw[...]
    staged[atoms + 1 : atoms + 2, :] = valid
    staged[atoms + 2 : atoms + 3, :] = act[...].astype(F32)
    return jnp.transpose(staged[...])


def shifted_blocks(x):
    rows = x.shape[0]
    return (
        x[:, 0:128],
        x[:, 112:240],
        jnp.concatenate([x[:, 224:336], jnp.zeros((rows, 16), x.dtype)], axis=1),
    )


def forward_kernel(shared, *refs):
    if shared:
        ins, refs = refs[:18], refs[18:]
        (x_ref, xn_ref, c1, c2, c3t, hm, hs, hb, fn, hn, vm, vs, am, adv_s, on, tt, cnt, act), refs = ins, refs
        (sw,), refs = refs[:1], refs[1:]
    else:
        (x_ref, xn_ref, k1_ref, k2_ref, k3_ref), refs = refs[:5], refs[5:]
    (a1_out, s1_out, *whole_out, y_out, y0_ref), refs = refs[:8], refs[8:]
    if shared:
        (w_out, slot_out, k2_ref, k3_ref), refs = refs[:4], refs[4:]
    (carry, a1s, b1_ref, b2_ref, b3_ref, *whole, whole_sem, slopes_one, shifted, step_sem), refs = refs[:13], refs[13:]
    a2_ref, s2_ref, f_ref, s3_ref = whole
    i = pl.program_id(0)
    rows = x_ref.shape[2]
    s1_ref, y_ref = slopes_one.at[lax.rem(i, 2)], shifted.at[lax.rem(i, 2)]

    def step_copies(step):
        slot, two = lax.rem(step, 2), pl.ds(2 * step, 2)
        return [
            pltpu.make_async_copy(a1s.at[two], a1_out.at[two], step_sem.at[slot, 0]),
            pltpu.make_async_copy(slopes_one.at[slot], s1_out.at[two], step_sem.at[slot, 1]),
            pltpu.make_async_copy(shifted.at[slot], y_out.at[pl.ds(4 * step, 4)], step_sem.at[slot, 2]),
        ]

    @pl.when(i >= 2)
    def _():
        finish(step_copies(i - 2))

    if shared:
        k1_ref, shard, kern_own, kern_buf, staged, slot_src, slot_buf, kern_s, kern_r, slot_s, slot_r, own_sem, sems, core_sems = refs
        flow_stage = {
            (f, s): (shard, w_out, flow, s, sems.at[0, f, s], sems.at[1, f, s])
            for f, flow in enumerate(GATHER_FLOWS)
            for s in range(3)
        }

        def kern_copies():
            return share("dp", 8, lambda _: kern_own, kern_buf, kern_s, kern_r)

        def slot_copies():
            ids = [lax.rem(lax.axis_index("dp") + j, 8) for j in range(1, 8)]
            return share("dp", 8, lambda j: slot_src.at[ids[j]], slot_buf, slot_s, slot_r)

        def own_copies():
            me = coordinates()
            return [
                pltpu.make_async_copy(shard.at[h], w_out.at[h, me["x"], me["c"], me["z"], me["y"]], own_sem.at[h])
                for h in range(2)
            ]

        def to_core(f, last):
            return core_copies(w_out, GATHER_FLOWS[f], last, core_sems.at[0, f, last], core_sems.at[1, f, last])

        def begin():
            greet()
            kern_own[...] = pack_shards(c1[...], c2[...], c3t[...]).astype(BF16)
            kern_buf[lax.axis_index("dp")] = kern_own[...]
            noisy_weights(shard, hm, hs, hb, fn, hn, vm, vs, am, adv_s, on)
            packed = slot_rows(staged, tt, cnt, act, sw).reshape(8, 2, 32, 128)
            lane = lax.broadcasted_iota(jnp.int32, (8, 32, 128), 2)
            slot_src[...] = jnp.where(lane < 64, packed[:, 0], pltpu.roll(packed[:, 1].reshape(256, 128), 64, 1).reshape(8, 32, 128))
            slot_buf[lax.axis_index("dp")] = slot_src[lax.axis_index("dp")]
            greeted()
            start(kern_copies())
            for f, s in GATHER_FIRST:
                enter(f, s)
            start(own_copies())
            prepare()
            finish(own_copies())
            finish(kern_copies())
            for d in range(8):
                unpack_shards(d, kern_buf[d].astype(F32), k1_ref, k2_ref, k3_ref)

        def enter(f, s):
            if s > 0:
                finish(gather_copies(*flow_stage[f, s - 1]))
            start(gather_copies(*flow_stage[f, s]))
            if s == 2:
                start(to_core(f, 0))

        def point(step, k):
            for (at, where), entries in GATHER_PLAN.items():
                if where == k:

                    @pl.when(step == at)
                    def _():
                        for f, s in entries:
                            enter(f, s)

            if k == 0:

                @pl.when(step == 4)
                def _():
                    start(slot_copies())

        def end():
            for f, s in GATHER_LAST:
                enter(f, s)
            for f in GATHER_DONE:
                finish(gather_copies(*flow_stage[f, 2]))
                start(to_core(f, 1))
            finish(slot_copies())
            slot_out[:, 0:32] = slot_buf[...]
            slot_out[:, 32:64] = pltpu.roll(slot_buf[...].reshape(256, 128), 64, 1).reshape(8, 32, 128)
            for f in GATHER_DONE:
                for last in range(2):
                    finish(to_core(f, last))

    def prepare():
        b2_ref[...] = jnp.zeros_like(b2_ref)
        b3_ref[...] = jnp.zeros_like(b3_ref)
        for r in range(4):
            for j, blk in enumerate(shifted_blocks(x_ref[0, r])):
                carry[j, :, 128 * r : 128 * r + 128] = blk
        y0_ref[...] = carry[...]

    @pl.when(i == 0)
    def _():
        if shared:
            begin()
        else:
            prepare()
        fill_band_one(k1_ref, b1_ref)
        fill_band_two(k2_ref, b2_ref)
        fill_band_three(k3_ref, b3_ref)

    for pp in range(4):
        for r in range(4):
            src = x_ref[pp + 1, r] if pp < 3 else xn_ref[0, r]
            for j, blk in enumerate(shifted_blocks(src)):
                y_ref[pp, j, :, 128 * r : 128 * r + 128] = blk
        for j in range(3):
            lhs = jnp.concatenate([carry[j] if pp == 0 else y_ref[pp - 1, j], y_ref[pp, j]], axis=1)
            act, slope = silu_and_slope(dot(lhs, b1_ref[...]))
            act = act.astype(BF16)
            a1s[2 * i + pp // 2, pp % 2, :, 256 * j : 256 * j + 256] = act
            s1_ref[pp // 2, pp % 2, :, 256 * j : 256 * j + 256] = slope.astype(BF16)
        if shared:
            point(i, pp)
    carry[...] = y_ref[3]
    start(step_copies(i))

    def second(p):
        for lo, hi, n0, n1 in ((0, 384, 0, 256), (256, 640, 256, 512), (512, 768, 512, 640)):
            lhs = jnp.concatenate([a1s[p + u // 2, u % 2, :, lo:hi] for u in range(4)], axis=1)
            rhs = jnp.concatenate([b2_ref[u, lo:hi, n0:n1] for u in range(4)], axis=0)
            act, slope = silu_and_slope(dot(lhs, rhs))
            act = act.astype(BF16)
            a2_ref[p, :, n0:n1] = act
            s2_ref[p, :, n0:n1] = slope.astype(BF16)

    def third(p, odd):
        acts, slopes = [], []
        for lo, hi, n0, n1 in ((0, 384, 0, 256), (256, 640, 256, 512)):
            lhs = jnp.concatenate([a2_ref[p + u, :, lo:hi] for u in range(3)], axis=1)
            rhs = jnp.concatenate([b3_ref[u, lo:hi, n0:n1] for u in range(3)], axis=0)
            act, slope = silu_and_slope(dot(lhs, rhs))
            acts.append(act)
            slopes.append(slope)
        lane = lax.broadcasted_iota(jnp.int32, (rows, 512), 1)
        base = (p // 2) * 896
        for out, parts in ((f_ref, acts), (s3_ref, slopes)):
            whole = jnp.where(lane < 448, jnp.concatenate(parts, axis=1), 0.0)
            if not odd:
                out[:, pl.ds(pl.multiple_of(base, 128), 512)] = whole.astype(BF16)
            else:
                whole = pltpu.roll(whole, 64, 1)
                at = pl.ds(pl.multiple_of(base + 384, 128), 128)
                out[:, at] = (out[:, at].astype(F32) + whole[:, :128]).astype(BF16)
                out[:, pl.ds(pl.multiple_of(base + 512, 128), 384)] = whole[:, 128:].astype(BF16)

    @pl.when(i >= 1)
    def _():
        second(2 * i - 1)

    if shared:
        point(i, 4)
    second(2 * i)
    if shared:
        point(i, 5)

    @pl.when(i >= 2)
    def _():
        third(2 * i - 3, True)

    if shared:
        point(i, 6)

    @pl.when(i >= 1)
    def _():
        third(2 * i - 2, False)

    @pl.when(i == 4)
    def _():
        lane = lax.broadcasted_iota(jnp.int32, (rows, 128), 1)
        last = f_ref[:, 3072:3200].astype(F32)
        f_ref[:, 3072:3200] = jnp.where(lane == 64, 1.0, last).astype(BF16)
        leaving = [pltpu.make_async_copy(whole[k], whole_out[k], whole_sem.at[k]) for k in range(4)]
        start(leaving)
        if shared:
            end()
        finish(leaving)
        for step in (i - 1, i):
            finish(step_copies(step))


def full(shape):
    return pl.BlockSpec(shape, lambda *_: (0,) * len(shape))


def once(shape):
    return pl.BlockSpec(shape, lambda *_: (0,) * len(shape), pipeline_mode=pl.Buffered(1))


BANDS = [(1024, 256), (4, 768, 640), (3, 640, 512)]


def torso_forward(x, kernels, shared=None):
    rows = x.shape[2]
    shapes = [(10, 2, rows, 768)] * 2 + [(9, rows, 640)] * 2 + [(rows, 3200)] * 2 + [(20, 3, rows, 512), (3, rows, 512)]
    args = [x, x, *kernels]
    out_specs = (
        [pl.BlockSpec(memory_space=pl.ANY)] * 7
        + [once((3, rows, 512))]
    )
    out_shape = [jax.ShapeDtypeStruct(s, BF16) for s in shapes]
    scratch = [
        pltpu.VMEM((3, rows, 512), BF16),
        pltpu.VMEM((10, 2, rows, 768), BF16),
        *[pltpu.VMEM(s, BF16) for s in BANDS],
        *[pltpu.VMEM(s, BF16) for s in shapes[2:6]],
        pltpu.SemaphoreType.DMA((4,)),
        pltpu.VMEM((2, 2, 2, rows, 768), BF16),
        pltpu.VMEM((2, 4, 3, rows, 512), BF16),
        pltpu.SemaphoreType.DMA((2, 3)),
    ]
    params = {}
    if shared is not None:
        args += shared
        out_specs += [pl.BlockSpec(memory_space=pl.ANY), once((8, 64, 128)), once((512, 128)), once((576, 128))]
        out_shape += [
            jax.ShapeDtypeStruct((2, 2, 2, 4, 2, 16, HALF), BF16),
            jax.ShapeDtypeStruct((8, 64, 128), F32),
            jax.ShapeDtypeStruct((512, 128), F32),
            jax.ShapeDtypeStruct((576, 128), F32),
        ]
        scratch += [
            pltpu.VMEM((256, 128), F32),
            pltpu.VMEM((2, 16, HALF), BF16),
            pltpu.VMEM((80, 128), BF16),
            pltpu.VMEM((8, 80, 128), BF16),
            pltpu.VMEM((128, 512), F32),
            pltpu.VMEM((8, 32, 128), F32),
            pltpu.VMEM((8, 32, 128), F32),
            *[pltpu.SemaphoreType.DMA((7,))] * 4,
            pltpu.SemaphoreType.DMA((2,)),
            pltpu.SemaphoreType.DMA((2, len(GATHER_FLOWS), 3, 3)),
            pltpu.SemaphoreType.DMA((2, len(GATHER_FLOWS), 2, 3)),
        ]
        params = dict(collective_id=0, has_side_effects=True)
    return pl.pallas_call(
        functools.partial(forward_kernel, shared is not None),
        grid=(5,),
        in_specs=[
            pl.BlockSpec((4, 4, rows, 336), lambda i: (i, 0, 0, 0)),
            pl.BlockSpec((1, 4, rows, 336), lambda i: (4 * i + 4, 0, 0, 0)),
            *[once(v.shape) for v in args[2:]],
        ],
        out_specs=out_specs,
        out_shape=out_shape,
        scratch_shapes=scratch,
        compiler_params=pltpu.CompilerParams(vmem_limit_bytes=VMEM_LIMIT, **params),
        name="torso_forward",
    )(*args)


KERNEL_ROWS = [(72, 8, 16), (0, 72, 80)]


def pack_first(d, o1):
    lane = lax.broadcasted_iota(jnp.int32, (8, 128), 1) // 32
    one = jnp.zeros((8, 128), F32)
    for k in range(4):
        one = jnp.where(lane == k, o1[32 * d + 8 * k : 32 * d + 8 * k + 8, :], one)
    return jnp.concatenate([one, jnp.zeros((8, 128), F32)], axis=0)


def pack_others(d, o2, o3):
    lane = lax.broadcasted_iota(jnp.int32, (32, 128), 1)
    two = jnp.where(lane < 64, o2[64 * d : 64 * d + 32, :], o2[64 * d + 32 : 64 * d + 64, :])
    three = jnp.where(lane < 64, o3[72 * d : 72 * d + 32, :], o3[72 * d + 32 : 72 * d + 64, :])
    return jnp.concatenate([two, three, o3[72 * d + 64 : 72 * d + 72, :], jnp.zeros((8, 128), F32)], axis=0)


BACK_LANES = ((0, 256), (128, 512), (384, 640))


def backward_kernel(summed, *refs):
    (*streams, y0_in, a2_in, s2_in, s3_in, fg_in, k2_ref, k3_ref), refs = refs[:10], refs[10:]
    whole_in = (y0_in, a2_in, s2_in, s3_in, fg_in)
    if summed:
        (dw_ref, stat_ref, dsum_ref, stat_out, kern_out), refs = refs[:5], refs[5:]
    (o1_ref, o2_ref, o3_ref), refs = refs[:3], refs[3:]
    (carry, *whole, whole_sem), refs = refs[:6], refs[6:]
    slots, step_sem, refs = refs[:3], refs[3], refs[4:]
    (back, grad, g3, g2, b2_ref, b3_ref, d1_ref, d2a_ref, d2b_ref, d2c_ref, d3_ref), refs = refs[:11], refs[11:]
    a2_ref, s2_ref, s3_ref, fg_ref = whole
    coming = [pltpu.make_async_copy(whole_in[k], (carry, *whole)[k], whole_sem.at[k]) for k in range(5)]
    if summed:
        (acc, stat_dp, stat_mp, load_sem, sems, send_s, recv_s), bufs = refs[:7], refs[7:]
        kern_bufs, bufs = bufs[:6], bufs[6:]
        me = coordinates()
        stages = {}
        at = 0
        for f, flow in enumerate(SUM_FLOWS):
            for s in range(3):
                stages[f, s] = (dw_ref if s == 0 else acc, flow, s, bufs[at], sems.at[0, at], sems.at[1, at])
                at += 1

        loaded = {
            f: pltpu.make_async_copy(
                dw_ref.at[half, :, :, :, :, lo:hi], acc.at[half, :, :, :, :, lo:hi], load_sem.at[f]
            )
            for f, (half, lo, hi, _) in enumerate(SUM_FLOWS)
        }

        def stat_copies(axis, count, k):
            src = stat_ref if k == 0 else stat_mp.at[lax.axis_index("mp")]
            return share(axis, count, lambda _: src, (stat_dp, stat_mp)[k], send_s.at[k], recv_s.at[k])

        def kern_copies(group, k):
            kern_send, kern_dp, kern_mp = kern_bufs[3 * group : 3 * group + 3]
            sem = 2 + 2 * group + k
            if k == 1:
                return share("mp", 4, lambda _: kern_mp.at[lax.axis_index("mp")], kern_mp, send_s.at[sem], recv_s.at[sem])
            ids = [lax.rem(lax.axis_index("dp") + j, 8) for j in range(1, 8)]
            return share("dp", 8, lambda j: kern_send.at[ids[j]], kern_dp, send_s.at[sem], recv_s.at[sem])

        def first():
            start(list(loaded.values()))
            greeted()
            for f, s in SUM_FIRST:
                enter(f, s)
            start(stat_copies("dp", 8, 0))
            stat_dp[lax.axis_index("dp")] = stat_ref[...]

        def stats_over():
            finish(stat_copies("dp", 8, 0))
            stat_mp[lax.axis_index("mp")] = in_order(stat_dp, 8)
            start(stat_copies("mp", 4, 1))

        def enter(f, s):
            if s > 0:
                leave(f, s - 1)
            start(sum_copies(*stages[f, s]))

        def leave(f, s):
            if s == 0:
                finish([loaded[f]])
            finish(sum_copies(*stages[f, s]))
            add_arrived(acc, *stages[f, s][1:4], out=dsum_ref if s == 2 else None)

        def point(step, k):
            for (at, where), entries in SUM_PLAN.items():
                if where == k:

                    @pl.when(step == at)
                    def _():
                        for f, s in entries:
                            enter(f, s)

            extra = [(0, 5, stats_over), (1, 6, stats_done), (4, 3, lambda: kernel_out(1))]
            for at, where, what in extra:
                if where == k:

                    @pl.when(step == at)
                    def _():
                        what()

        def stats_done():
            finish(stat_copies("mp", 4, 1))
            stat_out[...] = in_order(stat_mp, 4)

        def kernel_out(group):
            kern_send, kern_dp, _ = kern_bufs[3 * group : 3 * group + 3]
            if group == 0:
                take_band_one(d1_ref, o1_ref)
            else:
                take_band_two(((d2a_ref, 0, 0, 4), (d2b_ref, 8, 4, 4), (d2c_ref, 16, 8, 1)), o2_ref)
                take_band_three(d3_ref, o3_ref)
            for d in range(8):
                rows_out = pack_first(d, o1_ref) if group == 0 else pack_others(d, o2_ref, o3_ref)
                kern_send[d] = rows_out.astype(BF16)
            kern_dp[lax.axis_index("dp")] = kern_send[lax.axis_index("dp")]
            start(kern_copies(group, 0))

        def kernel_over(group):
            _, kern_dp, kern_mp = kern_bufs[3 * group : 3 * group + 3]
            finish(kern_copies(group, 0))
            kern_mp[lax.axis_index("mp")] = in_order(kern_dp, 8)
            start(kern_copies(group, 1))

        def kernel_done(group):
            at, count, _ = KERNEL_ROWS[group]
            finish(kern_copies(group, 1))
            total = in_order(kern_bufs[3 * group + 2], 4) / stat_out[9:10, :]
            kern_out[at : at + count, :] = total[:count]

    i = pl.program_id(0)
    rows = g3.shape[1]
    y_ref, a1_ref, s1_ref = (slot.at[lax.rem(i, 2)] for slot in slots)

    def step_copies(step):
        return [
            pltpu.make_async_copy(
                streams[k].at[pl.ds(count * step, count)], slots[k].at[lax.rem(step, 2)], step_sem.at[lax.rem(step, 2), k]
            )
            for k, count in enumerate((4, 2, 2))
        ]


    @pl.when(i == 0)
    def _():
        if summed:
            greet()
        start(coming[::-1])
        start(step_copies(i))
        b2_ref[...] = jnp.zeros_like(b2_ref)
        b3_ref[...] = jnp.zeros_like(b3_ref)
        fill_band_two(k2_ref, b2_ref)
        fill_band_three(k3_ref, b3_ref)
        for r in range(2):
            for j, (n0, n1) in enumerate(BACK_LANES):
                for t in range(2):
                    turned = jnp.transpose(b2_ref[2 * t + r, 256 * j : 256 * j + 256, n0:n1].astype(F32))
                    back[j, r, t * (n1 - n0) : (t + 1) * (n1 - n0), :] = turned.astype(BF16)
        grad[3] = jnp.zeros(grad.shape[1:], BF16)
        finish(coming[3:])
        for at in (0, 1, 9, 10):
            g3[at] = jnp.zeros((rows, 512), BF16)
        for at in (0, 10):
            g2[at] = jnp.zeros((rows, 640), BF16)
        lane = lax.broadcasted_iota(jnp.int32, (rows, 512), 1)
        for p in range(7):
            base = (p // 2) * 896 + (384 if p % 2 else 0)
            both = fg_ref[:, base : base + 512].astype(F32) * s3_ref[:, base : base + 512].astype(F32)
            if p % 2:
                both = pltpu.roll(both, 448, 1)
            g3[p + 2] = jnp.where(lane < 448, both, 0.0).astype(BF16)
        if summed:
            first()
            point(i, "a0")
        finish([coming[1]])
        for u in range(3):
            total = 0.0
            for m in range(2):
                lhs = a2_ref[u : u + 7, :, 256 * m : 256 * m + 384].reshape(7 * rows, 384)
                rhs = g3[2:9, :, 256 * m : 256 * m + 256].reshape(7 * rows, 256)
                total = total + dot_tn(lhs, rhs)
            d3_ref[u] = total
            if summed:
                point(i, "a%d" % (1 + u))
        d1_ref[...] = jnp.zeros_like(d1_ref)
        d2a_ref[...] = jnp.zeros_like(d2a_ref)
        d2b_ref[...] = jnp.zeros_like(d2b_ref)
        d2c_ref[...] = jnp.zeros_like(d2c_ref)
        for at, (lo, hi, n0, n1) in enumerate(((0, 256, 0, 256), (256, 512, 128, 512), (512, 640, 384, 512))):
            rhs = jnp.concatenate([b3_ref[u, lo:hi, n0:n1] for u in range(3)], axis=1)
            if at == 0:
                finish([coming[0], coming[2]])
            for p in (0, 3, 6):
                lhs = jnp.concatenate([g3[p + 2 - u : p + 5 - u, :, n0:n1].reshape(3 * rows, n1 - n0) for u in range(3)], axis=1)
                product = dot_nt(lhs, rhs) * s2_ref[p : p + 3, :, lo:hi].reshape(3 * rows, hi - lo).astype(F32)
                g2[p + 1 : p + 4, :, lo:hi] = product.astype(BF16).reshape(3, rows, hi - lo)
            if summed:
                point(i, "a%d" % (4 + at))

    finish(step_copies(i))

    @pl.when(i < 4)
    def _():
        start(step_copies(i + 1))

    for r in range(2):
        for ref, lo, hi, n0, n1 in ((d2a_ref, 0, 384, 0, 256), (d2b_ref, 256, 640, 256, 512), (d2c_ref, 512, 768, 512, 640)):
            lhs = a1_ref[:, r, :, lo:hi].reshape(2 * rows, hi - lo)
            rhs = [g2[pl.ds(2 * i + 1 - t, 2), :, n0:n1].reshape(2 * rows, n1 - n0) for t in range(2)]
            both = dot_tn(lhs, jnp.concatenate(rhs, axis=1))
            for t in range(2):
                ref[2 * t + r] += both[:, t * (n1 - n0) : (t + 1) * (n1 - n0)]
        if summed:
            point(i, 2 * r)
            point(i, 2 * r + 1)

    for j, (n0, n1) in enumerate(BACK_LANES):
        lanes = slice(256 * j, 256 * j + 256)
        before = grad[3, :, lanes]
        for r in range(2):
            lhs = [g2[pl.ds(2 * i + 1 - t, 2), :, n0:n1].reshape(2 * rows, n1 - n0) for t in range(2)]
            product = dot(jnp.concatenate(lhs, axis=1), back[j, r, : 2 * (n1 - n0), :])
            for k in range(2):
                slope = s1_ref[k, r, :, lanes].astype(F32)
                grad[2 * k + r, :, lanes] = (product[k * rows : (k + 1) * rows] * slope).astype(BF16)
        now = [grad[k, :, lanes] for k in range(4)]
        rhs = jnp.concatenate([jnp.concatenate(now, axis=0), jnp.concatenate([before, *now[:3]], axis=0)], axis=1)
        lhs = jnp.concatenate([carry[j], *[y_ref[k, j] for k in range(3)]], axis=0)
        both = dot_tn(lhs, rhs)
        d1_ref[0:512, :] += both[:, 0:256]
        d1_ref[512:1024, :] += both[:, 256:512]
        if summed:
            point(i, 4 + j)
    carry[...] = y_ref[3]

    @pl.when(i == 4)
    def _():
        for j in range(3):
            d1_ref[512:1024, :] += dot_tn(y_ref[3, j], grad[3, :, 256 * j : 256 * j + 256])

    @pl.when(i == 4)
    def _():
        if summed:
            kernel_out(0)
            for f, s in SUM_LAST:
                enter(f, s)
            kernel_over(1)
            kernel_over(0)
            for f in SUM_DONE:
                leave(f, 2)
            kernel_done(1)
            kernel_done(0)
        else:
            take_band_one(d1_ref, o1_ref)
            take_band_two(((d2a_ref, 0, 0, 4), (d2b_ref, 8, 4, 4), (d2c_ref, 16, 8, 1)), o2_ref)
            take_band_three(d3_ref, o3_ref)


def torso_backward(y, y0, a1, s1, a2, s2, s3, fg, kern2, kern3, summed=None):
    rows = y.shape[2]
    sums = [(1024, 256), (4, 384, 256), (4, 384, 256), (4, 256, 128), (3, 384, 256)]
    own = [(256, 128), (512, 128), (576, 128)]
    args = [y, a1, s1, y0, a2, s2, s3, fg, kern2, kern3]
    in_specs = [
        *[pl.BlockSpec(memory_space=pl.ANY)] * 8,
        *[once(v.shape) for v in args[8:]],
    ]
    scratch = [
        *[pltpu.VMEM(v.shape, BF16) for v in args[3:8]],
        pltpu.SemaphoreType.DMA((5,)),
        pltpu.VMEM((2, 4, 3, rows, 512), BF16),
        pltpu.VMEM((2, 2, 2, rows, 768), BF16),
        pltpu.VMEM((2, 2, 2, rows, 768), BF16),
        pltpu.SemaphoreType.DMA((2, 3)),
        pltpu.VMEM((3, 2, 768, 256), BF16),
        pltpu.VMEM((4, rows, 768), BF16),
        pltpu.VMEM((11, rows, 512), BF16),
        pltpu.VMEM((11, rows, 640), BF16),
        *[pltpu.VMEM(s, BF16) for s in BANDS[1:]],
        *[pltpu.VMEM(s, F32) for s in sums],
    ]
    outs = own
    params = {}
    if summed is not None:
        args += summed
        block = (2, *AXES.values(), 16, HALF)
        in_specs += [pl.BlockSpec(memory_space=pl.ANY), once((16, 128))]
        outs = [(2, 16, HALF), (16, 128), (80, 128)]
        buffers = flow_buffers(SUM_FLOWS)
        scratch = [pltpu.VMEM(s, F32) for s in own] + scratch
        scratch += [
            pltpu.VMEM(block, BF16),
            pltpu.VMEM((8, 16, 128), F32),
            pltpu.VMEM((4, 16, 128), F32),
            pltpu.SemaphoreType.DMA((len(SUM_FLOWS),)),
            pltpu.SemaphoreType.DMA((2, len(buffers), 3)),
            pltpu.SemaphoreType.DMA((6, 7)),
            pltpu.SemaphoreType.DMA((6, 7)),
            *[
                pltpu.VMEM((count, padded, 128), kind)
                for _, _, padded in KERNEL_ROWS
                for count, kind in ((8, BF16), (8, BF16), (4, F32))
            ],
            *[pltpu.VMEM(s, BF16) for s in buffers],
        ]
        params = dict(collective_id=1, has_side_effects=True)
    return pl.pallas_call(
        functools.partial(backward_kernel, summed is not None),
        grid=(5,),
        in_specs=in_specs,
        out_specs=[once(s) for s in outs],
        out_shape=[jax.ShapeDtypeStruct(s, F32) for s in outs],
        scratch_shapes=scratch,
        compiler_params=pltpu.CompilerParams(vmem_limit_bytes=VMEM_LIMIT, **params),
        name="torso_backward",
    )(*args)


def high_low(v):
    high = v.astype(BF16)
    return high, (v - high.astype(F32)).astype(BF16)


HEAD_COLUMNS = [(0, 1024), (1024, 2048), (2048, HALF)]


def heads_kernel(atoms, acts, paired, f_ref, w_ref, bias_ref, slot_ref, row_ref, dw_out, fg_ref, prio_ref, stat_ref, *refs):
    if paired:
        dw_ref, arrived, w_hbm, w_ref, summed, dw_hbm = *refs[:2], w_ref, refs[2], refs[3], dw_out
        send, recv, load, save = refs[4:]
        loads = {
            (h, k): pltpu.make_async_copy(w_hbm.at[h, :, lo:hi], w_ref.at[h, :, lo:hi], load.at[h, k])
            for h in range(2)
            for k, (lo, hi) in enumerate(HEAD_COLUMNS)
        }
        start(list(loads.values()))
        me = coordinates()
        other = device_at({**me, "c": 1 - me["c"]})
        barrier = pltpu.get_barrier_semaphore()
        pl.semaphore_signal(barrier, inc=1, **other)

        def to_core(h, k):
            lo, hi = HEAD_COLUMNS[k]
            src = dw_ref.at[h, :, 1 - me["c"], :, :, :, lo:hi]
            return pltpu.make_async_remote_copy(src, arrived.at[h, :, :, :, :, lo:hi], send.at[h, k], recv.at[h, k], **other)

        def saving(h, k):
            lo, hi = HEAD_COLUMNS[k]
            return pltpu.make_async_copy(summed.at[h, :, :, :, :, lo:hi], dw_hbm.at[h, :, :, :, :, lo:hi], save.at[h, k])

        def add_core(h, k):
            lo, hi = HEAD_COLUMNS[k]
            to_core(h, k).wait()

            def one(j, _):
                x, z, y = j // 8, (j // 2) % 4, j % 2
                own = dw_ref[h, x, me["c"], z, y, :, lo:hi]
                summed[h, x, z, y, :, lo:hi] = own + arrived[h, x, z, y, :, lo:hi]
                return 0

            lax.fori_loop(0, 16, one, 0)
            saving(h, k).start()


    def put(h, lo, hi, v):
        v = v.astype(BF16)
        if paired:
            dw_ref[h, :, :, :, :, :, lo:hi] = v.reshape(2, 2, 4, 2, 16, hi - lo)
        else:
            dw_out[h, :, lo:hi] = v

    rows = f_ref.shape[0]
    slots = slot_ref.shape[0]
    wide = 1024
    lane = lax.broadcasted_iota(jnp.int32, (1, wide), 1)
    selt = jnp.where(lax.broadcasted_iota(jnp.int32, (rows, slots), 0) == row_ref[...], 1.0, 0.0).astype(BF16)
    action = slot_ref[:, atoms + 2 : atoms + 3]
    which = jnp.where(lane < atoms, -1, jnp.where(lane < atoms * (acts + 1), (lane - atoms) // atoms, -2)).astype(F32)
    coeff = jnp.where(which == -1.0, 1.0, 0.0) + jnp.where(which == action, 1.0, 0.0) - jnp.where(which >= 0.0, 1.0 / acts, 0.0)
    atom = jnp.where(which >= -1.0, lane - atoms * (which.astype(jnp.int32) + 1), -1)
    fold = jnp.where(lax.broadcasted_iota(jnp.int32, (128, wide), 0) == atom, 1.0, 0.0).astype(BF16)
    pre = []
    for h in range(2):
        total = 0.0
        for k, (lo, hi) in enumerate(HEAD_COLUMNS):
            if paired:
                loads[h, k].wait()
            hi = min(hi, 3200)
            total = total + dot_nt(f_ref[:, lo:hi], w_ref[h, :, lo:hi])
        pre.append(total)
    hidden, slope = [], []
    for k in range(2):
        a, s = silu_and_slope(pre[k])
        hidden.append(a.astype(BF16))
        slope.append(s)
    out_w = jnp.concatenate([w_ref[0, :, 3200:], w_ref[1, :, 3200:]], axis=1)
    zero = jnp.zeros((), BF16)
    w_val = jnp.where(lane[:, :128] < atoms, out_w[:, :128].astype(F32), 0.0).astype(BF16)
    w_adv = jnp.where(lane >= atoms, out_w.astype(F32), 0.0).astype(BF16)
    outs = bias_ref.shape[1]
    bias = jnp.concatenate([bias_ref[...], jnp.zeros((1, wide - outs), F32)], axis=1)
    logits = dot(hidden[1], w_adv) + bias
    logits = jnp.concatenate([logits[:, :128] + dot(hidden[0], w_val), logits[:, 128:]], axis=1)
    high, low = high_low(logits)
    per_slot = dot_tn(selt, high) + dot_tn(selt, low)
    high, low = high_low(per_slot * coeff)
    q = dot_nt(high, fold) + dot_nt(low, fold)
    lane_q = lax.broadcasted_iota(jnp.int32, (slots, 128), 1)
    used = lane_q < atoms
    top = jnp.max(jnp.where(used, q, -jnp.inf), axis=1, keepdims=True)
    shifted = jnp.where(used, jnp.exp(jnp.where(used, q - top, 0.0)), 0.0)
    total = jnp.sum(shifted, axis=1, keepdims=True)
    tgt = jnp.where(used, slot_ref[...], 0.0)
    cross = -jnp.sum(jnp.where(used, tgt * (q - top - jnp.log(total)), 0.0), axis=1, keepdims=True)
    coef = slot_ref[:, atoms : atoms + 1]
    valid = slot_ref[:, atoms + 1 : atoms + 2]
    prio_ref[...] = jnp.transpose(jnp.broadcast_to(valid * cross, (slots, 128)))[0:1]
    q_grad = coef * (shifted * (jnp.sum(tgt, axis=1, keepdims=True) / total) - tgt)
    high, low = high_low(q_grad)
    lgrad = ((dot(high, fold) + dot(low, fold)) * coeff).astype(BF16)
    bias_grad = jnp.sum(lgrad.astype(F32), axis=0, keepdims=True)
    for k in range(8):
        stat_ref[k : k + 1, :] = bias_grad[:, 128 * k : 128 * k + 128]
    stat_ref[8:9, :] = jnp.broadcast_to(jnp.sum(coef * cross, axis=0, keepdims=True), (1, 128))
    stat_ref[9:10, :] = jnp.broadcast_to(jnp.sum(valid, axis=0, keepdims=True), (1, 128))
    stat_ref[10:16, :] = jnp.zeros((6, 128), F32)
    grad = dot(selt, lgrad).astype(BF16)
    d_adv = dot_tn(hidden[1], grad)
    d_val = dot_tn(hidden[0], grad[:, :128])
    put(0, 3200, 3328, jnp.where(lane[:, :128] < atoms, d_val, d_adv[:, :128]))
    put(0, 3328, HALF, d_adv[:, 128:512])
    put(1, 3200, HALF, d_adv[:, 512:])
    pre_grad = [
        (dot_nt(grad[:, :128], w_val) * slope[0]).astype(BF16),
        (dot_nt(grad, w_adv) * slope[1]).astype(BF16),
    ]
    for k in range(2):
        for part, (lo, hi) in enumerate(((0, 1024), (1024, 2048), (2048, 3200))):
            put(k, lo, hi, dot_tn(pre_grad[k], f_ref[:, lo:hi]))
            if paired:
                if (k, part) == (0, 0):
                    pl.semaphore_wait(barrier, 1)
                to_core(k, part).start()
    for part, (lo, hi) in enumerate(((0, 1024), (1024, 2048), (2048, 3200))):
        back = dot(pre_grad[0], w_ref[0, :, lo:hi]) + dot(pre_grad[1], w_ref[1, :, lo:hi])
        fg_ref[:, lo:hi] = back.astype(BF16)
        if paired:
            add_core(0, part)
    if paired:
        for part in range(3):
            add_core(1, part)
        for h in range(2):
            for part in range(3):
                saving(h, part).wait()


def heads(atoms, acts, feats, weights, bias, per_slot, rows_of_slot, paired=False):
    slots = per_slot.shape[0]
    block = (2, 2, 4, 2, 16, HALF)
    scratch, params = [], {}
    if paired:
        scratch = [
            pltpu.VMEM((2, 2, 2, 4, 2, 16, HALF), BF16),
            pltpu.VMEM(block, BF16),
            pltpu.VMEM(weights.shape, BF16),
            pltpu.VMEM(block, BF16),
            *[pltpu.SemaphoreType.DMA((2, 3))] * 4,
        ]
        params = dict(collective_id=3, has_side_effects=True)
    vmem = pl.BlockSpec(memory_space=pltpu.VMEM)
    large = pl.BlockSpec(memory_space=pl.ANY) if paired else vmem
    return pl.pallas_call(
        functools.partial(heads_kernel, atoms, acts, paired),
        in_specs=[vmem, large, vmem, vmem, vmem],
        out_specs=[large, vmem, vmem, vmem],
        out_shape=[
            jax.ShapeDtypeStruct(block if paired else weights.shape, BF16),
            jax.ShapeDtypeStruct(feats.shape, BF16),
            jax.ShapeDtypeStruct((1, slots), F32),
            jax.ShapeDtypeStruct((16, 128), F32),
        ],
        scratch_shapes=scratch,
        compiler_params=pltpu.CompilerParams(vmem_limit_bytes=VMEM_LIMIT, **params),
        name="heads",
    )(feats, weights, bias, per_slot, rows_of_slot[None, :])


def finish_kernel(
    dsum, stat, kern, fn, hn, on, loss, g1, g2, g3t, mean_g, spread_g, bias_g, val_g, val_s, adv_g, adv_s, out_g
):
    feat, atoms, outs = fn.shape[1], val_g.shape[1], on.shape[1]
    inverse = 1.0 / stat[9:10, 0:1]
    loss[...] = stat[8:9, 0:1] * inverse
    v = kern[...]
    turned = pltpu.roll(v, 64, 1)
    g2[0:32, :] = v[0:32, 0:64]
    g2[32:64, :] = turned[0:32, 0:64]
    third = jnp.concatenate([v[32:64], turned[32:64], v[64:72], jnp.zeros((56, 128), F32)], axis=0)
    g3t[...] = jnp.transpose(third)[0:64, 0:72]
    for k in range(4):
        g1[8 * k : 8 * k + 8, :] = v[72:80, 32 * k : 32 * k + 32]
    for h in range(2):
        mean = dsum[h, :, 0:feat] * inverse
        mean_g[h] = mean
        spread_g[h] = mean * fn[h : h + 1, :] * as_column(hn[0, h : h + 1, :])
        bias_g[h : h + 1, :] = as_row(dsum[h, :, feat : feat + 1] * inverse)
    out = jnp.concatenate([dsum[0, :, 3200:], dsum[1, :, 3200:]], axis=1) * inverse
    val, adv = out[:, :atoms], out[:, atoms:outs]
    val_g[...] = val
    val_s[...] = val * as_column(hn[1, 0:1, :]) * on[:, :atoms]
    adv_g[...] = adv
    adv_s[...] = adv * as_column(hn[1, 1:2, :]) * on[:, atoms:]
    out_g[...] = jnp.concatenate([stat[k : k + 1, :] for k in range(8)], axis=1)[:, :outs] * inverse


def outputs(dsum, stat, kern, fn, hn, on, atoms):
    feat, outs = fn.shape[1], on.shape[1]
    shapes = [(1, 1), (32, 32), (64, 64), (64, 72), (2, 16, feat), (2, 16, feat), (2, 16)]
    shapes += [(16, atoms)] * 2 + [(16, outs - atoms)] * 2 + [(1, outs)]
    return pl.pallas_call(
        finish_kernel,
        out_shape=[jax.ShapeDtypeStruct(s, F32) for s in shapes],
        compiler_params=pltpu.CompilerParams(vmem_limit_bytes=VMEM_LIMIT),
        name="outputs",
    )(dsum, stat, kern, fn, hn, on)


def exchange_kernel(count, kern_ref, slot_ref, kerns_out, slots_out, send_kern, recv_kern, send_slot, recv_slot, own):
    me = lax.axis_index("dp")
    peers = [lax.rem(me + k, count) for k in range(count)]
    barrier = pltpu.get_barrier_semaphore()
    for k in range(1, count):
        pl.semaphore_signal(barrier, inc=1, device_id={"dp": peers[k]}, device_id_type=pl.DeviceIdType.MESH)
    pl.semaphore_wait(barrier, count - 1)
    mine = [
        pltpu.make_async_copy(kern_ref, kerns_out.at[me], own.at[0]),
        pltpu.make_async_copy(slot_ref.at[me], slots_out.at[me], own.at[1]),
    ]
    sent = []
    for k in range(1, count):
        to = dict(device_id={"dp": peers[k]}, device_id_type=pl.DeviceIdType.MESH)
        sent.append(pltpu.make_async_remote_copy(kern_ref, kerns_out.at[me], send_kern.at[k], recv_kern.at[k], **to))
        sent.append(pltpu.make_async_remote_copy(slot_ref.at[peers[k]], slots_out.at[me], send_slot.at[k], recv_slot.at[k], **to))
    for copy in mine + sent:
        copy.start()
    for copy in mine + sent:
        copy.wait()


def exchange(kern, slot):
    count = slot.shape[0]
    return pl.pallas_call(
        functools.partial(exchange_kernel, count),
        in_specs=[pl.BlockSpec(memory_space=pltpu.VMEM)] * 2,
        out_specs=[pl.BlockSpec(memory_space=pltpu.VMEM)] * 2,
        out_shape=[jax.ShapeDtypeStruct((count, *kern.shape), kern.dtype), jax.ShapeDtypeStruct(slot.shape, slot.dtype)],
        scratch_shapes=[pltpu.SemaphoreType.DMA((count,))] * 4 + [pltpu.SemaphoreType.DMA((2,))],
        compiler_params=pltpu.CompilerParams(collective_id=2, has_side_effects=True, vmem_limit_bytes=VMEM_LIMIT),
        name="exchange",
    )(kern, slot)


def on_device(
    frames,
    send_rows,
    recv_counts,
    actions,
    target_dist,
    sample_weight,
    conv_first,
    conv_second,
    conv_third,
    hidden_mean,
    hidden_spread,
    hidden_bias,
    feature_noise,
    hidden_noise,
    value_mean,
    value_spread,
    advantage_mean,
    advantage_spread,
    output_noise,
    output_bias,
):
    dp_count = lax.axis_size("dp")
    slots = send_rows.shape[0]
    capacity = slots // dp_count
    atoms = value_mean.shape[1]
    acts = advantage_mean.shape[1] // atoms
    rows = frames.shape[0]
    feat, own = hidden_mean.shape[1:]
    outs = atoms * (acts + 1)

    x = frames.transpose(1, 0, 2).reshape(21, 4, rows, 336)
    bias = output_bias[None, :]
    mean_t = hidden_mean.transpose(0, 2, 1)
    spread_t = hidden_spread.transpose(0, 2, 1)

    if (dp_count, lax.axis_size("mp"), own, slots) == (8, 4, 16, 512):
        noise = output_noise[None, :]
        shared = [mean_t, spread_t, hidden_bias, feature_noise, hidden_noise]
        shared += [value_mean, value_spread, advantage_mean, advantage_spread, noise]
        shared += [target_dist.T, recv_counts[None, :], actions[None, :], sample_weight[None, :]]
        kernels = [conv_first, conv_second, conv_third.T]
        a1, s1, a2, s2, feats, s3, y, y0, weights, per_slot, kern2, kern3 = torso_forward(x, kernels, shared)
        weights, per_slot = weights.reshape(2, 512, HALF), per_slot.reshape(slots, 128)
        dweights, feat_grad, prio, stat = heads(atoms, acts, feats, weights, bias, per_slot, send_rows, paired=True)
        summed = [dweights, stat]
        summed = torso_backward(y, y0, a1, s1, a2, s2, s3, feat_grad, kern2, kern3, summed=summed)
        loss, g1, g2, g3t, mean_g, spread_g, bias_g, *outer, out_g = outputs(
            *summed, feature_noise, hidden_noise, noise, atoms
        )
        return (
            loss[0, 0],
            g1,
            g2,
            g3t.T,
            mean_g.transpose(0, 2, 1),
            spread_g.transpose(0, 2, 1),
            bias_g,
            *outer,
            out_g[0],
            prio[0],
        )

    sizes = [w.size for w in (conv_first, conv_second, conv_third)]
    flat = jnp.concatenate([w.astype(BF16).reshape(-1) for w in (conv_first, conv_second, conv_third)])
    tall = -(-flat.size // 2048) * 16
    flat = jnp.pad(flat, (0, tall * 128 - flat.size)).reshape(tall, 128)
    is_valid = jnp.arange(capacity, dtype=jnp.int32)[None, :] < recv_counts[:, None]
    is_valid = is_valid.astype(F32).reshape(slots)
    per_slot = jnp.stack([is_valid * sample_weight, is_valid, actions.astype(F32)], axis=1)
    per_slot = jnp.concatenate([target_dist, per_slot, jnp.zeros((slots, 125 - atoms), F32)], axis=1)
    flat, per_slot = exchange(flat, per_slot.reshape(dp_count, capacity, 128))
    per_slot = per_slot.reshape(slots, 128)
    flat = flat.reshape(dp_count, -1)
    kern1 = jnp.tile(flat[:, : sizes[0]].reshape(-1, 32), (1, 4))
    kern2 = jnp.tile(flat[:, sizes[0] : sizes[0] + sizes[1]].reshape(-1, 64), (1, 2))
    kern3 = jnp.tile(flat[:, sizes[0] + sizes[1] : sum(sizes)].reshape(-1, 64), (1, 2))

    wide_one = mean_t + spread_t * feature_noise[:, None, :] * hidden_noise[0][:, :, None]
    wide_one = jnp.concatenate([wide_one, hidden_bias[:, :, None], jnp.zeros((2, own, 63), F32)], axis=2)
    wide_val = value_mean + value_spread * hidden_noise[1, 0][:, None] * output_noise[None, :atoms]
    wide_adv = advantage_mean + advantage_spread * hidden_noise[1, 1][:, None] * output_noise[None, atoms:]
    wide_out = jnp.concatenate([wide_val, wide_adv, jnp.zeros((own, 1024 - outs), F32)], axis=1)
    wide_out = wide_out.reshape(own, 2, 512).transpose(1, 0, 2)
    shard = jnp.concatenate([wide_one, wide_out], axis=2).astype(BF16)
    weights = lax.all_gather(shard, ("mp", "dp"), axis=1, tiled=True)

    a1, s1, a2, s2, feats, s3, y, y0 = torso_forward(x, [kern1, kern2, kern3])
    dweights, feat_grad, prio, stat = heads(atoms, acts, feats, weights, bias, per_slot, send_rows)
    dshard = lax.psum_scatter(dweights, ("mp", "dp"), scatter_dimension=1, tiled=True).astype(F32)
    stat = lax.psum(stat, ("dp", "mp"))
    inverse = 1.0 / stat[9, 0]
    k1, k2, k3 = torso_backward(y, y0, a1, s1, a2, s2, s3, feat_grad, kern2, kern3)
    kflat = jnp.concatenate([g.reshape(dp_count, -1) for g in (k1[:, :32], k2[:, :64], k3[:, :64])], axis=1)
    kflat = lax.psum(lax.psum_scatter(kflat, "dp", scatter_dimension=0, tiled=True)[0], "mp") * inverse
    conv_grads = (
        kflat[: sizes[0]].reshape(conv_first.shape),
        kflat[sizes[0] : sizes[0] + sizes[1]].reshape(conv_second.shape),
        kflat[sizes[0] + sizes[1] :].reshape(conv_third.shape),
    )
    dshard = dshard * inverse
    mean_grad_t = dshard[:, :, :feat]
    spread_grad_t = mean_grad_t * feature_noise[:, None, :] * hidden_noise[0][:, :, None]
    out_grad = dshard[:, :, 3200:].transpose(1, 0, 2).reshape(own, 1024)
    value_mean_grad = out_grad[:, :atoms]
    adv_mean_grad = out_grad[:, atoms:outs]
    return (
        stat[8, 0] * inverse,
        *conv_grads,
        mean_grad_t.transpose(0, 2, 1),
        spread_grad_t.transpose(0, 2, 1),
        dshard[:, :, feat],
        value_mean_grad,
        value_mean_grad * hidden_noise[1, 0][:, None] * output_noise[None, :atoms],
        adv_mean_grad,
        adv_mean_grad * hidden_noise[1, 1][:, None] * output_noise[None, atoms:],
        stat[:8].reshape(-1)[:outs] * inverse,
        prio[0],
    )


def solution(mesh):
    both, heads_dim = P(("dp", "mp")), P(("mp", "dp"), None)
    return jax.shard_map(
        on_device,
        mesh=mesh,
        in_specs=(
            P(("dp", "mp"), None, None),
            both,
            both,
            both,
            P(("dp", "mp"), None),
            both,
            P("dp", None),
            P("dp", None),
            P("dp", None),
            P(None, None, ("mp", "dp")),
            P(None, None, ("mp", "dp")),
            P(None, ("mp", "dp")),
            P(),
            P(None, None, ("mp", "dp")),
            heads_dim,
            heads_dim,
            heads_dim,
            heads_dim,
            P(),
            P(),
        ),
        out_specs=(
            P(),
            P("dp", None),
            P("dp", None),
            P("dp", None),
            P(None, None, ("mp", "dp")),
            P(None, None, ("mp", "dp")),
            P(None, ("mp", "dp")),
            heads_dim,
            heads_dim,
            heads_dim,
            heads_dim,
            P(),
            both,
        ),
        check_vma=False,
    )
```

```python
import functools

import jax
import jax.numpy as jnp
from jax import lax
from jax.experimental import pallas as pl
from jax.experimental.pallas import tpu as pltpu
from jax.sharding import PartitionSpec as P

F32 = jnp.float32
BF16 = jnp.bfloat16
VMEM_LIMIT = 60 * 1024 * 1024


def sigmoid(v):
    return 0.5 * jnp.tanh(0.5 * v) + 0.5


def silu_and_slope(v):
    s = sigmoid(v)
    a = v * s
    return a, s + a * (1.0 - s)


def dot(a, b):
    return lax.dot_general(a, b, (((1,), (0,)), ((), ())), preferred_element_type=F32)


def dot_nt(a, b):
    return lax.dot_general(a, b, (((1,), (1,)), ((), ())), preferred_element_type=F32)


def dot_tn(a, b):
    return lax.dot_general(a, b, (((0,), (0,)), ((), ())), preferred_element_type=F32)


def columns_of_one():
    return [7 * (g // 8) + g % 8 if g % 8 < 7 and 7 * (g // 8) + g % 8 < 20 else -9 for g in range(24)]


def half_lanes(left, right, rows):
    lane = lax.broadcasted_iota(jnp.int32, (rows, 128), 1)
    zero = jnp.zeros((rows, 128), F32)
    return jnp.where(lane < 64, zero if left is None else left, zero if right is None else right)


def fill_band_one(k1_ref, band):
    lane = lax.broadcasted_iota(jnp.int32, (16, 128), 1) // 32
    for u in range(8):
        taps = [k1_ref[((u // 4) * 2 + v) * 64 + (u % 4) * 16 :][:16].astype(F32) for v in range(2)]
        for g in range(8):
            for h in range(2):
                col = lane + 4 * h
                here = jnp.where((col == g) & (col < 7), taps[0], 0.0) + jnp.where((col == g - 1) & (col < 7), taps[1], 0.0)
                band[128 * u + 16 * g : 128 * u + 16 * g + 16, 128 * h : 128 * h + 128] = here.astype(BF16)


def fill_band_two(k2_ref, band):
    cols = columns_of_one()
    for u in range(4):

        def tap(v):
            at = ((u // 2) * 2 + v // 2) * 128 + ((u % 2) * 2 + v % 2) * 32
            return k2_ref[at : at + 32, :].astype(F32)

        for g, q in enumerate(cols):
            if q < 0:
                continue
            used = {(q - v) // 2: v for v in (q % 2, q % 2 + 2) if 0 <= (q - v) // 2 < 9}
            for m in sorted({c // 2 for c in used}):
                sides = [tap(used[2 * m + side]) if 2 * m + side in used else None for side in range(2)]
                band[u, 32 * g : 32 * g + 32, 128 * m : 128 * m + 128] = half_lanes(*sides, 32).astype(BF16)


def fill_band_three(k3_ref, band):
    for u in range(3):

        def tap(v):
            return k3_ref[(u * 3 + v) * 64 : (u * 3 + v) * 64 + 64, :].astype(F32)

        for q in range(9):
            used = {q - v: v for v in range(3) if 0 <= q - v < 7}
            for m in sorted({c // 2 for c in used}):
                sides = [tap(used[2 * m + side]) if 2 * m + side in used else None for side in range(2)]
                band[u, 64 * q : 64 * q + 64, 128 * m : 128 * m + 128] = half_lanes(*sides, 64).astype(BF16)


def fold_lanes(v, width):
    step = 64
    while step >= width:
        v = v + pltpu.roll(v, step, 1)
        step //= 2
    return v


def take_band_one(d1, out):
    lane = lax.broadcasted_iota(jnp.int32, (16, 128), 1) // 32
    for u in range(8):
        for v in range(2):
            total = jnp.zeros((16, 128), F32)
            for col in range(7):
                at = 128 * u + 16 * (col + v)
                h = col // 4
                total = total + jnp.where(lane + 4 * h == col, d1[at : at + 16, 128 * h : 128 * h + 128], 0.0)
            at = ((u // 4) * 2 + v) * 64 + (u % 4) * 16
            out[at : at + 16, :] = total
    out[...] = fold_lanes(out[...], 32)


def take_band_two(blocks, out):
    cols = columns_of_one()
    lane = lax.broadcasted_iota(jnp.int32, (32, 128), 1)
    for u in range(4):
        for v in range(4):
            total = jnp.zeros((32, 128), F32)
            for ref, first, c0, count in blocks:
                for c in range(count):
                    at = 32 * (cols.index(2 * (c0 + c) + v) - first)
                    piece = ref[u, at : at + 32, 128 * (c // 2) : 128 * (c // 2) + 128]
                    total = total + jnp.where((lane < 64) == (c % 2 == 0), piece, 0.0)
            at = ((u // 2) * 2 + v // 2) * 128 + ((u % 2) * 2 + v % 2) * 32
            out[at : at + 32, :] = total
    out[...] = fold_lanes(out[...], 64)


def take_band_three(d3, out):
    lane = lax.broadcasted_iota(jnp.int32, (64, 128), 1)
    for u in range(3):
        for v in range(3):
            total = jnp.zeros((64, 128), F32)
            for c in range(4):
                piece = d3[u, 64 * (c + v) : 64 * (c + v) + 64, 128 * (c // 2) : 128 * (c // 2) + 128]
                total = total + jnp.where((lane < 64) == (c % 2 == 0), piece, 0.0)
            at = (u * 3 + v) * 64
            out[at : at + 64, :] = total
    out[...] = fold_lanes(out[...], 64)


def coordinates():
    d, m = lax.axis_index("dp"), lax.axis_index("mp")
    return {"z": d // 2, "y": d % 2, "x": m // 2, "c": m % 2}


def device_at(at):
    return dict(
        device_id={"dp": at["z"] * 2 + at["y"], "mp": at["x"] * 2 + at["c"]}, device_id_type=pl.DeviceIdType.MESH
    )


AXES = {"x": 2, "z": 4, "y": 2}
HALF = 3712
CUTS = [(0, 1408, "zyx", "zxy"), (1408, 2816, "zyx", "zxy"), (2816, HALF, "xyz", "yxz")]
GATHER_FLOWS = [(half, lo, hi, orders[half]) for lo, hi, *orders in CUTS for half in range(2)]
SUM_FLOWS = [(half, lo, hi, order[::-1]) for half, lo, hi, order in GATHER_FLOWS]
GATHER_FIRST = [(4, 0), (5, 0), (0, 0)]
GATHER_PLAN = {(0, 0): [(4, 1), (5, 1), (1, 0), (0, 1)], (0, 1): [(2, 0)], (0, 3): [(1, 1)], (1, 0): [(3, 0)], (1, 3): [(2, 1), (0, 2)], (1, 5): [(4, 2)], (2, 1): [(1, 2)], (3, 0): [(3, 1)], (3, 4): [(5, 2)], (3, 5): [(2, 2)], (4, 1): [(3, 2)]}
GATHER_LAST = []
GATHER_DONE = [0, 4, 1, 2, 5, 3]
SUM_FIRST = [(0, 0), (1, 0), (4, 0)]
SUM_PLAN = {(0, 2): [(2, 0), (3, 0)], (0, 4): [(5, 0)], (1, 4): [(0, 1), (1, 1)], (2, 0): [(2, 1), (3, 1)], (2, 4): [(0, 2)], (2, 5): [(4, 1), (5, 1)], (2, 6): [(1, 2)], (3, 2): [(4, 2), (5, 2)], (3, 5): [(2, 2)], (4, 2): [(3, 2)]}
SUM_LAST = []
SUM_DONE = [0, 4, 5, 1, 2, 3]

def flow_buffers(flows):
    shapes = []
    for _, lo, hi, order in flows:
        for s, axis in enumerate(order):
            rest = [AXES[a] for a in AXES if a in order[s + 1 :]]
            shapes.append((AXES[axis] - 1, *rest, 16, hi - lo))
    return shapes


def peers_of(axis):
    me = coordinates()
    n = AXES[axis]
    return [{**me, axis: lax.rem(me[axis] + k, n)} for k in range(1, n)]


def block_of(ref, half, lo, hi, at):
    return ref.at[(half, *[at.get(a, slice(None)) for a in AXES], slice(None), slice(lo, hi))]


def sum_copies(acc, flow, stage, buf, send, recv):
    half, lo, hi, order = flow
    me = coordinates()
    held = {a: me[a] for a in order[:stage]}
    copies = []
    for k, peer in enumerate(peers_of(order[stage])):
        src = block_of(acc, half, lo, hi, {**held, order[stage]: peer[order[stage]]})
        copies.append(pltpu.make_async_remote_copy(src, buf.at[k], send.at[k], recv.at[k], **device_at(peer)))
    return copies


def add_arrived(acc, flow, stage, buf, out=None):
    half, lo, hi, order = flow
    me = coordinates()
    own = block_of(acc, half, lo, hi, {a: me[a] for a in order[: stage + 1]})
    if out is None and AXES[order[stage]] == 2:
        own[...] = own[...] + buf[0]
        return
    total = own[...].astype(F32)
    for k in range(AXES[order[stage]] - 1):
        total = total + buf[k].astype(F32)
    if out is None:
        own[...] = total.astype(BF16)
    else:
        out[half, :, lo:hi] = total


def everyone(axis, count):
    me = lax.axis_index(axis)
    return [dict(device_id={axis: lax.rem(me + k, count)}, device_id_type=pl.DeviceIdType.MESH) for k in range(1, count)]


def share(axis, count, src, buf, send, recv):
    me = lax.axis_index(axis)
    return [
        pltpu.make_async_remote_copy(src(k), buf.at[me], send.at[k], recv.at[k], **to)
        for k, to in enumerate(everyone(axis, count))
    ]


def in_order(buf, count):
    total = buf[0].astype(F32)
    for k in range(1, count):
        total = total + buf[k].astype(F32)
    return total


def gathered_block(ref, half, lo, hi, core, at):
    x, z, y = (at.get(a, slice(None)) for a in AXES)
    return ref.at[half, x, core, z, y, :, lo:hi]


def gather_copies(shard, out, flow, stage, send, recv):
    half, lo, hi, order = flow
    me = coordinates()
    at = {a: me[a] for a in order[stage:]}
    dst = gathered_block(out, half, lo, hi, me["c"], at)
    src = shard.at[half, :, lo:hi] if stage == 0 else dst
    return [
        pltpu.make_async_remote_copy(src, dst, send.at[k], recv.at[k], **device_at(peer))
        for k, peer in enumerate(peers_of(order[stage]))
    ]


def core_copies(out, flow, last, send, recv):
    half, lo, hi, order = flow
    me = coordinates()
    other = {**me, "c": 1 - me["c"]}
    copies = []
    for k, at in enumerate([peer[order[2]] for peer in peers_of(order[2])] if last else [me[order[2]]]):
        block = gathered_block(out, half, lo, hi, me["c"], {order[2]: at})
        copies.append(pltpu.make_async_remote_copy(block, block, send.at[k], recv.at[k], **device_at(other)))
    return copies


def start(copies):
    for copy in copies:
        copy.start()


def finish(copies):
    for copy in copies:
        copy.wait()


def greet():
    for to in everyone("dp", 8) + everyone("mp", 4):
        pl.semaphore_signal(pltpu.get_barrier_semaphore(), inc=1, **to)


def greeted():
    pl.semaphore_wait(pltpu.get_barrier_semaphore(), 10)


def as_column(row):
    n = row.shape[1]
    eye = lax.broadcasted_iota(jnp.int32, (n, n), 0) == lax.broadcasted_iota(jnp.int32, (n, n), 1)
    return jnp.sum(jnp.where(eye, row, 0.0), axis=1, keepdims=True)


def as_row(column):
    n = column.shape[0]
    eye = lax.broadcasted_iota(jnp.int32, (n, n), 0) == lax.broadcasted_iota(jnp.int32, (n, n), 1)
    return jnp.sum(jnp.where(eye, column, 0.0), axis=0, keepdims=True)


def pack_shards(c1, c2, c3t):
    c3 = jnp.transpose(jnp.concatenate([c3t, jnp.zeros((64, 56), F32)], axis=1))
    blank = jnp.zeros((8, 64), F32)
    return jnp.concatenate(
        [
            jnp.concatenate([c2[0:32], c2[32:64]], axis=1),
            jnp.concatenate([c3[0:32], c3[32:64]], axis=1),
            jnp.concatenate([c3[64:72], blank], axis=1),
            jnp.concatenate([c1[8 * k : 8 * k + 8] for k in range(4)], axis=1),
        ],
        axis=0,
    )


def unpack_shards(d, v, k1, k2, k3):
    lane = lax.broadcasted_iota(jnp.int32, (32, 128), 1)

    def sides(w):
        turned = pltpu.roll(w, 64, 1)
        low = lane[: w.shape[0]] < 64
        return jnp.where(low, w, turned), jnp.where(low, turned, w)

    k2[64 * d : 64 * d + 32, :], k2[64 * d + 32 : 64 * d + 64, :] = sides(v[0:32])
    k3[72 * d : 72 * d + 32, :], k3[72 * d + 32 : 72 * d + 64, :] = sides(v[32:64])
    k3[72 * d + 64 : 72 * d + 72, :] = sides(v[64:72])[0]
    for k in range(4):
        part = jnp.where(lane[:8] // 32 == k, v[72:80], 0.0)
        k1[32 * d + 8 * k : 32 * d + 8 * k + 8, :] = fold_lanes(part, 32)


def noisy_weights(shard, hm, hs, hb, fn, hn, vm, vs, am, adv_s, on):
    atoms, outs = vm.shape[1], on.shape[1]
    lane = lax.broadcasted_iota(jnp.int32, (16, 128), 1)
    for h in range(2):
        wide = hm[h] + hs[h] * fn[h : h + 1, :] * as_column(hn[0, h : h + 1, :])
        shard[h, :, 0:3072] = wide[:, 0:3072].astype(BF16)
        last = jnp.concatenate([wide[:, 3072:], jnp.zeros((16, 64), F32)], axis=1)
        last = jnp.where(lane == 64, as_column(hb[h : h + 1, :]), last)
        shard[h, :, 3072:3200] = last.astype(BF16)
    val = vm[...] + vs[...] * as_column(hn[1, 0:1, :]) * on[:, :atoms]
    adv = am[...] + adv_s[...] * as_column(hn[1, 1:2, :]) * on[:, atoms:]
    out = jnp.concatenate([val, adv, jnp.zeros((16, 1024 - outs), F32)], axis=1).astype(BF16)
    shard[0, :, 3200:] = out[:, :512]
    shard[1, :, 3200:] = out[:, 512:]


def slot_rows(staged, tt, cnt, act, sw):
    atoms, slots = tt.shape
    lane = lax.broadcasted_iota(jnp.int32, (8, slots), 1)
    source = lax.broadcasted_iota(jnp.int32, (8, slots), 0)
    cap = slots // 8
    used = jnp.sum(jnp.where(lane // cap == source, as_column(cnt[...].astype(F32)), 0.0), axis=0, keepdims=True)
    valid = jnp.where((lane[0:1] % cap).astype(F32) < used, 1.0, 0.0)
    staged[...] = jnp.zeros_like(staged)
    staged[0:atoms, :] = tt[...]
    staged[atoms : atoms + 1, :] = valid * sw[...]
    staged[atoms + 1 : atoms + 2, :] = valid
    staged[atoms + 2 : atoms + 3, :] = act[...].astype(F32)
    return jnp.transpose(staged[...])


def shifted_blocks(x):
    rows = x.shape[0]
    return (
        x[:, 0:128],
        x[:, 112:240],
        jnp.concatenate([x[:, 224:336], jnp.zeros((rows, 16), x.dtype)], axis=1),
    )


def forward_kernel(shared, *refs):
    if shared:
        ins, refs = refs[:17], refs[17:]
        (x_in, c1, c2, c3t, hm, hs, hb, fn, hn, vm, vs, am, adv_s, on, tt, cnt, act), refs = ins, refs
        (sw,), refs = refs[:1], refs[1:]
    else:
        (x_in, k1_ref, k2_ref, k3_ref), refs = refs[:4], refs[4:]
    (a1_out, s1_out, *whole_out, y_out, y0_ref), refs = refs[:8], refs[8:]
    if shared:
        (w_out, slot_out, k2_ref, k3_ref), refs = refs[:4], refs[4:]
    (carry, a1s, b1_ref, b2_ref, b3_ref, *whole, whole_sem, slopes_one, shifted, step_sem, x_first, x_slots, x_sem), refs = refs[:16], refs[16:]
    a2_ref, s2_ref, f_ref, s3_ref = whole
    i = pl.program_id(0)
    rows = x_first.shape[1]
    x_ref = x_slots.at[lax.rem(i, 2)]
    s1_ref, y_ref = slopes_one.at[lax.rem(i, 2)], shifted.at[lax.rem(i, 2)]

    def step_copies(step):
        slot, two = lax.rem(step, 2), pl.ds(2 * step, 2)
        return [
            pltpu.make_async_copy(a1s.at[two], a1_out.at[two], step_sem.at[slot, 0]),
            pltpu.make_async_copy(slopes_one.at[slot], s1_out.at[two], step_sem.at[slot, 1]),
            pltpu.make_async_copy(shifted.at[slot], y_out.at[pl.ds(4 * step, 4)], step_sem.at[slot, 2]),
        ]

    def frame_copy(step):
        slot = lax.rem(step, 2)
        return pltpu.make_async_copy(x_in.at[pl.ds(4 * step + 1, 4)], x_slots.at[slot], x_sem.at[slot])

    first_frames = pltpu.make_async_copy(x_in.at[0], x_first, x_sem.at[2])

    @pl.when(i == 0)
    def _():
        start([first_frames, frame_copy(i)])

    @pl.when(i >= 2)
    def _():
        finish(step_copies(i - 2))

    if shared:
        k1_ref, shard, kern_own, kern_buf, staged, slot_src, slot_buf, kern_s, kern_r, slot_s, slot_r, own_sem, sems, core_sems = refs
        flow_stage = {
            (f, s): (shard, w_out, flow, s, sems.at[0, f, s], sems.at[1, f, s])
            for f, flow in enumerate(GATHER_FLOWS)
            for s in range(3)
        }

        def kern_copies():
            return share("dp", 8, lambda _: kern_own, kern_buf, kern_s, kern_r)

        def slot_copies():
            ids = [lax.rem(lax.axis_index("dp") + j, 8) for j in range(1, 8)]
            return share("dp", 8, lambda j: slot_src.at[ids[j]], slot_buf, slot_s, slot_r)

        def own_copies():
            me = coordinates()
            return [
                pltpu.make_async_copy(shard.at[h], w_out.at[h, me["x"], me["c"], me["z"], me["y"]], own_sem.at[h])
                for h in range(2)
            ]

        def to_core(f, last):
            return core_copies(w_out, GATHER_FLOWS[f], last, core_sems.at[0, f, last], core_sems.at[1, f, last])

        def begin():
            greet()
            kern_own[...] = pack_shards(c1[...], c2[...], c3t[...]).astype(BF16)
            kern_buf[lax.axis_index("dp")] = kern_own[...]
            noisy_weights(shard, hm, hs, hb, fn, hn, vm, vs, am, adv_s, on)
            packed = slot_rows(staged, tt, cnt, act, sw).reshape(8, 2, 32, 128)
            lane = lax.broadcasted_iota(jnp.int32, (8, 32, 128), 2)
            slot_src[...] = jnp.where(lane < 64, packed[:, 0], pltpu.roll(packed[:, 1].reshape(256, 128), 64, 1).reshape(8, 32, 128))
            slot_buf[lax.axis_index("dp")] = slot_src[lax.axis_index("dp")]
            greeted()
            start(kern_copies())
            for f, s in GATHER_FIRST:
                enter(f, s)
            start(own_copies())
            prepare()
            finish(own_copies())
            finish(kern_copies())
            for d in range(8):
                unpack_shards(d, kern_buf[d].astype(F32), k1_ref, k2_ref, k3_ref)

        def enter(f, s):
            if s > 0:
                finish(gather_copies(*flow_stage[f, s - 1]))
            start(gather_copies(*flow_stage[f, s]))
            if s == 2:
                start(to_core(f, 0))

        def point(step, k):
            for (at, where), entries in GATHER_PLAN.items():
                if where == k:

                    @pl.when(step == at)
                    def _():
                        for f, s in entries:
                            enter(f, s)

            if k == 0:

                @pl.when(step == 4)
                def _():
                    start(slot_copies())

        def end():
            for f, s in GATHER_LAST:
                enter(f, s)
            for f in GATHER_DONE:
                finish(gather_copies(*flow_stage[f, 2]))
                start(to_core(f, 1))
            finish(slot_copies())
            slot_out[:, 0:32] = slot_buf[...]
            slot_out[:, 32:64] = pltpu.roll(slot_buf[...].reshape(256, 128), 64, 1).reshape(8, 32, 128)
            for f in GATHER_DONE:
                for last in range(2):
                    finish(to_core(f, last))

    def prepare():
        b2_ref[...] = jnp.zeros_like(b2_ref)
        b3_ref[...] = jnp.zeros_like(b3_ref)
        finish([first_frames])
        for r in range(4):
            for j, blk in enumerate(shifted_blocks(x_first[r])):
                carry[j, :, 128 * r : 128 * r + 128] = blk
        y0_ref[...] = carry[...]

    @pl.when(i == 0)
    def _():
        if shared:
            begin()
        else:
            prepare()
        fill_band_one(k1_ref, b1_ref)
        fill_band_two(k2_ref, b2_ref)
        fill_band_three(k3_ref, b3_ref)

    finish([frame_copy(i)])

    @pl.when(i < 4)
    def _():
        start([frame_copy(i + 1)])

    for pp in range(4):
        for r in range(4):
            for j, blk in enumerate(shifted_blocks(x_ref[pp, r])):
                y_ref[pp, j, :, 128 * r : 128 * r + 128] = blk
        for j in range(3):
            lhs = jnp.concatenate([carry[j] if pp == 0 else y_ref[pp - 1, j], y_ref[pp, j]], axis=1)
            act, slope = silu_and_slope(dot(lhs, b1_ref[...]))
            act = act.astype(BF16)
            a1s[2 * i + pp // 2, pp % 2, :, 256 * j : 256 * j + 256] = act
            s1_ref[pp // 2, pp % 2, :, 256 * j : 256 * j + 256] = slope.astype(BF16)
        if shared:
            point(i, pp)
    carry[...] = y_ref[3]
    start(step_copies(i))

    def second(p):
        for lo, hi, n0, n1 in ((0, 384, 0, 256), (256, 640, 256, 512), (512, 768, 512, 640)):
            lhs = jnp.concatenate([a1s[p + u // 2, u % 2, :, lo:hi] for u in range(4)], axis=1)
            rhs = jnp.concatenate([b2_ref[u, lo:hi, n0:n1] for u in range(4)], axis=0)
            act, slope = silu_and_slope(dot(lhs, rhs))
            act = act.astype(BF16)
            a2_ref[p, :, n0:n1] = act
            s2_ref[p, :, n0:n1] = slope.astype(BF16)

    def third(p, odd):
        acts, slopes = [], []
        for lo, hi, n0, n1 in ((0, 384, 0, 256), (256, 640, 256, 512)):
            lhs = jnp.concatenate([a2_ref[p + u, :, lo:hi] for u in range(3)], axis=1)
            rhs = jnp.concatenate([b3_ref[u, lo:hi, n0:n1] for u in range(3)], axis=0)
            act, slope = silu_and_slope(dot(lhs, rhs))
            acts.append(act)
            slopes.append(slope)
        lane = lax.broadcasted_iota(jnp.int32, (rows, 512), 1)
        base = (p // 2) * 896
        for out, parts in ((f_ref, acts), (s3_ref, slopes)):
            whole = jnp.where(lane < 448, jnp.concatenate(parts, axis=1), 0.0)
            if not odd:
                out[:, pl.ds(pl.multiple_of(base, 128), 512)] = whole.astype(BF16)
            else:
                whole = pltpu.roll(whole, 64, 1)
                at = pl.ds(pl.multiple_of(base + 384, 128), 128)
                out[:, at] = (out[:, at].astype(F32) + whole[:, :128]).astype(BF16)
                out[:, pl.ds(pl.multiple_of(base + 512, 128), 384)] = whole[:, 128:].astype(BF16)

    @pl.when(i >= 1)
    def _():
        second(2 * i - 1)

    if shared:
        point(i, 4)
    second(2 * i)
    if shared:
        point(i, 5)

    @pl.when(i >= 2)
    def _():
        third(2 * i - 3, True)

    if shared:
        point(i, 6)

    @pl.when(i >= 1)
    def _():
        third(2 * i - 2, False)

    @pl.when(i == 4)
    def _():
        lane = lax.broadcasted_iota(jnp.int32, (rows, 128), 1)
        last = f_ref[:, 3072:3200].astype(F32)
        f_ref[:, 3072:3200] = jnp.where(lane == 64, 1.0, last).astype(BF16)
        leaving = [pltpu.make_async_copy(whole[k], whole_out[k], whole_sem.at[k]) for k in range(4)]
        start(leaving)
        if shared:
            end()
        finish(leaving)
        for step in (i - 1, i):
            finish(step_copies(step))


def full(shape):
    return pl.BlockSpec(shape, lambda *_: (0,) * len(shape))


def once(shape):
    return pl.BlockSpec(shape, lambda *_: (0,) * len(shape), pipeline_mode=pl.Buffered(1))


BANDS = [(1024, 256), (4, 768, 640), (3, 640, 512)]


def torso_forward(x, kernels, shared=None):
    rows = x.shape[2]
    shapes = [(10, 2, rows, 768)] * 2 + [(9, rows, 640)] * 2 + [(rows, 3200)] * 2 + [(20, 3, rows, 512), (3, rows, 512)]
    args = [x, *kernels]
    out_specs = (
        [pl.BlockSpec(memory_space=pl.ANY)] * 7
        + [once((3, rows, 512))]
    )
    out_shape = [jax.ShapeDtypeStruct(s, BF16) for s in shapes]
    scratch = [
        pltpu.VMEM((3, rows, 512), BF16),
        pltpu.VMEM((10, 2, rows, 768), BF16),
        *[pltpu.VMEM(s, BF16) for s in BANDS],
        *[pltpu.VMEM(s, BF16) for s in shapes[2:6]],
        pltpu.SemaphoreType.DMA((4,)),
        pltpu.VMEM((2, 2, 2, rows, 768), BF16),
        pltpu.VMEM((2, 4, 3, rows, 512), BF16),
        pltpu.SemaphoreType.DMA((2, 3)),
        pltpu.VMEM((4, rows, 336), BF16),
        pltpu.VMEM((2, 4, 4, rows, 336), BF16),
        pltpu.SemaphoreType.DMA((3,)),
    ]
    params = {}
    if shared is not None:
        args += shared
        out_specs += [pl.BlockSpec(memory_space=pl.ANY), once((8, 64, 128)), once((512, 128)), once((576, 128))]
        out_shape += [
            jax.ShapeDtypeStruct((2, 2, 2, 4, 2, 16, HALF), BF16),
            jax.ShapeDtypeStruct((8, 64, 128), F32),
            jax.ShapeDtypeStruct((512, 128), F32),
            jax.ShapeDtypeStruct((576, 128), F32),
        ]
        scratch += [
            pltpu.VMEM((256, 128), F32),
            pltpu.VMEM((2, 16, HALF), BF16),
            pltpu.VMEM((80, 128), BF16),
            pltpu.VMEM((8, 80, 128), BF16),
            pltpu.VMEM((128, 512), F32),
            pltpu.VMEM((8, 32, 128), F32),
            pltpu.VMEM((8, 32, 128), F32),
            *[pltpu.SemaphoreType.DMA((7,))] * 4,
            pltpu.SemaphoreType.DMA((2,)),
            pltpu.SemaphoreType.DMA((2, len(GATHER_FLOWS), 3, 3)),
            pltpu.SemaphoreType.DMA((2, len(GATHER_FLOWS), 2, 3)),
        ]
        params = dict(collective_id=0, has_side_effects=True)
    return pl.pallas_call(
        functools.partial(forward_kernel, shared is not None),
        grid=(5,),
        in_specs=[
            pl.BlockSpec(memory_space=pl.ANY),
            *[once(v.shape) for v in args[1:]],
        ],
        out_specs=out_specs,
        out_shape=out_shape,
        scratch_shapes=scratch,
        compiler_params=pltpu.CompilerParams(vmem_limit_bytes=VMEM_LIMIT, **params),
        name="torso_forward",
    )(*args)


KERNEL_ROWS = [(72, 8, 16), (0, 72, 80)]


def pack_first(d, o1):
    lane = lax.broadcasted_iota(jnp.int32, (8, 128), 1) // 32
    one = jnp.zeros((8, 128), F32)
    for k in range(4):
        one = jnp.where(lane == k, o1[32 * d + 8 * k : 32 * d + 8 * k + 8, :], one)
    return jnp.concatenate([one, jnp.zeros((8, 128), F32)], axis=0)


def pack_others(d, o2, o3):
    lane = lax.broadcasted_iota(jnp.int32, (32, 128), 1)
    two = jnp.where(lane < 64, o2[64 * d : 64 * d + 32, :], o2[64 * d + 32 : 64 * d + 64, :])
    three = jnp.where(lane < 64, o3[72 * d : 72 * d + 32, :], o3[72 * d + 32 : 72 * d + 64, :])
    return jnp.concatenate([two, three, o3[72 * d + 64 : 72 * d + 72, :], jnp.zeros((8, 128), F32)], axis=0)


BACK_LANES = ((0, 256), (128, 512), (384, 640))


def backward_kernel(summed, *refs):
    (*streams, y0_in, a2_in, s2_in, s3_in, fg_in, k2_ref, k3_ref), refs = refs[:10], refs[10:]
    whole_in = (y0_in, a2_in, s2_in, s3_in, fg_in)
    if summed:
        (dw_ref, stat_ref, dsum_ref, stat_out, kern_out), refs = refs[:5], refs[5:]
    (o1_ref, o2_ref, o3_ref), refs = refs[:3], refs[3:]
    (carry, *whole, whole_sem), refs = refs[:6], refs[6:]
    slots, step_sem, refs = refs[:3], refs[3], refs[4:]
    (back, grad, g3, g2, b2_ref, b3_ref, d1_ref, d2a_ref, d2b_ref, d2c_ref, d3_ref), refs = refs[:11], refs[11:]
    a2_ref, s2_ref, s3_ref, fg_ref = whole
    coming = [pltpu.make_async_copy(whole_in[k], (carry, *whole)[k], whole_sem.at[k]) for k in range(5)]
    if summed:
        (acc, stat_dp, stat_mp, load_sem, sems, send_s, recv_s), bufs = refs[:7], refs[7:]
        kern_bufs, bufs = bufs[:6], bufs[6:]
        me = coordinates()
        stages = {}
        at = 0
        for f, flow in enumerate(SUM_FLOWS):
            for s in range(3):
                stages[f, s] = (dw_ref if s == 0 else acc, flow, s, bufs[at], sems.at[0, at], sems.at[1, at])
                at += 1

        loaded = {
            f: pltpu.make_async_copy(
                dw_ref.at[half, :, :, :, :, lo:hi], acc.at[half, :, :, :, :, lo:hi], load_sem.at[f]
            )
            for f, (half, lo, hi, _) in enumerate(SUM_FLOWS)
        }

        def stat_copies(axis, count, k):
            src = stat_ref if k == 0 else stat_mp.at[lax.axis_index("mp")]
            return share(axis, count, lambda _: src, (stat_dp, stat_mp)[k], send_s.at[k], recv_s.at[k])

        def kern_copies(group, k):
            kern_send, kern_dp, kern_mp = kern_bufs[3 * group : 3 * group + 3]
            sem = 2 + 2 * group + k
            if k == 1:
                return share("mp", 4, lambda _: kern_mp.at[lax.axis_index("mp")], kern_mp, send_s.at[sem], recv_s.at[sem])
            ids = [lax.rem(lax.axis_index("dp") + j, 8) for j in range(1, 8)]
            return share("dp", 8, lambda j: kern_send.at[ids[j]], kern_dp, send_s.at[sem], recv_s.at[sem])

        def first():
            start(list(loaded.values()))
            greeted()
            for f, s in SUM_FIRST:
                enter(f, s)
            start(stat_copies("dp", 8, 0))
            stat_dp[lax.axis_index("dp")] = stat_ref[...]

        def stats_over():
            finish(stat_copies("dp", 8, 0))
            stat_mp[lax.axis_index("mp")] = in_order(stat_dp, 8)
            start(stat_copies("mp", 4, 1))

        def enter(f, s):
            if s > 0:
                leave(f, s - 1)
            start(sum_copies(*stages[f, s]))

        def leave(f, s):
            if s == 0:
                finish([loaded[f]])
            finish(sum_copies(*stages[f, s]))
            add_arrived(acc, *stages[f, s][1:4], out=dsum_ref if s == 2 else None)

        def point(step, k):
            for (at, where), entries in SUM_PLAN.items():
                if where == k:

                    @pl.when(step == at)
                    def _():
                        for f, s in entries:
                            enter(f, s)

            extra = [(0, 5, stats_over), (1, 6, stats_done), (4, 3, lambda: kernel_out(1))]
            for at, where, what in extra:
                if where == k:

                    @pl.when(step == at)
                    def _():
                        what()

        def stats_done():
            finish(stat_copies("mp", 4, 1))
            stat_out[...] = in_order(stat_mp, 4)

        def kernel_out(group):
            kern_send, kern_dp, _ = kern_bufs[3 * group : 3 * group + 3]
            if group == 0:
                take_band_one(d1_ref, o1_ref)
            else:
                take_band_two(((d2a_ref, 0, 0, 4), (d2b_ref, 8, 4, 4), (d2c_ref, 16, 8, 1)), o2_ref)
                take_band_three(d3_ref, o3_ref)
            for d in range(8):
                rows_out = pack_first(d, o1_ref) if group == 0 else pack_others(d, o2_ref, o3_ref)
                kern_send[d] = rows_out.astype(BF16)
            kern_dp[lax.axis_index("dp")] = kern_send[lax.axis_index("dp")]
            start(kern_copies(group, 0))

        def kernel_over(group):
            _, kern_dp, kern_mp = kern_bufs[3 * group : 3 * group + 3]
            finish(kern_copies(group, 0))
            kern_mp[lax.axis_index("mp")] = in_order(kern_dp, 8)
            start(kern_copies(group, 1))

        def kernel_done(group):
            at, count, _ = KERNEL_ROWS[group]
            finish(kern_copies(group, 1))
            total = in_order(kern_bufs[3 * group + 2], 4) / stat_out[9:10, :]
            kern_out[at : at + count, :] = total[:count]

    i = pl.program_id(0)
    rows = g3.shape[1]
    y_ref, a1_ref, s1_ref = (slot.at[lax.rem(i, 2)] for slot in slots)

    def step_copies(step):
        return [
            pltpu.make_async_copy(
                streams[k].at[pl.ds(count * step, count)], slots[k].at[lax.rem(step, 2)], step_sem.at[lax.rem(step, 2), k]
            )
            for k, count in enumerate((4, 2, 2))
        ]


    @pl.when(i == 0)
    def _():
        if summed:
            greet()
        start(coming[::-1])
        start(step_copies(i))
        b2_ref[...] = jnp.zeros_like(b2_ref)
        b3_ref[...] = jnp.zeros_like(b3_ref)
        fill_band_two(k2_ref, b2_ref)
        fill_band_three(k3_ref, b3_ref)
        for r in range(2):
            for j, (n0, n1) in enumerate(BACK_LANES):
                for t in range(2):
                    turned = jnp.transpose(b2_ref[2 * t + r, 256 * j : 256 * j + 256, n0:n1].astype(F32))
                    back[j, r, t * (n1 - n0) : (t + 1) * (n1 - n0), :] = turned.astype(BF16)
        grad[3] = jnp.zeros(grad.shape[1:], BF16)
        finish(coming[3:])
        for at in (0, 1, 9, 10):
            g3[at] = jnp.zeros((rows, 512), BF16)
        for at in (0, 10):
            g2[at] = jnp.zeros((rows, 640), BF16)
        lane = lax.broadcasted_iota(jnp.int32, (rows, 512), 1)
        for p in range(7):
            base = (p // 2) * 896 + (384 if p % 2 else 0)
            both = fg_ref[:, base : base + 512].astype(F32) * s3_ref[:, base : base + 512].astype(F32)
            if p % 2:
                both = pltpu.roll(both, 448, 1)
            g3[p + 2] = jnp.where(lane < 448, both, 0.0).astype(BF16)
        if summed:
            first()
            point(i, "a0")
        finish([coming[1]])
        for u in range(3):
            total = 0.0
            for m in range(2):
                lhs = a2_ref[u : u + 7, :, 256 * m : 256 * m + 384].reshape(7 * rows, 384)
                rhs = g3[2:9, :, 256 * m : 256 * m + 256].reshape(7 * rows, 256)
                total = total + dot_tn(lhs, rhs)
            d3_ref[u] = total
            if summed:
                point(i, "a%d" % (1 + u))
        d1_ref[...] = jnp.zeros_like(d1_ref)
        d2a_ref[...] = jnp.zeros_like(d2a_ref)
        d2b_ref[...] = jnp.zeros_like(d2b_ref)
        d2c_ref[...] = jnp.zeros_like(d2c_ref)
        for at, (lo, hi, n0, n1) in enumerate(((0, 256, 0, 256), (256, 512, 128, 512), (512, 640, 384, 512))):
            rhs = jnp.concatenate([b3_ref[u, lo:hi, n0:n1] for u in range(3)], axis=1)
            if at == 0:
                finish([coming[0], coming[2]])
            for p in (0, 3, 6):
                lhs = jnp.concatenate([g3[p + 2 - u : p + 5 - u, :, n0:n1].reshape(3 * rows, n1 - n0) for u in range(3)], axis=1)
                product = dot_nt(lhs, rhs) * s2_ref[p : p + 3, :, lo:hi].reshape(3 * rows, hi - lo).astype(F32)
                g2[p + 1 : p + 4, :, lo:hi] = product.astype(BF16).reshape(3, rows, hi - lo)
            if summed:
                point(i, "a%d" % (4 + at))

    finish(step_copies(i))

    @pl.when(i < 4)
    def _():
        start(step_copies(i + 1))

    for r in range(2):
        for ref, lo, hi, n0, n1 in ((d2a_ref, 0, 384, 0, 256), (d2b_ref, 256, 640, 256, 512), (d2c_ref, 512, 768, 512, 640)):
            lhs = a1_ref[:, r, :, lo:hi].reshape(2 * rows, hi - lo)
            rhs = [g2[pl.ds(2 * i + 1 - t, 2), :, n0:n1].reshape(2 * rows, n1 - n0) for t in range(2)]
            both = dot_tn(lhs, jnp.concatenate(rhs, axis=1))
            for t in range(2):
                ref[2 * t + r] += both[:, t * (n1 - n0) : (t + 1) * (n1 - n0)]
        if summed:
            point(i, 2 * r)
            point(i, 2 * r + 1)

    for j, (n0, n1) in enumerate(BACK_LANES):
        lanes = slice(256 * j, 256 * j + 256)
        before = grad[3, :, lanes]
        for r in range(2):
            lhs = [g2[pl.ds(2 * i + 1 - t, 2), :, n0:n1].reshape(2 * rows, n1 - n0) for t in range(2)]
            product = dot(jnp.concatenate(lhs, axis=1), back[j, r, : 2 * (n1 - n0), :])
            for k in range(2):
                slope = s1_ref[k, r, :, lanes].astype(F32)
                grad[2 * k + r, :, lanes] = (product[k * rows : (k + 1) * rows] * slope).astype(BF16)
        now = [grad[k, :, lanes] for k in range(4)]
        rhs = jnp.concatenate([jnp.concatenate(now, axis=0), jnp.concatenate([before, *now[:3]], axis=0)], axis=1)
        lhs = jnp.concatenate([carry[j], *[y_ref[k, j] for k in range(3)]], axis=0)
        both = dot_tn(lhs, rhs)
        d1_ref[0:512, :] += both[:, 0:256]
        d1_ref[512:1024, :] += both[:, 256:512]
        if summed:
            point(i, 4 + j)
    carry[...] = y_ref[3]

    @pl.when(i == 4)
    def _():
        for j in range(3):
            d1_ref[512:1024, :] += dot_tn(y_ref[3, j], grad[3, :, 256 * j : 256 * j + 256])

    @pl.when(i == 4)
    def _():
        if summed:
            kernel_out(0)
            for f, s in SUM_LAST:
                enter(f, s)
            kernel_over(1)
            kernel_over(0)
            for f in SUM_DONE:
                leave(f, 2)
            kernel_done(1)
            kernel_done(0)
        else:
            take_band_one(d1_ref, o1_ref)
            take_band_two(((d2a_ref, 0, 0, 4), (d2b_ref, 8, 4, 4), (d2c_ref, 16, 8, 1)), o2_ref)
            take_band_three(d3_ref, o3_ref)


def torso_backward(y, y0, a1, s1, a2, s2, s3, fg, kern2, kern3, summed=None):
    rows = y.shape[2]
    sums = [(1024, 256), (4, 384, 256), (4, 384, 256), (4, 256, 128), (3, 384, 256)]
    own = [(256, 128), (512, 128), (576, 128)]
    args = [y, a1, s1, y0, a2, s2, s3, fg, kern2, kern3]
    in_specs = [
        *[pl.BlockSpec(memory_space=pl.ANY)] * 8,
        *[once(v.shape) for v in args[8:]],
    ]
    scratch = [
        *[pltpu.VMEM(v.shape, BF16) for v in args[3:8]],
        pltpu.SemaphoreType.DMA((5,)),
        pltpu.VMEM((2, 4, 3, rows, 512), BF16),
        pltpu.VMEM((2, 2, 2, rows, 768), BF16),
        pltpu.VMEM((2, 2, 2, rows, 768), BF16),
        pltpu.SemaphoreType.DMA((2, 3)),
        pltpu.VMEM((3, 2, 768, 256), BF16),
        pltpu.VMEM((4, rows, 768), BF16),
        pltpu.VMEM((11, rows, 512), BF16),
        pltpu.VMEM((11, rows, 640), BF16),
        *[pltpu.VMEM(s, BF16) for s in BANDS[1:]],
        *[pltpu.VMEM(s, F32) for s in sums],
    ]
    outs = own
    params = {}
    if summed is not None:
        args += summed
        block = (2, *AXES.values(), 16, HALF)
        in_specs += [pl.BlockSpec(memory_space=pl.ANY), once((16, 128))]
        outs = [(2, 16, HALF), (16, 128), (80, 128)]
        buffers = flow_buffers(SUM_FLOWS)
        scratch = [pltpu.VMEM(s, F32) for s in own] + scratch
        scratch += [
            pltpu.VMEM(block, BF16),
            pltpu.VMEM((8, 16, 128), F32),
            pltpu.VMEM((4, 16, 128), F32),
            pltpu.SemaphoreType.DMA((len(SUM_FLOWS),)),
            pltpu.SemaphoreType.DMA((2, len(buffers), 3)),
            pltpu.SemaphoreType.DMA((6, 7)),
            pltpu.SemaphoreType.DMA((6, 7)),
            *[
                pltpu.VMEM((count, padded, 128), kind)
                for _, _, padded in KERNEL_ROWS
                for count, kind in ((8, BF16), (8, BF16), (4, F32))
            ],
            *[pltpu.VMEM(s, BF16) for s in buffers],
        ]
        params = dict(collective_id=1, has_side_effects=True)
    return pl.pallas_call(
        functools.partial(backward_kernel, summed is not None),
        grid=(5,),
        in_specs=in_specs,
        out_specs=[once(s) for s in outs],
        out_shape=[jax.ShapeDtypeStruct(s, F32) for s in outs],
        scratch_shapes=scratch,
        compiler_params=pltpu.CompilerParams(vmem_limit_bytes=VMEM_LIMIT, **params),
        name="torso_backward",
    )(*args)


def high_low(v):
    high = v.astype(BF16)
    return high, (v - high.astype(F32)).astype(BF16)


HEAD_COLUMNS = [(0, 1024), (1024, 2048), (2048, HALF)]


def heads_kernel(atoms, acts, paired, f_ref, w_ref, bias_ref, slot_ref, row_ref, dw_out, fg_ref, prio_ref, stat_ref, *refs):
    if paired:
        dw_ref, arrived, w_hbm, w_ref, summed, dw_hbm = *refs[:2], w_ref, refs[2], refs[3], dw_out
        send, recv, load, save = refs[4:]
        loads = {
            (h, k): pltpu.make_async_copy(w_hbm.at[h, :, lo:hi], w_ref.at[h, :, lo:hi], load.at[h, k])
            for h in range(2)
            for k, (lo, hi) in enumerate(HEAD_COLUMNS)
        }
        start(list(loads.values()))
        me = coordinates()
        other = device_at({**me, "c": 1 - me["c"]})
        barrier = pltpu.get_barrier_semaphore()
        pl.semaphore_signal(barrier, inc=1, **other)

        def to_core(h, k):
            lo, hi = HEAD_COLUMNS[k]
            src = dw_ref.at[h, :, 1 - me["c"], :, :, :, lo:hi]
            return pltpu.make_async_remote_copy(src, arrived.at[h, :, :, :, :, lo:hi], send.at[h, k], recv.at[h, k], **other)

        def saving(h, k):
            lo, hi = HEAD_COLUMNS[k]
            return pltpu.make_async_copy(summed.at[h, :, :, :, :, lo:hi], dw_hbm.at[h, :, :, :, :, lo:hi], save.at[h, k])

        def add_core(h, k):
            lo, hi = HEAD_COLUMNS[k]
            to_core(h, k).wait()

            def one(j, _):
                x, z, y = j // 8, (j // 2) % 4, j % 2
                own = dw_ref[h, x, me["c"], z, y, :, lo:hi]
                summed[h, x, z, y, :, lo:hi] = own + arrived[h, x, z, y, :, lo:hi]
                return 0

            lax.fori_loop(0, 16, one, 0)
            saving(h, k).start()


    def put(h, lo, hi, v):
        v = v.astype(BF16)
        if paired:
            dw_ref[h, :, :, :, :, :, lo:hi] = v.reshape(2, 2, 4, 2, 16, hi - lo)
        else:
            dw_out[h, :, lo:hi] = v

    rows = f_ref.shape[0]
    slots = slot_ref.shape[0]
    wide = 1024
    lane = lax.broadcasted_iota(jnp.int32, (1, wide), 1)
    selt = jnp.where(lax.broadcasted_iota(jnp.int32, (rows, slots), 0) == row_ref[...], 1.0, 0.0).astype(BF16)
    action = slot_ref[:, atoms + 2 : atoms + 3]
    which = jnp.where(lane < atoms, -1, jnp.where(lane < atoms * (acts + 1), (lane - atoms) // atoms, -2)).astype(F32)
    coeff = jnp.where(which == -1.0, 1.0, 0.0) + jnp.where(which == action, 1.0, 0.0) - jnp.where(which >= 0.0, 1.0 / acts, 0.0)
    atom = jnp.where(which >= -1.0, lane - atoms * (which.astype(jnp.int32) + 1), -1)
    fold = jnp.where(lax.broadcasted_iota(jnp.int32, (128, wide), 0) == atom, 1.0, 0.0).astype(BF16)
    pre = []
    for h in range(2):
        total = 0.0
        for k, (lo, hi) in enumerate(HEAD_COLUMNS):
            if paired:
                loads[h, k].wait()
            hi = min(hi, 3200)
            total = total + dot_nt(f_ref[:, lo:hi], w_ref[h, :, lo:hi])
        pre.append(total)
    hidden, slope = [], []
    for k in range(2):
        a, s = silu_and_slope(pre[k])
        hidden.append(a.astype(BF16))
        slope.append(s)
    out_w = jnp.concatenate([w_ref[0, :, 3200:], w_ref[1, :, 3200:]], axis=1)
    zero = jnp.zeros((), BF16)
    w_val = jnp.where(lane[:, :128] < atoms, out_w[:, :128].astype(F32), 0.0).astype(BF16)
    w_adv = jnp.where(lane >= atoms, out_w.astype(F32), 0.0).astype(BF16)
    outs = bias_ref.shape[1]
    bias = jnp.concatenate([bias_ref[...], jnp.zeros((1, wide - outs), F32)], axis=1)
    logits = dot(hidden[1], w_adv) + bias
    logits = jnp.concatenate([logits[:, :128] + dot(hidden[0], w_val), logits[:, 128:]], axis=1)
    high, low = high_low(logits)
    per_slot = dot_tn(selt, high) + dot_tn(selt, low)
    high, low = high_low(per_slot * coeff)
    q = dot_nt(high, fold) + dot_nt(low, fold)
    lane_q = lax.broadcasted_iota(jnp.int32, (slots, 128), 1)
    used = lane_q < atoms
    top = jnp.max(jnp.where(used, q, -jnp.inf), axis=1, keepdims=True)
    shifted = jnp.where(used, jnp.exp(jnp.where(used, q - top, 0.0)), 0.0)
    total = jnp.sum(shifted, axis=1, keepdims=True)
    tgt = jnp.where(used, slot_ref[...], 0.0)
    cross = -jnp.sum(jnp.where(used, tgt * (q - top - jnp.log(total)), 0.0), axis=1, keepdims=True)
    coef = slot_ref[:, atoms : atoms + 1]
    valid = slot_ref[:, atoms + 1 : atoms + 2]
    prio_ref[...] = jnp.transpose(jnp.broadcast_to(valid * cross, (slots, 128)))[0:1]
    q_grad = coef * (shifted * (jnp.sum(tgt, axis=1, keepdims=True) / total) - tgt)
    high, low = high_low(q_grad)
    lgrad = ((dot(high, fold) + dot(low, fold)) * coeff).astype(BF16)
    bias_grad = jnp.sum(lgrad.astype(F32), axis=0, keepdims=True)
    for k in range(8):
        stat_ref[k : k + 1, :] = bias_grad[:, 128 * k : 128 * k + 128]
    stat_ref[8:9, :] = jnp.broadcast_to(jnp.sum(coef * cross, axis=0, keepdims=True), (1, 128))
    stat_ref[9:10, :] = jnp.broadcast_to(jnp.sum(valid, axis=0, keepdims=True), (1, 128))
    stat_ref[10:16, :] = jnp.zeros((6, 128), F32)
    grad = dot(selt, lgrad).astype(BF16)
    d_adv = dot_tn(hidden[1], grad)
    d_val = dot_tn(hidden[0], grad[:, :128])
    put(0, 3200, 3328, jnp.where(lane[:, :128] < atoms, d_val, d_adv[:, :128]))
    put(0, 3328, HALF, d_adv[:, 128:512])
    put(1, 3200, HALF, d_adv[:, 512:])
    pre_grad = [
        (dot_nt(grad[:, :128], w_val) * slope[0]).astype(BF16),
        (dot_nt(grad, w_adv) * slope[1]).astype(BF16),
    ]
    for k in range(2):
        for part, (lo, hi) in enumerate(((0, 1024), (1024, 2048), (2048, 3200))):
            put(k, lo, hi, dot_tn(pre_grad[k], f_ref[:, lo:hi]))
            if paired:
                if (k, part) == (0, 0):
                    pl.semaphore_wait(barrier, 1)
                to_core(k, part).start()
    for part, (lo, hi) in enumerate(((0, 1024), (1024, 2048), (2048, 3200))):
        back = dot(pre_grad[0], w_ref[0, :, lo:hi]) + dot(pre_grad[1], w_ref[1, :, lo:hi])
        fg_ref[:, lo:hi] = back.astype(BF16)
        if paired:
            add_core(0, part)
    if paired:
        for part in range(3):
            add_core(1, part)
        for h in range(2):
            for part in range(3):
                saving(h, part).wait()


def heads(atoms, acts, feats, weights, bias, per_slot, rows_of_slot, paired=False):
    slots = per_slot.shape[0]
    block = (2, 2, 4, 2, 16, HALF)
    scratch, params = [], {}
    if paired:
        scratch = [
            pltpu.VMEM((2, 2, 2, 4, 2, 16, HALF), BF16),
            pltpu.VMEM(block, BF16),
            pltpu.VMEM(weights.shape, BF16),
            pltpu.VMEM(block, BF16),
            *[pltpu.SemaphoreType.DMA((2, 3))] * 4,
        ]
        params = dict(collective_id=3, has_side_effects=True)
    vmem = pl.BlockSpec(memory_space=pltpu.VMEM)
    large = pl.BlockSpec(memory_space=pl.ANY) if paired else vmem
    return pl.pallas_call(
        functools.partial(heads_kernel, atoms, acts, paired),
        in_specs=[vmem, large, vmem, vmem, vmem],
        out_specs=[large, vmem, vmem, vmem],
        out_shape=[
            jax.ShapeDtypeStruct(block if paired else weights.shape, BF16),
            jax.ShapeDtypeStruct(feats.shape, BF16),
            jax.ShapeDtypeStruct((1, slots), F32),
            jax.ShapeDtypeStruct((16, 128), F32),
        ],
        scratch_shapes=scratch,
        compiler_params=pltpu.CompilerParams(vmem_limit_bytes=VMEM_LIMIT, **params),
        name="heads",
    )(feats, weights, bias, per_slot, rows_of_slot[None, :])


def finish_kernel(
    dsum, stat, kern, fn, hn, on, loss, g1, g2, g3t, mean_g, spread_g, bias_g, val_g, val_s, adv_g, adv_s, out_g
):
    feat, atoms, outs = fn.shape[1], val_g.shape[1], on.shape[1]
    inverse = 1.0 / stat[9:10, 0:1]
    loss[...] = stat[8:9, 0:1] * inverse
    v = kern[...]
    turned = pltpu.roll(v, 64, 1)
    g2[0:32, :] = v[0:32, 0:64]
    g2[32:64, :] = turned[0:32, 0:64]
    third = jnp.concatenate([v[32:64], turned[32:64], v[64:72], jnp.zeros((56, 128), F32)], axis=0)
    g3t[...] = jnp.transpose(third)[0:64, 0:72]
    for k in range(4):
        g1[8 * k : 8 * k + 8, :] = v[72:80, 32 * k : 32 * k + 32]
    for h in range(2):
        mean = dsum[h, :, 0:feat] * inverse
        mean_g[h] = mean
        spread_g[h] = mean * fn[h : h + 1, :] * as_column(hn[0, h : h + 1, :])
        bias_g[h : h + 1, :] = as_row(dsum[h, :, feat : feat + 1] * inverse)
    out = jnp.concatenate([dsum[0, :, 3200:], dsum[1, :, 3200:]], axis=1) * inverse
    val, adv = out[:, :atoms], out[:, atoms:outs]
    val_g[...] = val
    val_s[...] = val * as_column(hn[1, 0:1, :]) * on[:, :atoms]
    adv_g[...] = adv
    adv_s[...] = adv * as_column(hn[1, 1:2, :]) * on[:, atoms:]
    out_g[...] = jnp.concatenate([stat[k : k + 1, :] for k in range(8)], axis=1)[:, :outs] * inverse


def outputs(dsum, stat, kern, fn, hn, on, atoms):
    feat, outs = fn.shape[1], on.shape[1]
    shapes = [(1, 1), (32, 32), (64, 64), (64, 72), (2, 16, feat), (2, 16, feat), (2, 16)]
    shapes += [(16, atoms)] * 2 + [(16, outs - atoms)] * 2 + [(1, outs)]
    return pl.pallas_call(
        finish_kernel,
        out_shape=[jax.ShapeDtypeStruct(s, F32) for s in shapes],
        compiler_params=pltpu.CompilerParams(vmem_limit_bytes=VMEM_LIMIT),
        name="outputs",
    )(dsum, stat, kern, fn, hn, on)


def exchange_kernel(count, kern_ref, slot_ref, kerns_out, slots_out, send_kern, recv_kern, send_slot, recv_slot, own):
    me = lax.axis_index("dp")
    peers = [lax.rem(me + k, count) for k in range(count)]
    barrier = pltpu.get_barrier_semaphore()
    for k in range(1, count):
        pl.semaphore_signal(barrier, inc=1, device_id={"dp": peers[k]}, device_id_type=pl.DeviceIdType.MESH)
    pl.semaphore_wait(barrier, count - 1)
    mine = [
        pltpu.make_async_copy(kern_ref, kerns_out.at[me], own.at[0]),
        pltpu.make_async_copy(slot_ref.at[me], slots_out.at[me], own.at[1]),
    ]
    sent = []
    for k in range(1, count):
        to = dict(device_id={"dp": peers[k]}, device_id_type=pl.DeviceIdType.MESH)
        sent.append(pltpu.make_async_remote_copy(kern_ref, kerns_out.at[me], send_kern.at[k], recv_kern.at[k], **to))
        sent.append(pltpu.make_async_remote_copy(slot_ref.at[peers[k]], slots_out.at[me], send_slot.at[k], recv_slot.at[k], **to))
    for copy in mine + sent:
        copy.start()
    for copy in mine + sent:
        copy.wait()


def exchange(kern, slot):
    count = slot.shape[0]
    return pl.pallas_call(
        functools.partial(exchange_kernel, count),
        in_specs=[pl.BlockSpec(memory_space=pltpu.VMEM)] * 2,
        out_specs=[pl.BlockSpec(memory_space=pltpu.VMEM)] * 2,
        out_shape=[jax.ShapeDtypeStruct((count, *kern.shape), kern.dtype), jax.ShapeDtypeStruct(slot.shape, slot.dtype)],
        scratch_shapes=[pltpu.SemaphoreType.DMA((count,))] * 4 + [pltpu.SemaphoreType.DMA((2,))],
        compiler_params=pltpu.CompilerParams(collective_id=2, has_side_effects=True, vmem_limit_bytes=VMEM_LIMIT),
        name="exchange",
    )(kern, slot)


def on_device(
    frames,
    send_rows,
    recv_counts,
    actions,
    target_dist,
    sample_weight,
    conv_first,
    conv_second,
    conv_third,
    hidden_mean,
    hidden_spread,
    hidden_bias,
    feature_noise,
    hidden_noise,
    value_mean,
    value_spread,
    advantage_mean,
    advantage_spread,
    output_noise,
    output_bias,
):
    dp_count = lax.axis_size("dp")
    slots = send_rows.shape[0]
    capacity = slots // dp_count
    atoms = value_mean.shape[1]
    acts = advantage_mean.shape[1] // atoms
    rows = frames.shape[0]
    feat, own = hidden_mean.shape[1:]
    outs = atoms * (acts + 1)

    x = frames.transpose(1, 0, 2).reshape(21, 4, rows, 336)
    bias = output_bias[None, :]
    mean_t = hidden_mean.transpose(0, 2, 1)
    spread_t = hidden_spread.transpose(0, 2, 1)

    if (dp_count, lax.axis_size("mp"), own, slots) == (8, 4, 16, 512):
        noise = output_noise[None, :]
        shared = [mean_t, spread_t, hidden_bias, feature_noise, hidden_noise]
        shared += [value_mean, value_spread, advantage_mean, advantage_spread, noise]
        shared += [target_dist.T, recv_counts[None, :], actions[None, :], sample_weight[None, :]]
        kernels = [conv_first, conv_second, conv_third.T]
        a1, s1, a2, s2, feats, s3, y, y0, weights, per_slot, kern2, kern3 = torso_forward(x, kernels, shared)
        weights, per_slot = weights.reshape(2, 512, HALF), per_slot.reshape(slots, 128)
        dweights, feat_grad, prio, stat = heads(atoms, acts, feats, weights, bias, per_slot, send_rows, paired=True)
        summed = [dweights, stat]
        summed = torso_backward(y, y0, a1, s1, a2, s2, s3, feat_grad, kern2, kern3, summed=summed)
        loss, g1, g2, g3t, mean_g, spread_g, bias_g, *outer, out_g = outputs(
            *summed, feature_noise, hidden_noise, noise, atoms
        )
        return (
            loss[0, 0],
            g1,
            g2,
            g3t.T,
            mean_g.transpose(0, 2, 1),
            spread_g.transpose(0, 2, 1),
            bias_g,
            *outer,
            out_g[0],
            prio[0],
        )

    sizes = [w.size for w in (conv_first, conv_second, conv_third)]
    flat = jnp.concatenate([w.astype(BF16).reshape(-1) for w in (conv_first, conv_second, conv_third)])
    tall = -(-flat.size // 2048) * 16
    flat = jnp.pad(flat, (0, tall * 128 - flat.size)).reshape(tall, 128)
    is_valid = jnp.arange(capacity, dtype=jnp.int32)[None, :] < recv_counts[:, None]
    is_valid = is_valid.astype(F32).reshape(slots)
    per_slot = jnp.stack([is_valid * sample_weight, is_valid, actions.astype(F32)], axis=1)
    per_slot = jnp.concatenate([target_dist, per_slot, jnp.zeros((slots, 125 - atoms), F32)], axis=1)
    flat, per_slot = exchange(flat, per_slot.reshape(dp_count, capacity, 128))
    per_slot = per_slot.reshape(slots, 128)
    flat = flat.reshape(dp_count, -1)
    kern1 = jnp.tile(flat[:, : sizes[0]].reshape(-1, 32), (1, 4))
    kern2 = jnp.tile(flat[:, sizes[0] : sizes[0] + sizes[1]].reshape(-1, 64), (1, 2))
    kern3 = jnp.tile(flat[:, sizes[0] + sizes[1] : sum(sizes)].reshape(-1, 64), (1, 2))

    wide_one = mean_t + spread_t * feature_noise[:, None, :] * hidden_noise[0][:, :, None]
    wide_one = jnp.concatenate([wide_one, hidden_bias[:, :, None], jnp.zeros((2, own, 63), F32)], axis=2)
    wide_val = value_mean + value_spread * hidden_noise[1, 0][:, None] * output_noise[None, :atoms]
    wide_adv = advantage_mean + advantage_spread * hidden_noise[1, 1][:, None] * output_noise[None, atoms:]
    wide_out = jnp.concatenate([wide_val, wide_adv, jnp.zeros((own, 1024 - outs), F32)], axis=1)
    wide_out = wide_out.reshape(own, 2, 512).transpose(1, 0, 2)
    shard = jnp.concatenate([wide_one, wide_out], axis=2).astype(BF16)
    weights = lax.all_gather(shard, ("mp", "dp"), axis=1, tiled=True)

    a1, s1, a2, s2, feats, s3, y, y0 = torso_forward(x, [kern1, kern2, kern3])
    dweights, feat_grad, prio, stat = heads(atoms, acts, feats, weights, bias, per_slot, send_rows)
    dshard = lax.psum_scatter(dweights, ("mp", "dp"), scatter_dimension=1, tiled=True).astype(F32)
    stat = lax.psum(stat, ("dp", "mp"))
    inverse = 1.0 / stat[9, 0]
    k1, k2, k3 = torso_backward(y, y0, a1, s1, a2, s2, s3, feat_grad, kern2, kern3)
    kflat = jnp.concatenate([g.reshape(dp_count, -1) for g in (k1[:, :32], k2[:, :64], k3[:, :64])], axis=1)
    kflat = lax.psum(lax.psum_scatter(kflat, "dp", scatter_dimension=0, tiled=True)[0], "mp") * inverse
    conv_grads = (
        kflat[: sizes[0]].reshape(conv_first.shape),
        kflat[sizes[0] : sizes[0] + sizes[1]].reshape(conv_second.shape),
        kflat[sizes[0] + sizes[1] :].reshape(conv_third.shape),
    )
    dshard = dshard * inverse
    mean_grad_t = dshard[:, :, :feat]
    spread_grad_t = mean_grad_t * feature_noise[:, None, :] * hidden_noise[0][:, :, None]
    out_grad = dshard[:, :, 3200:].transpose(1, 0, 2).reshape(own, 1024)
    value_mean_grad = out_grad[:, :atoms]
    adv_mean_grad = out_grad[:, atoms:outs]
    return (
        stat[8, 0] * inverse,
        *conv_grads,
        mean_grad_t.transpose(0, 2, 1),
        spread_grad_t.transpose(0, 2, 1),
        dshard[:, :, feat],
        value_mean_grad,
        value_mean_grad * hidden_noise[1, 0][:, None] * output_noise[None, :atoms],
        adv_mean_grad,
        adv_mean_grad * hidden_noise[1, 1][:, None] * output_noise[None, atoms:],
        stat[:8].reshape(-1)[:outs] * inverse,
        prio[0],
    )


def solution(mesh):
    both, heads_dim = P(("dp", "mp")), P(("mp", "dp"), None)
    return jax.shard_map(
        on_device,
        mesh=mesh,
        in_specs=(
            P(("dp", "mp"), None, None),
            both,
            both,
            both,
            P(("dp", "mp"), None),
            both,
            P("dp", None),
            P("dp", None),
            P("dp", None),
            P(None, None, ("mp", "dp")),
            P(None, None, ("mp", "dp")),
            P(None, ("mp", "dp")),
            P(),
            P(None, None, ("mp", "dp")),
            heads_dim,
            heads_dim,
            heads_dim,
            heads_dim,
            P(),
            P(),
        ),
        out_specs=(
            P(),
            P("dp", None),
            P("dp", None),
            P("dp", None),
            P(None, None, ("mp", "dp")),
            P(None, None, ("mp", "dp")),
            P(None, ("mp", "dp")),
            heads_dim,
            heads_dim,
            heads_dim,
            heads_dim,
            P(),
            both,
        ),
        check_vma=False,
    )
```

```python
import functools

import jax
import jax.numpy as jnp
from jax import lax
from jax.experimental import pallas as pl
from jax.experimental.pallas import tpu as pltpu
from jax.sharding import PartitionSpec as P

F32 = jnp.float32
BF16 = jnp.bfloat16
VMEM_LIMIT = 60 * 1024 * 1024


def sigmoid(v):
    return 0.5 * jnp.tanh(0.5 * v) + 0.5


def silu_and_slope(v):
    s = sigmoid(v)
    a = v * s
    return a, s + a * (1.0 - s)


def dot(a, b):
    return lax.dot_general(a, b, (((1,), (0,)), ((), ())), preferred_element_type=F32)


def dot_nt(a, b):
    return lax.dot_general(a, b, (((1,), (1,)), ((), ())), preferred_element_type=F32)


def dot_tn(a, b):
    return lax.dot_general(a, b, (((0,), (0,)), ((), ())), preferred_element_type=F32)


def columns_of_one():
    return [7 * (g // 8) + g % 8 if g % 8 < 7 and 7 * (g // 8) + g % 8 < 20 else -9 for g in range(24)]


def half_lanes(left, right, rows):
    lane = lax.broadcasted_iota(jnp.int32, (rows, 128), 1)
    zero = jnp.zeros((rows, 128), F32)
    return jnp.where(lane < 64, zero if left is None else left, zero if right is None else right)


def fill_band_one(k1_ref, band):
    lane = lax.broadcasted_iota(jnp.int32, (16, 128), 1) // 32
    for u in range(8):
        taps = [k1_ref[((u // 4) * 2 + v) * 64 + (u % 4) * 16 :][:16].astype(F32) for v in range(2)]
        for g in range(8):
            for h in range(2):
                col = lane + 4 * h
                here = jnp.where((col == g) & (col < 7), taps[0], 0.0) + jnp.where((col == g - 1) & (col < 7), taps[1], 0.0)
                band[128 * u + 16 * g : 128 * u + 16 * g + 16, 128 * h : 128 * h + 128] = here.astype(BF16)


def fill_band_two(k2_ref, band):
    cols = columns_of_one()
    for u in range(4):

        def tap(v):
            at = ((u // 2) * 2 + v // 2) * 128 + ((u % 2) * 2 + v % 2) * 32
            return k2_ref[at : at + 32, :].astype(F32)

        for g, q in enumerate(cols):
            if q < 0:
                continue
            used = {(q - v) // 2: v for v in (q % 2, q % 2 + 2) if 0 <= (q - v) // 2 < 9}
            for m in sorted({c // 2 for c in used}):
                sides = [tap(used[2 * m + side]) if 2 * m + side in used else None for side in range(2)]
                band[u, 32 * g : 32 * g + 32, 128 * m : 128 * m + 128] = half_lanes(*sides, 32).astype(BF16)


def fill_band_three(k3_ref, band):
    for u in range(3):

        def tap(v):
            return k3_ref[(u * 3 + v) * 64 : (u * 3 + v) * 64 + 64, :].astype(F32)

        for q in range(9):
            used = {q - v: v for v in range(3) if 0 <= q - v < 7}
            for m in sorted({c // 2 for c in used}):
                sides = [tap(used[2 * m + side]) if 2 * m + side in used else None for side in range(2)]
                band[u, 64 * q : 64 * q + 64, 128 * m : 128 * m + 128] = half_lanes(*sides, 64).astype(BF16)


def fold_lanes(v, width):
    step = 64
    while step >= width:
        v = v + pltpu.roll(v, step, 1)
        step //= 2
    return v


def take_band_one(d1, out):
    lane = lax.broadcasted_iota(jnp.int32, (16, 128), 1) // 32
    for u in range(8):
        for v in range(2):
            total = jnp.zeros((16, 128), F32)
            for col in range(7):
                at = 128 * u + 16 * (col + v)
                h = col // 4
                total = total + jnp.where(lane + 4 * h == col, d1[at : at + 16, 128 * h : 128 * h + 128], 0.0)
            at = ((u // 4) * 2 + v) * 64 + (u % 4) * 16
            out[at : at + 16, :] = total
    out[...] = fold_lanes(out[...], 32)


def take_band_two(blocks, out):
    cols = columns_of_one()
    lane = lax.broadcasted_iota(jnp.int32, (32, 128), 1)
    for u in range(4):
        for v in range(4):
            total = jnp.zeros((32, 128), F32)
            for ref, first, c0, count in blocks:
                for c in range(count):
                    at = 32 * (cols.index(2 * (c0 + c) + v) - first)
                    piece = ref[u, at : at + 32, 128 * (c // 2) : 128 * (c // 2) + 128]
                    total = total + jnp.where((lane < 64) == (c % 2 == 0), piece, 0.0)
            at = ((u // 2) * 2 + v // 2) * 128 + ((u % 2) * 2 + v % 2) * 32
            out[at : at + 32, :] = total
    out[...] = fold_lanes(out[...], 64)


def take_band_three(d3, out):
    lane = lax.broadcasted_iota(jnp.int32, (64, 128), 1)
    for u in range(3):
        for v in range(3):
            total = jnp.zeros((64, 128), F32)
            for c in range(4):
                piece = d3[u, 64 * (c + v) : 64 * (c + v) + 64, 128 * (c // 2) : 128 * (c // 2) + 128]
                total = total + jnp.where((lane < 64) == (c % 2 == 0), piece, 0.0)
            at = (u * 3 + v) * 64
            out[at : at + 64, :] = total
    out[...] = fold_lanes(out[...], 64)


def coordinates():
    d, m = lax.axis_index("dp"), lax.axis_index("mp")
    return {"z": d // 2, "y": d % 2, "x": m // 2, "c": m % 2}


def device_at(at):
    return dict(
        device_id={"dp": at["z"] * 2 + at["y"], "mp": at["x"] * 2 + at["c"]}, device_id_type=pl.DeviceIdType.MESH
    )


AXES = {"x": 2, "z": 4, "y": 2}
HALF = 3712
CUTS = [(0, 1408, "zyx", "zxy"), (1408, 2816, "zyx", "zxy"), (2816, HALF, "xyz", "yxz")]
GATHER_FLOWS = [(half, lo, hi, orders[half]) for lo, hi, *orders in CUTS for half in range(2)]
SUM_FLOWS = [(half, lo, hi, order[::-1]) for half, lo, hi, order in GATHER_FLOWS]
GATHER_FIRST = [(4, 0), (5, 0), (0, 0)]
GATHER_PLAN = {(0, 0): [(4, 1), (5, 1), (1, 0), (0, 1)], (0, 1): [(2, 0)], (0, 3): [(1, 1)], (1, 0): [(3, 0)], (1, 3): [(2, 1), (0, 2)], (1, 5): [(4, 2)], (2, 1): [(1, 2)], (3, 0): [(3, 1)], (3, 4): [(5, 2)], (3, 5): [(2, 2)], (4, 1): [(3, 2)]}
GATHER_LAST = []
GATHER_DONE = [0, 4, 1, 2, 5, 3]
SUM_FIRST = [(0, 0), (1, 0), (4, 0)]
SUM_PLAN = {(0, 2): [(2, 0), (3, 0)], (0, 4): [(5, 0)], (1, 4): [(0, 1), (1, 1)], (2, 0): [(2, 1), (3, 1)], (2, 4): [(0, 2)], (2, 5): [(4, 1), (5, 1)], (2, 6): [(1, 2)], (3, 2): [(4, 2), (5, 2)], (3, 5): [(2, 2)], (4, 2): [(3, 2)]}
SUM_LAST = []
SUM_DONE = [0, 4, 5, 1, 2, 3]

def flow_buffers(flows):
    shapes = []
    for _, lo, hi, order in flows:
        for s, axis in enumerate(order):
            rest = [AXES[a] for a in AXES if a in order[s + 1 :]]
            shapes.append((AXES[axis] - 1, *rest, 16, hi - lo))
    return shapes


def peers_of(axis):
    me = coordinates()
    n = AXES[axis]
    return [{**me, axis: lax.rem(me[axis] + k, n)} for k in range(1, n)]


def block_of(ref, half, lo, hi, at):
    return ref.at[(half, *[at.get(a, slice(None)) for a in AXES], slice(None), slice(lo, hi))]


def sum_copies(acc, flow, stage, buf, send, recv):
    half, lo, hi, order = flow
    me = coordinates()
    held = {a: me[a] for a in order[:stage]}
    copies = []
    for k, peer in enumerate(peers_of(order[stage])):
        src = block_of(acc, half, lo, hi, {**held, order[stage]: peer[order[stage]]})
        copies.append(pltpu.make_async_remote_copy(src, buf.at[k], send.at[k], recv.at[k], **device_at(peer)))
    return copies


def add_arrived(acc, flow, stage, buf, out=None):
    half, lo, hi, order = flow
    me = coordinates()
    own = block_of(acc, half, lo, hi, {a: me[a] for a in order[: stage + 1]})
    if out is None and AXES[order[stage]] == 2:
        own[...] = own[...] + buf[0]
        return
    total = own[...].astype(F32)
    for k in range(AXES[order[stage]] - 1):
        total = total + buf[k].astype(F32)
    if out is None:
        own[...] = total.astype(BF16)
    else:
        out[half, :, lo:hi] = total


def everyone(axis, count):
    me = lax.axis_index(axis)
    return [dict(device_id={axis: lax.rem(me + k, count)}, device_id_type=pl.DeviceIdType.MESH) for k in range(1, count)]


def share(axis, count, src, buf, send, recv):
    me = lax.axis_index(axis)
    return [
        pltpu.make_async_remote_copy(src(k), buf.at[me], send.at[k], recv.at[k], **to)
        for k, to in enumerate(everyone(axis, count))
    ]


def in_order(buf, count):
    total = buf[0].astype(F32)
    for k in range(1, count):
        total = total + buf[k].astype(F32)
    return total


def gathered_block(ref, half, lo, hi, core, at):
    x, z, y = (at.get(a, slice(None)) for a in AXES)
    return ref.at[half, x, core, z, y, :, lo:hi]


def gather_copies(shard, out, flow, stage, send, recv):
    half, lo, hi, order = flow
    me = coordinates()
    at = {a: me[a] for a in order[stage:]}
    dst = gathered_block(out, half, lo, hi, me["c"], at)
    src = shard.at[half, :, lo:hi] if stage == 0 else dst
    return [
        pltpu.make_async_remote_copy(src, dst, send.at[k], recv.at[k], **device_at(peer))
        for k, peer in enumerate(peers_of(order[stage]))
    ]


def core_copies(out, flow, last, send, recv):
    half, lo, hi, order = flow
    me = coordinates()
    other = {**me, "c": 1 - me["c"]}
    copies = []
    for k, at in enumerate([peer[order[2]] for peer in peers_of(order[2])] if last else [me[order[2]]]):
        block = gathered_block(out, half, lo, hi, me["c"], {order[2]: at})
        copies.append(pltpu.make_async_remote_copy(block, block, send.at[k], recv.at[k], **device_at(other)))
    return copies


def start(copies):
    for copy in copies:
        copy.start()


def finish(copies):
    for copy in copies:
        copy.wait()


def greet():
    for to in everyone("dp", 8) + everyone("mp", 4):
        pl.semaphore_signal(pltpu.get_barrier_semaphore(), inc=1, **to)


def greeted():
    pl.semaphore_wait(pltpu.get_barrier_semaphore(), 10)


def as_column(row):
    n = row.shape[1]
    eye = lax.broadcasted_iota(jnp.int32, (n, n), 0) == lax.broadcasted_iota(jnp.int32, (n, n), 1)
    return jnp.sum(jnp.where(eye, row, 0.0), axis=1, keepdims=True)


def as_row(column):
    n = column.shape[0]
    eye = lax.broadcasted_iota(jnp.int32, (n, n), 0) == lax.broadcasted_iota(jnp.int32, (n, n), 1)
    return jnp.sum(jnp.where(eye, column, 0.0), axis=0, keepdims=True)


def pack_shards(c1, c2, c3t):
    c3 = jnp.transpose(jnp.concatenate([c3t, jnp.zeros((64, 56), F32)], axis=1))
    blank = jnp.zeros((8, 64), F32)
    return jnp.concatenate(
        [
            jnp.concatenate([c2[0:32], c2[32:64]], axis=1),
            jnp.concatenate([c3[0:32], c3[32:64]], axis=1),
            jnp.concatenate([c3[64:72], blank], axis=1),
            jnp.concatenate([c1[8 * k : 8 * k + 8] for k in range(4)], axis=1),
        ],
        axis=0,
    )


def unpack_shards(d, v, k1, k2, k3):
    lane = lax.broadcasted_iota(jnp.int32, (32, 128), 1)

    def sides(w):
        turned = pltpu.roll(w, 64, 1)
        low = lane[: w.shape[0]] < 64
        return jnp.where(low, w, turned), jnp.where(low, turned, w)

    k2[64 * d : 64 * d + 32, :], k2[64 * d + 32 : 64 * d + 64, :] = sides(v[0:32])
    k3[72 * d : 72 * d + 32, :], k3[72 * d + 32 : 72 * d + 64, :] = sides(v[32:64])
    k3[72 * d + 64 : 72 * d + 72, :] = sides(v[64:72])[0]
    for k in range(4):
        part = jnp.where(lane[:8] // 32 == k, v[72:80], 0.0)
        k1[32 * d + 8 * k : 32 * d + 8 * k + 8, :] = fold_lanes(part, 32)


def noisy_weights(shard, hm, hs, hb, fn, hn, vm, vs, am, adv_s, on):
    atoms, outs = vm.shape[1], on.shape[1]
    lane = lax.broadcasted_iota(jnp.int32, (16, 128), 1)
    for h in range(2):
        wide = hm[h] + hs[h] * fn[h : h + 1, :] * as_column(hn[0, h : h + 1, :])
        shard[h, :, 0:3072] = wide[:, 0:3072].astype(BF16)
        last = jnp.concatenate([wide[:, 3072:], jnp.zeros((16, 64), F32)], axis=1)
        last = jnp.where(lane == 64, as_column(hb[h : h + 1, :]), last)
        shard[h, :, 3072:3200] = last.astype(BF16)
    val = vm[...] + vs[...] * as_column(hn[1, 0:1, :]) * on[:, :atoms]
    adv = am[...] + adv_s[...] * as_column(hn[1, 1:2, :]) * on[:, atoms:]
    out = jnp.concatenate([val, adv, jnp.zeros((16, 1024 - outs), F32)], axis=1).astype(BF16)
    shard[0, :, 3200:] = out[:, :512]
    shard[1, :, 3200:] = out[:, 512:]


def slot_rows(staged, tt, cnt, act, sw):
    atoms, slots = tt.shape
    lane = lax.broadcasted_iota(jnp.int32, (8, slots), 1)
    source = lax.broadcasted_iota(jnp.int32, (8, slots), 0)
    cap = slots // 8
    used = jnp.sum(jnp.where(lane // cap == source, as_column(cnt[...].astype(F32)), 0.0), axis=0, keepdims=True)
    valid = jnp.where((lane[0:1] % cap).astype(F32) < used, 1.0, 0.0)
    staged[...] = jnp.zeros_like(staged)
    staged[0:atoms, :] = tt[...]
    staged[atoms : atoms + 1, :] = valid * sw[...]
    staged[atoms + 1 : atoms + 2, :] = valid
    staged[atoms + 2 : atoms + 3, :] = act[...].astype(F32)
    return jnp.transpose(staged[...])


def shifted_blocks(x):
    rows = x.shape[0]
    return (
        x[:, 0:128],
        x[:, 112:240],
        jnp.concatenate([x[:, 224:336], jnp.zeros((rows, 16), x.dtype)], axis=1),
    )


def forward_kernel(shared, *refs):
    if shared:
        ins, refs = refs[:17], refs[17:]
        (x_in, c1, c2, c3t, hm, hs, hb, fn, hn, vm, vs, am, adv_s, on, tt, cnt, act), refs = ins, refs
        (sw,), refs = refs[:1], refs[1:]
    else:
        (x_in, k1_ref, k2_ref, k3_ref), refs = refs[:4], refs[4:]
    (a1_out, s1_out, *whole_out, y_out, y0_ref), refs = refs[:8], refs[8:]
    if shared:
        (w_out, slot_out, k2_ref, k3_ref), refs = refs[:4], refs[4:]
    (carry, a1s, b1_ref, b2_ref, b3_ref, *whole, whole_sem, slopes_one, shifted, step_sem, x_first, x_slots, x_sem), refs = refs[:16], refs[16:]
    a2_ref, s2_ref, f_ref, s3_ref = whole
    i = pl.program_id(0)
    rows = x_first.shape[1]
    x_ref = x_slots.at[lax.rem(i, 2)]
    s1_ref, y_ref = slopes_one.at[lax.rem(i, 2)], shifted.at[lax.rem(i, 2)]

    def step_copies(step):
        slot, two = lax.rem(step, 2), pl.ds(2 * step, 2)
        return [
            pltpu.make_async_copy(a1s.at[two], a1_out.at[two], step_sem.at[slot, 0]),
            pltpu.make_async_copy(slopes_one.at[slot], s1_out.at[two], step_sem.at[slot, 1]),
            pltpu.make_async_copy(shifted.at[slot], y_out.at[pl.ds(4 * step, 4)], step_sem.at[slot, 2]),
        ]

    def frame_copy(step):
        slot = lax.rem(step, 2)
        return pltpu.make_async_copy(x_in.at[pl.ds(4 * step + 1, 4)], x_slots.at[slot], x_sem.at[slot])

    first_frames = pltpu.make_async_copy(x_in.at[0], x_first, x_sem.at[2])

    @pl.when(i == 0)
    def _():
        start([first_frames, frame_copy(i)])

    @pl.when(i >= 2)
    def _():
        finish(step_copies(i - 2))

    if shared:
        k1_ref, shard, kern_own, kern_buf, staged, slot_src, slot_buf, kern_s, kern_r, slot_s, slot_r, own_sem, sems, core_sems = refs
        flow_stage = {
            (f, s): (shard, w_out, flow, s, sems.at[0, f, s], sems.at[1, f, s])
            for f, flow in enumerate(GATHER_FLOWS)
            for s in range(3)
        }

        def kern_copies():
            return share("dp", 8, lambda _: kern_own, kern_buf, kern_s, kern_r)

        def slot_copies():
            ids = [lax.rem(lax.axis_index("dp") + j, 8) for j in range(1, 8)]
            return share("dp", 8, lambda j: slot_src.at[ids[j]], slot_buf, slot_s, slot_r)

        def own_copies():
            me = coordinates()
            return [
                pltpu.make_async_copy(shard.at[h], w_out.at[h, me["x"], me["c"], me["z"], me["y"]], own_sem.at[h])
                for h in range(2)
            ]

        def to_core(f, last):
            return core_copies(w_out, GATHER_FLOWS[f], last, core_sems.at[0, f, last], core_sems.at[1, f, last])

        def begin():
            greet()
            kern_own[...] = pack_shards(c1[...], c2[...], c3t[...]).astype(BF16)
            kern_buf[lax.axis_index("dp")] = kern_own[...]
            noisy_weights(shard, hm, hs, hb, fn, hn, vm, vs, am, adv_s, on)
            packed = slot_rows(staged, tt, cnt, act, sw).reshape(8, 2, 32, 128)
            lane = lax.broadcasted_iota(jnp.int32, (8, 32, 128), 2)
            slot_src[...] = jnp.where(lane < 64, packed[:, 0], pltpu.roll(packed[:, 1].reshape(256, 128), 64, 1).reshape(8, 32, 128))
            slot_buf[lax.axis_index("dp")] = slot_src[lax.axis_index("dp")]
            greeted()
            start(kern_copies())
            for f, s in GATHER_FIRST:
                enter(f, s)
            start(own_copies())
            prepare()
            finish(own_copies())
            finish(kern_copies())
            for d in range(8):
                unpack_shards(d, kern_buf[d].astype(F32), k1_ref, k2_ref, k3_ref)

        def enter(f, s):
            if s > 0:
                finish(gather_copies(*flow_stage[f, s - 1]))
            start(gather_copies(*flow_stage[f, s]))
            if s == 2:
                start(to_core(f, 0))

        def point(step, k):
            for (at, where), entries in GATHER_PLAN.items():
                if where == k:

                    @pl.when(step == at)
                    def _():
                        for f, s in entries:
                            enter(f, s)

            if k == 0:

                @pl.when(step == 4)
                def _():
                    start(slot_copies())

        def end():
            for f, s in GATHER_LAST:
                enter(f, s)
            for f in GATHER_DONE:
                finish(gather_copies(*flow_stage[f, 2]))
                start(to_core(f, 1))
            finish(slot_copies())
            slot_out[:, 0:32] = slot_buf[...]
            slot_out[:, 32:64] = pltpu.roll(slot_buf[...].reshape(256, 128), 64, 1).reshape(8, 32, 128)
            for f in GATHER_DONE:
                for last in range(2):
                    finish(to_core(f, last))

    def prepare():
        b2_ref[...] = jnp.zeros_like(b2_ref)
        b3_ref[...] = jnp.zeros_like(b3_ref)
        finish([first_frames])
        for r in range(4):
            for j, blk in enumerate(shifted_blocks(x_first[r])):
                carry[j, :, 128 * r : 128 * r + 128] = blk
        y0_ref[...] = carry[...]

    @pl.when(i == 0)
    def _():
        if shared:
            begin()
        else:
            prepare()
        fill_band_one(k1_ref, b1_ref)
        fill_band_two(k2_ref, b2_ref)
        fill_band_three(k3_ref, b3_ref)

    finish([frame_copy(i)])

    @pl.when(i < 4)
    def _():
        start([frame_copy(i + 1)])

    for pp in range(4):
        for r in range(4):
            for j, blk in enumerate(shifted_blocks(x_ref[pp, r])):
                y_ref[pp, j, :, 128 * r : 128 * r + 128] = blk
        for j in range(3):
            lhs = jnp.concatenate([carry[j] if pp == 0 else y_ref[pp - 1, j], y_ref[pp, j]], axis=1)
            act, slope = silu_and_slope(dot(lhs, b1_ref[...]))
            act = act.astype(BF16)
            a1s[2 * i + pp // 2, pp % 2, :, 256 * j : 256 * j + 256] = act
            s1_ref[pp // 2, pp % 2, :, 256 * j : 256 * j + 256] = slope.astype(BF16)
        if shared:
            point(i, pp)
    carry[...] = y_ref[3]
    start(step_copies(i))

    def second(p):
        for lo, hi, n0, n1 in ((0, 384, 0, 256), (256, 640, 256, 512), (512, 768, 512, 640)):
            lhs = jnp.concatenate([a1s[p + u // 2, u % 2, :, lo:hi] for u in range(4)], axis=1)
            rhs = jnp.concatenate([b2_ref[u, lo:hi, n0:n1] for u in range(4)], axis=0)
            act, slope = silu_and_slope(dot(lhs, rhs))
            act = act.astype(BF16)
            a2_ref[p, :, n0:n1] = act
            s2_ref[p, :, n0:n1] = slope.astype(BF16)

    def third(p, odd):
        acts, slopes = [], []
        for lo, hi, n0, n1 in ((0, 384, 0, 256), (256, 640, 256, 512)):
            lhs = jnp.concatenate([a2_ref[p + u, :, lo:hi] for u in range(3)], axis=1)
            rhs = jnp.concatenate([b3_ref[u, lo:hi, n0:n1] for u in range(3)], axis=0)
            act, slope = silu_and_slope(dot(lhs, rhs))
            acts.append(act)
            slopes.append(slope)
        lane = lax.broadcasted_iota(jnp.int32, (rows, 512), 1)
        base = (p // 2) * 896
        for out, parts in ((f_ref, acts), (s3_ref, slopes)):
            whole = jnp.where(lane < 448, jnp.concatenate(parts, axis=1), 0.0)
            if not odd:
                out[:, pl.ds(pl.multiple_of(base, 128), 512)] = whole.astype(BF16)
            else:
                whole = pltpu.roll(whole, 64, 1)
                at = pl.ds(pl.multiple_of(base + 384, 128), 128)
                out[:, at] = (out[:, at].astype(F32) + whole[:, :128]).astype(BF16)
                out[:, pl.ds(pl.multiple_of(base + 512, 128), 384)] = whole[:, 128:].astype(BF16)

    @pl.when(i >= 1)
    def _():
        second(2 * i - 1)

    if shared:
        point(i, 4)
    second(2 * i)
    if shared:
        point(i, 5)

    @pl.when(i >= 2)
    def _():
        third(2 * i - 3, True)

    if shared:
        point(i, 6)

    @pl.when(i >= 1)
    def _():
        third(2 * i - 2, False)

    @pl.when(i == 4)
    def _():
        lane = lax.broadcasted_iota(jnp.int32, (rows, 128), 1)
        last = f_ref[:, 3072:3200].astype(F32)
        f_ref[:, 3072:3200] = jnp.where(lane == 64, 1.0, last).astype(BF16)
        leaving = [pltpu.make_async_copy(whole[k], whole_out[k], whole_sem.at[k]) for k in range(4)]
        start(leaving)
        if shared:
            end()
        finish(leaving)
        for step in (i - 1, i):
            finish(step_copies(step))


def full(shape):
    return pl.BlockSpec(shape, lambda *_: (0,) * len(shape))


def once(shape):
    return pl.BlockSpec(shape, lambda *_: (0,) * len(shape), pipeline_mode=pl.Buffered(1))


BANDS = [(1024, 256), (4, 768, 640), (3, 640, 512)]


def torso_forward(x, kernels, shared=None):
    rows = x.shape[2]
    shapes = [(10, 2, rows, 768)] * 2 + [(9, rows, 640)] * 2 + [(rows, 3200)] * 2 + [(20, 3, rows, 512), (3, rows, 512)]
    args = [x, *kernels]
    out_specs = (
        [pl.BlockSpec(memory_space=pl.ANY)] * 7
        + [once((3, rows, 512))]
    )
    out_shape = [jax.ShapeDtypeStruct(s, BF16) for s in shapes]
    scratch = [
        pltpu.VMEM((3, rows, 512), BF16),
        pltpu.VMEM((10, 2, rows, 768), BF16),
        *[pltpu.VMEM(s, BF16) for s in BANDS],
        *[pltpu.VMEM(s, BF16) for s in shapes[2:6]],
        pltpu.SemaphoreType.DMA((4,)),
        pltpu.VMEM((2, 2, 2, rows, 768), BF16),
        pltpu.VMEM((2, 4, 3, rows, 512), BF16),
        pltpu.SemaphoreType.DMA((2, 3)),
        pltpu.VMEM((4, rows, 336), BF16),
        pltpu.VMEM((2, 4, 4, rows, 336), BF16),
        pltpu.SemaphoreType.DMA((3,)),
    ]
    params = {}
    if shared is not None:
        args += shared
        out_specs += [pl.BlockSpec(memory_space=pl.ANY), once((8, 64, 128)), once((512, 128)), once((576, 128))]
        out_shape += [
            jax.ShapeDtypeStruct((2, 2, 2, 4, 2, 16, HALF), BF16),
            jax.ShapeDtypeStruct((8, 64, 128), F32),
            jax.ShapeDtypeStruct((512, 128), F32),
            jax.ShapeDtypeStruct((576, 128), F32),
        ]
        scratch += [
            pltpu.VMEM((256, 128), F32),
            pltpu.VMEM((2, 16, HALF), BF16),
            pltpu.VMEM((80, 128), BF16),
            pltpu.VMEM((8, 80, 128), BF16),
            pltpu.VMEM((128, 512), F32),
            pltpu.VMEM((8, 32, 128), F32),
            pltpu.VMEM((8, 32, 128), F32),
            *[pltpu.SemaphoreType.DMA((7,))] * 4,
            pltpu.SemaphoreType.DMA((2,)),
            pltpu.SemaphoreType.DMA((2, len(GATHER_FLOWS), 3, 3)),
            pltpu.SemaphoreType.DMA((2, len(GATHER_FLOWS), 2, 3)),
        ]
        params = dict(collective_id=0, has_side_effects=True)
    return pl.pallas_call(
        functools.partial(forward_kernel, shared is not None),
        grid=(5,),
        in_specs=[
            pl.BlockSpec(memory_space=pl.ANY),
            *[once(v.shape) for v in args[1:]],
        ],
        out_specs=out_specs,
        out_shape=out_shape,
        scratch_shapes=scratch,
        compiler_params=pltpu.CompilerParams(vmem_limit_bytes=VMEM_LIMIT, **params),
        name="torso_forward",
    )(*args)


KERNEL_ROWS = [(72, 8, 16), (0, 72, 80)]


def pack_first(d, o1):
    lane = lax.broadcasted_iota(jnp.int32, (8, 128), 1) // 32
    one = jnp.zeros((8, 128), F32)
    for k in range(4):
        one = jnp.where(lane == k, o1[32 * d + 8 * k : 32 * d + 8 * k + 8, :], one)
    return jnp.concatenate([one, jnp.zeros((8, 128), F32)], axis=0)


def pack_others(d, o2, o3):
    lane = lax.broadcasted_iota(jnp.int32, (32, 128), 1)
    two = jnp.where(lane < 64, o2[64 * d : 64 * d + 32, :], o2[64 * d + 32 : 64 * d + 64, :])
    three = jnp.where(lane < 64, o3[72 * d : 72 * d + 32, :], o3[72 * d + 32 : 72 * d + 64, :])
    return jnp.concatenate([two, three, o3[72 * d + 64 : 72 * d + 72, :], jnp.zeros((8, 128), F32)], axis=0)


BACK_LANES = ((0, 256), (128, 512), (384, 640))


def backward_kernel(summed, *refs):
    (*streams, y0_in, a2_in, s2_in, s3_in, fg_in, k2_ref, k3_ref), refs = refs[:10], refs[10:]
    whole_in = (y0_in, a2_in, s2_in, s3_in, fg_in)
    if summed:
        (dw_ref, stat_ref, dsum_ref, stat_out, kern_out), refs = refs[:5], refs[5:]
    (o1_ref, o2_ref, o3_ref), refs = refs[:3], refs[3:]
    (carry, *whole, whole_sem), refs = refs[:6], refs[6:]
    slots, step_sem, refs = refs[:3], refs[3], refs[4:]
    (back, grad, g3, g2, b2_ref, b3_ref, d1_ref, d2a_ref, d2b_ref, d2c_ref, d3_ref), refs = refs[:11], refs[11:]
    a2_ref, s2_ref, s3_ref, fg_ref = whole
    coming = [pltpu.make_async_copy(whole_in[k], (carry, *whole)[k], whole_sem.at[k]) for k in range(5)]
    if summed:
        (acc, stat_dp, stat_mp, load_sem, sems, send_s, recv_s), bufs = refs[:7], refs[7:]
        kern_bufs, bufs = bufs[:6], bufs[6:]
        me = coordinates()
        stages = {}
        at = 0
        for f, flow in enumerate(SUM_FLOWS):
            for s in range(3):
                stages[f, s] = (dw_ref if s == 0 else acc, flow, s, bufs[at], sems.at[0, at], sems.at[1, at])
                at += 1

        loaded = {
            f: pltpu.make_async_copy(
                dw_ref.at[half, :, :, :, :, lo:hi], acc.at[half, :, :, :, :, lo:hi], load_sem.at[f]
            )
            for f, (half, lo, hi, _) in enumerate(SUM_FLOWS)
        }

        def stat_copies(axis, count, k):
            src = stat_ref if k == 0 else stat_mp.at[lax.axis_index("mp")]
            return share(axis, count, lambda _: src, (stat_dp, stat_mp)[k], send_s.at[k], recv_s.at[k])

        def kern_copies(group, k):
            kern_send, kern_dp, kern_mp = kern_bufs[3 * group : 3 * group + 3]
            sem = 2 + 2 * group + k
            if k == 1:
                return share("mp", 4, lambda _: kern_mp.at[lax.axis_index("mp")], kern_mp, send_s.at[sem], recv_s.at[sem])
            ids = [lax.rem(lax.axis_index("dp") + j, 8) for j in range(1, 8)]
            return share("dp", 8, lambda j: kern_send.at[ids[j]], kern_dp, send_s.at[sem], recv_s.at[sem])

        def first():
            start(list(loaded.values()))
            greeted()
            for f, s in SUM_FIRST:
                enter(f, s)
            start(stat_copies("dp", 8, 0))
            stat_dp[lax.axis_index("dp")] = stat_ref[...]

        def stats_over():
            finish(stat_copies("dp", 8, 0))
            stat_mp[lax.axis_index("mp")] = in_order(stat_dp, 8)
            start(stat_copies("mp", 4, 1))

        def enter(f, s):
            if s > 0:
                leave(f, s - 1)
            start(sum_copies(*stages[f, s]))

        def leave(f, s):
            if s == 0:
                finish([loaded[f]])
            finish(sum_copies(*stages[f, s]))
            add_arrived(acc, *stages[f, s][1:4], out=dsum_ref if s == 2 else None)

        def point(step, k):
            for (at, where), entries in SUM_PLAN.items():
                if where == k:

                    @pl.when(step == at)
                    def _():
                        for f, s in entries:
                            enter(f, s)

            extra = [(0, 5, stats_over), (1, 6, stats_done), (4, 3, lambda: kernel_out(1))]
            for at, where, what in extra:
                if where == k:

                    @pl.when(step == at)
                    def _():
                        what()

        def stats_done():
            finish(stat_copies("mp", 4, 1))
            stat_out[...] = in_order(stat_mp, 4)

        def kernel_out(group):
            kern_send, kern_dp, _ = kern_bufs[3 * group : 3 * group + 3]
            if group == 0:
                take_band_one(d1_ref, o1_ref)
            else:
                take_band_two(((d2a_ref, 0, 0, 4), (d2b_ref, 8, 4, 4), (d2c_ref, 16, 8, 1)), o2_ref)
                take_band_three(d3_ref, o3_ref)
            for d in range(8):
                rows_out = pack_first(d, o1_ref) if group == 0 else pack_others(d, o2_ref, o3_ref)
                kern_send[d] = rows_out.astype(BF16)
            kern_dp[lax.axis_index("dp")] = kern_send[lax.axis_index("dp")]
            start(kern_copies(group, 0))

        def kernel_over(group):
            _, kern_dp, kern_mp = kern_bufs[3 * group : 3 * group + 3]
            finish(kern_copies(group, 0))
            kern_mp[lax.axis_index("mp")] = in_order(kern_dp, 8)
            start(kern_copies(group, 1))

        def kernel_done(group):
            at, count, _ = KERNEL_ROWS[group]
            finish(kern_copies(group, 1))
            total = in_order(kern_bufs[3 * group + 2], 4) / stat_out[9:10, :]
            kern_out[at : at + count, :] = total[:count]

    i = pl.program_id(0)
    rows = g3.shape[1]
    y_ref, a1_ref, s1_ref = (slot.at[lax.rem(i, 2)] for slot in slots)

    def step_copies(step):
        return [
            pltpu.make_async_copy(
                streams[k].at[pl.ds(count * step, count)], slots[k].at[lax.rem(step, 2)], step_sem.at[lax.rem(step, 2), k]
            )
            for k, count in enumerate((4, 2, 2))
        ]


    @pl.when(i == 0)
    def _():
        if summed:
            greet()
        start(coming[::-1])
        start(step_copies(i))
        b2_ref[...] = jnp.zeros_like(b2_ref)
        b3_ref[...] = jnp.zeros_like(b3_ref)
        fill_band_two(k2_ref, b2_ref)
        fill_band_three(k3_ref, b3_ref)
        for r in range(2):
            for j, (n0, n1) in enumerate(BACK_LANES):
                for t in range(2):
                    turned = jnp.transpose(b2_ref[2 * t + r, 256 * j : 256 * j + 256, n0:n1].astype(F32))
                    back[j, r, t * (n1 - n0) : (t + 1) * (n1 - n0), :] = turned.astype(BF16)
        grad[3] = jnp.zeros(grad.shape[1:], BF16)
        finish(coming[3:])
        for at in (0, 1, 9, 10):
            g3[at] = jnp.zeros((rows, 512), BF16)
        for at in (0, 10):
            g2[at] = jnp.zeros((rows, 640), BF16)
        lane = lax.broadcasted_iota(jnp.int32, (rows, 512), 1)
        for p in range(7):
            base = (p // 2) * 896 + (384 if p % 2 else 0)
            both = fg_ref[:, base : base + 512].astype(F32) * s3_ref[:, base : base + 512].astype(F32)
            if p % 2:
                both = pltpu.roll(both, 448, 1)
            g3[p + 2] = jnp.where(lane < 448, both, 0.0).astype(BF16)
        if summed:
            first()
            point(i, "a0")
        finish([coming[1]])
        for u in range(3):
            total = 0.0
            for m in range(2):
                lhs = a2_ref[u : u + 7, :, 256 * m : 256 * m + 384].reshape(7 * rows, 384)
                rhs = g3[2:9, :, 256 * m : 256 * m + 256].reshape(7 * rows, 256)
                total = total + dot_tn(lhs, rhs)
            d3_ref[u] = total
            if summed:
                point(i, "a%d" % (1 + u))
        d1_ref[...] = jnp.zeros_like(d1_ref)
        d2a_ref[...] = jnp.zeros_like(d2a_ref)
        d2b_ref[...] = jnp.zeros_like(d2b_ref)
        d2c_ref[...] = jnp.zeros_like(d2c_ref)
        for at, (lo, hi, n0, n1) in enumerate(((0, 256, 0, 256), (256, 512, 128, 512), (512, 640, 384, 512))):
            rhs = jnp.concatenate([b3_ref[u, lo:hi, n0:n1] for u in range(3)], axis=1)
            if at == 0:
                finish([coming[0], coming[2]])
            for p in (0, 3, 6):
                lhs = jnp.concatenate([g3[p + 2 - u : p + 5 - u, :, n0:n1].reshape(3 * rows, n1 - n0) for u in range(3)], axis=1)
                product = dot_nt(lhs, rhs) * s2_ref[p : p + 3, :, lo:hi].reshape(3 * rows, hi - lo).astype(F32)
                g2[p + 1 : p + 4, :, lo:hi] = product.astype(BF16).reshape(3, rows, hi - lo)
            if summed:
                point(i, "a%d" % (4 + at))

    finish(step_copies(i))

    @pl.when(i < 4)
    def _():
        start(step_copies(i + 1))

    for r in range(2):
        for ref, lo, hi, n0, n1 in ((d2a_ref, 0, 384, 0, 256), (d2b_ref, 256, 640, 256, 512), (d2c_ref, 512, 768, 512, 640)):
            lhs = a1_ref[:, r, :, lo:hi].reshape(2 * rows, hi - lo)
            rhs = [g2[pl.ds(2 * i + 1 - t, 2), :, n0:n1].reshape(2 * rows, n1 - n0) for t in range(2)]
            both = dot_tn(lhs, jnp.concatenate(rhs, axis=1))
            for t in range(2):
                ref[2 * t + r] += both[:, t * (n1 - n0) : (t + 1) * (n1 - n0)]
        if summed:
            point(i, 2 * r)
            point(i, 2 * r + 1)

    for j, (n0, n1) in enumerate(BACK_LANES):
        lanes = slice(256 * j, 256 * j + 256)
        before = grad[3, :, lanes]
        for r in range(2):
            lhs = [g2[pl.ds(2 * i + 1 - t, 2), :, n0:n1].reshape(2 * rows, n1 - n0) for t in range(2)]
            product = dot(jnp.concatenate(lhs, axis=1), back[j, r, : 2 * (n1 - n0), :])
            for k in range(2):
                slope = s1_ref[k, r, :, lanes].astype(F32)
                grad[2 * k + r, :, lanes] = (product[k * rows : (k + 1) * rows] * slope).astype(BF16)
        now = [grad[k, :, lanes] for k in range(4)]
        rhs = jnp.concatenate([jnp.concatenate(now, axis=0), jnp.concatenate([before, *now[:3]], axis=0)], axis=1)
        lhs = jnp.concatenate([carry[j], *[y_ref[k, j] for k in range(3)]], axis=0)
        both = dot_tn(lhs, rhs)
        d1_ref[0:512, :] += both[:, 0:256]
        d1_ref[512:1024, :] += both[:, 256:512]
        if summed:
            point(i, 4 + j)
    carry[...] = y_ref[3]

    @pl.when(i == 4)
    def _():
        for j in range(3):
            d1_ref[512:1024, :] += dot_tn(y_ref[3, j], grad[3, :, 256 * j : 256 * j + 256])

    @pl.when(i == 4)
    def _():
        if summed:
            kernel_out(0)
            for f, s in SUM_LAST:
                enter(f, s)
            kernel_over(1)
            kernel_over(0)
            for f in SUM_DONE:
                leave(f, 2)
            kernel_done(1)
            kernel_done(0)
        else:
            take_band_one(d1_ref, o1_ref)
            take_band_two(((d2a_ref, 0, 0, 4), (d2b_ref, 8, 4, 4), (d2c_ref, 16, 8, 1)), o2_ref)
            take_band_three(d3_ref, o3_ref)


def torso_backward(y, y0, a1, s1, a2, s2, s3, fg, kern2, kern3, summed=None):
    rows = y.shape[2]
    sums = [(1024, 256), (4, 384, 256), (4, 384, 256), (4, 256, 128), (3, 384, 256)]
    own = [(256, 128), (512, 128), (576, 128)]
    args = [y, a1, s1, y0, a2, s2, s3, fg, kern2, kern3]
    in_specs = [
        *[pl.BlockSpec(memory_space=pl.ANY)] * 8,
        *[once(v.shape) for v in args[8:]],
    ]
    scratch = [
        *[pltpu.VMEM(v.shape, BF16) for v in args[3:8]],
        pltpu.SemaphoreType.DMA((5,)),
        pltpu.VMEM((2, 4, 3, rows, 512), BF16),
        pltpu.VMEM((2, 2, 2, rows, 768), BF16),
        pltpu.VMEM((2, 2, 2, rows, 768), BF16),
        pltpu.SemaphoreType.DMA((2, 3)),
        pltpu.VMEM((3, 2, 768, 256), BF16),
        pltpu.VMEM((4, rows, 768), BF16),
        pltpu.VMEM((11, rows, 512), BF16),
        pltpu.VMEM((11, rows, 640), BF16),
        *[pltpu.VMEM(s, BF16) for s in BANDS[1:]],
        *[pltpu.VMEM(s, F32) for s in sums],
    ]
    outs = own
    params = {}
    if summed is not None:
        args += summed
        block = (2, *AXES.values(), 16, HALF)
        in_specs += [pl.BlockSpec(memory_space=pl.ANY), once((16, 128))]
        outs = [(2, 16, HALF), (16, 128), (80, 128)]
        buffers = flow_buffers(SUM_FLOWS)
        scratch = [pltpu.VMEM(s, F32) for s in own] + scratch
        scratch += [
            pltpu.VMEM(block, BF16),
            pltpu.VMEM((8, 16, 128), F32),
            pltpu.VMEM((4, 16, 128), F32),
            pltpu.SemaphoreType.DMA((len(SUM_FLOWS),)),
            pltpu.SemaphoreType.DMA((2, len(buffers), 3)),
            pltpu.SemaphoreType.DMA((6, 7)),
            pltpu.SemaphoreType.DMA((6, 7)),
            *[
                pltpu.VMEM((count, padded, 128), kind)
                for _, _, padded in KERNEL_ROWS
                for count, kind in ((8, BF16), (8, BF16), (4, F32))
            ],
            *[pltpu.VMEM(s, BF16) for s in buffers],
        ]
        params = dict(collective_id=1, has_side_effects=True)
    return pl.pallas_call(
        functools.partial(backward_kernel, summed is not None),
        grid=(5,),
        in_specs=in_specs,
        out_specs=[once(s) for s in outs],
        out_shape=[jax.ShapeDtypeStruct(s, F32) for s in outs],
        scratch_shapes=scratch,
        compiler_params=pltpu.CompilerParams(vmem_limit_bytes=VMEM_LIMIT, **params),
        name="torso_backward",
    )(*args)


def high_low(v):
    high = v.astype(BF16)
    return high, (v - high.astype(F32)).astype(BF16)


HEAD_COLUMNS = [(0, 1024), (1024, 2048), (2048, HALF)]


def heads_kernel(atoms, acts, paired, f_ref, w_ref, bias_ref, slot_ref, row_ref, dw_out, fg_ref, prio_ref, stat_ref, *refs):
    if paired:
        dw_ref, arrived, w_hbm, w_ref, summed, dw_hbm = *refs[:2], w_ref, refs[2], refs[3], dw_out
        send, recv, load, save = refs[4:]
        loads = {
            (h, k): pltpu.make_async_copy(w_hbm.at[h, :, lo:hi], w_ref.at[h, :, lo:hi], load.at[h, k])
            for h in range(2)
            for k, (lo, hi) in enumerate(HEAD_COLUMNS)
        }
        start(list(loads.values()))
        me = coordinates()
        other = device_at({**me, "c": 1 - me["c"]})
        barrier = pltpu.get_barrier_semaphore()
        pl.semaphore_signal(barrier, inc=1, **other)

        def to_core(h, k):
            lo, hi = HEAD_COLUMNS[k]
            src = dw_ref.at[h, :, 1 - me["c"], :, :, :, lo:hi]
            return pltpu.make_async_remote_copy(src, arrived.at[h, :, :, :, :, lo:hi], send.at[h, k], recv.at[h, k], **other)

        def saving(h, k):
            lo, hi = HEAD_COLUMNS[k]
            return pltpu.make_async_copy(summed.at[h, :, :, :, :, lo:hi], dw_hbm.at[h, :, :, :, :, lo:hi], save.at[h, k])

        def add_core(h, k):
            lo, hi = HEAD_COLUMNS[k]
            to_core(h, k).wait()

            def one(j, _):
                x, z = j // 4, j % 4
                own = dw_ref[h, x, me["c"], z, :, :, lo:hi]
                summed[h, x, z, :, :, lo:hi] = own + arrived[h, x, z, :, :, lo:hi]
                return 0

            lax.fori_loop(0, 8, one, 0)
            saving(h, k).start()


    def put(h, lo, hi, v):
        v = v.astype(BF16)
        if paired:
            dw_ref[h, :, :, :, :, :, lo:hi] = v.reshape(2, 2, 4, 2, 16, hi - lo)
        else:
            dw_out[h, :, lo:hi] = v

    rows = f_ref.shape[0]
    slots = slot_ref.shape[0]
    wide = 1024
    lane = lax.broadcasted_iota(jnp.int32, (1, wide), 1)
    selt = jnp.where(lax.broadcasted_iota(jnp.int32, (rows, slots), 0) == row_ref[...], 1.0, 0.0).astype(BF16)
    action = slot_ref[:, atoms + 2 : atoms + 3]
    which = jnp.where(lane < atoms, -1, jnp.where(lane < atoms * (acts + 1), (lane - atoms) // atoms, -2)).astype(F32)
    coeff = jnp.where(which == -1.0, 1.0, 0.0) + jnp.where(which == action, 1.0, 0.0) - jnp.where(which >= 0.0, 1.0 / acts, 0.0)
    atom = jnp.where(which >= -1.0, lane - atoms * (which.astype(jnp.int32) + 1), -1)
    fold = jnp.where(lax.broadcasted_iota(jnp.int32, (128, wide), 0) == atom, 1.0, 0.0).astype(BF16)
    pre = []
    for h in range(2):
        total = 0.0
        for k, (lo, hi) in enumerate(HEAD_COLUMNS):
            if paired:
                loads[h, k].wait()
            hi = min(hi, 3200)
            total = total + dot_nt(f_ref[:, lo:hi], w_ref[h, :, lo:hi])
        pre.append(total)
    hidden, slope = [], []
    for k in range(2):
        a, s = silu_and_slope(pre[k])
        hidden.append(a.astype(BF16))
        slope.append(s)
    out_w = jnp.concatenate([w_ref[0, :, 3200:], w_ref[1, :, 3200:]], axis=1)
    zero = jnp.zeros((), BF16)
    w_val = jnp.where(lane[:, :128] < atoms, out_w[:, :128].astype(F32), 0.0).astype(BF16)
    w_adv = jnp.where(lane >= atoms, out_w.astype(F32), 0.0).astype(BF16)
    outs = bias_ref.shape[1]
    bias = jnp.concatenate([bias_ref[...], jnp.zeros((1, wide - outs), F32)], axis=1)
    logits = dot(hidden[1], w_adv) + bias
    logits = jnp.concatenate([logits[:, :128] + dot(hidden[0], w_val), logits[:, 128:]], axis=1)
    high, low = high_low(logits)
    per_slot = dot_tn(selt, high) + dot_tn(selt, low)
    high, low = high_low(per_slot * coeff)
    q = dot_nt(high, fold) + dot_nt(low, fold)
    lane_q = lax.broadcasted_iota(jnp.int32, (slots, 128), 1)
    used = lane_q < atoms
    top = jnp.max(jnp.where(used, q, -jnp.inf), axis=1, keepdims=True)
    shifted = jnp.where(used, jnp.exp(jnp.where(used, q - top, 0.0)), 0.0)
    total = jnp.sum(shifted, axis=1, keepdims=True)
    tgt = jnp.where(used, slot_ref[...], 0.0)
    cross = -jnp.sum(jnp.where(used, tgt * (q - top - jnp.log(total)), 0.0), axis=1, keepdims=True)
    coef = slot_ref[:, atoms : atoms + 1]
    valid = slot_ref[:, atoms + 1 : atoms + 2]
    prio_ref[...] = jnp.transpose(jnp.broadcast_to(valid * cross, (slots, 128)))[0:1]
    q_grad = coef * (shifted * (jnp.sum(tgt, axis=1, keepdims=True) / total) - tgt)
    high, low = high_low(q_grad)
    lgrad = ((dot(high, fold) + dot(low, fold)) * coeff).astype(BF16)
    bias_grad = jnp.sum(lgrad.astype(F32), axis=0, keepdims=True)
    for k in range(8):
        stat_ref[k : k + 1, :] = bias_grad[:, 128 * k : 128 * k + 128]
    stat_ref[8:9, :] = jnp.broadcast_to(jnp.sum(coef * cross, axis=0, keepdims=True), (1, 128))
    stat_ref[9:10, :] = jnp.broadcast_to(jnp.sum(valid, axis=0, keepdims=True), (1, 128))
    stat_ref[10:16, :] = jnp.zeros((6, 128), F32)
    grad = dot(selt, lgrad).astype(BF16)
    d_adv = dot_tn(hidden[1], grad)
    d_val = dot_tn(hidden[0], grad[:, :128])
    put(0, 3200, 3328, jnp.where(lane[:, :128] < atoms, d_val, d_adv[:, :128]))
    put(0, 3328, HALF, d_adv[:, 128:512])
    put(1, 3200, HALF, d_adv[:, 512:])
    pre_grad = [
        (dot_nt(grad[:, :128], w_val) * slope[0]).astype(BF16),
        (dot_nt(grad, w_adv) * slope[1]).astype(BF16),
    ]
    for k in range(2):
        for part, (lo, hi) in enumerate(((0, 1024), (1024, 2048), (2048, 3200))):
            put(k, lo, hi, dot_tn(pre_grad[k], f_ref[:, lo:hi]))
            if paired:
                if (k, part) == (0, 0):
                    pl.semaphore_wait(barrier, 1)
                to_core(k, part).start()
    for part, (lo, hi) in enumerate(((0, 1024), (1024, 2048), (2048, 3200))):
        back = dot(pre_grad[0], w_ref[0, :, lo:hi]) + dot(pre_grad[1], w_ref[1, :, lo:hi])
        fg_ref[:, lo:hi] = back.astype(BF16)
        if paired:
            add_core(0, part)
    if paired:
        for part in range(3):
            add_core(1, part)
        for h in range(2):
            for part in range(3):
                saving(h, part).wait()


def heads(atoms, acts, feats, weights, bias, per_slot, rows_of_slot, paired=False):
    slots = per_slot.shape[0]
    block = (2, 2, 4, 2, 16, HALF)
    scratch, params = [], {}
    if paired:
        scratch = [
            pltpu.VMEM((2, 2, 2, 4, 2, 16, HALF), BF16),
            pltpu.VMEM(block, BF16),
            pltpu.VMEM(weights.shape, BF16),
            pltpu.VMEM(block, BF16),
            *[pltpu.SemaphoreType.DMA((2, 3))] * 4,
        ]
        params = dict(collective_id=3, has_side_effects=True)
    vmem = pl.BlockSpec(memory_space=pltpu.VMEM)
    large = pl.BlockSpec(memory_space=pl.ANY) if paired else vmem
    return pl.pallas_call(
        functools.partial(heads_kernel, atoms, acts, paired),
        in_specs=[vmem, large, vmem, vmem, vmem],
        out_specs=[large, vmem, vmem, vmem],
        out_shape=[
            jax.ShapeDtypeStruct(block if paired else weights.shape, BF16),
            jax.ShapeDtypeStruct(feats.shape, BF16),
            jax.ShapeDtypeStruct((1, slots), F32),
            jax.ShapeDtypeStruct((16, 128), F32),
        ],
        scratch_shapes=scratch,
        compiler_params=pltpu.CompilerParams(vmem_limit_bytes=VMEM_LIMIT, **params),
        name="heads",
    )(feats, weights, bias, per_slot, rows_of_slot[None, :])


def finish_kernel(
    dsum, stat, kern, fn, hn, on, loss, g1, g2, g3t, mean_g, spread_g, bias_g, val_g, val_s, adv_g, adv_s, out_g
):
    feat, atoms, outs = fn.shape[1], val_g.shape[1], on.shape[1]
    inverse = 1.0 / stat[9:10, 0:1]
    loss[...] = stat[8:9, 0:1] * inverse
    v = kern[...]
    turned = pltpu.roll(v, 64, 1)
    g2[0:32, :] = v[0:32, 0:64]
    g2[32:64, :] = turned[0:32, 0:64]
    third = jnp.concatenate([v[32:64], turned[32:64], v[64:72], jnp.zeros((56, 128), F32)], axis=0)
    g3t[...] = jnp.transpose(third)[0:64, 0:72]
    for k in range(4):
        g1[8 * k : 8 * k + 8, :] = v[72:80, 32 * k : 32 * k + 32]
    for h in range(2):
        mean = dsum[h, :, 0:feat] * inverse
        mean_g[h] = mean
        spread_g[h] = mean * fn[h : h + 1, :] * as_column(hn[0, h : h + 1, :])
        bias_g[h : h + 1, :] = as_row(dsum[h, :, feat : feat + 1] * inverse)
    out = jnp.concatenate([dsum[0, :, 3200:], dsum[1, :, 3200:]], axis=1) * inverse
    val, adv = out[:, :atoms], out[:, atoms:outs]
    val_g[...] = val
    val_s[...] = val * as_column(hn[1, 0:1, :]) * on[:, :atoms]
    adv_g[...] = adv
    adv_s[...] = adv * as_column(hn[1, 1:2, :]) * on[:, atoms:]
    out_g[...] = jnp.concatenate([stat[k : k + 1, :] for k in range(8)], axis=1)[:, :outs] * inverse


def outputs(dsum, stat, kern, fn, hn, on, atoms):
    feat, outs = fn.shape[1], on.shape[1]
    shapes = [(1, 1), (32, 32), (64, 64), (64, 72), (2, 16, feat), (2, 16, feat), (2, 16)]
    shapes += [(16, atoms)] * 2 + [(16, outs - atoms)] * 2 + [(1, outs)]
    return pl.pallas_call(
        finish_kernel,
        out_shape=[jax.ShapeDtypeStruct(s, F32) for s in shapes],
        compiler_params=pltpu.CompilerParams(vmem_limit_bytes=VMEM_LIMIT),
        name="outputs",
    )(dsum, stat, kern, fn, hn, on)


def exchange_kernel(count, kern_ref, slot_ref, kerns_out, slots_out, send_kern, recv_kern, send_slot, recv_slot, own):
    me = lax.axis_index("dp")
    peers = [lax.rem(me + k, count) for k in range(count)]
    barrier = pltpu.get_barrier_semaphore()
    for k in range(1, count):
        pl.semaphore_signal(barrier, inc=1, device_id={"dp": peers[k]}, device_id_type=pl.DeviceIdType.MESH)
    pl.semaphore_wait(barrier, count - 1)
    mine = [
        pltpu.make_async_copy(kern_ref, kerns_out.at[me], own.at[0]),
        pltpu.make_async_copy(slot_ref.at[me], slots_out.at[me], own.at[1]),
    ]
    sent = []
    for k in range(1, count):
        to = dict(device_id={"dp": peers[k]}, device_id_type=pl.DeviceIdType.MESH)
        sent.append(pltpu.make_async_remote_copy(kern_ref, kerns_out.at[me], send_kern.at[k], recv_kern.at[k], **to))
        sent.append(pltpu.make_async_remote_copy(slot_ref.at[peers[k]], slots_out.at[me], send_slot.at[k], recv_slot.at[k], **to))
    for copy in mine + sent:
        copy.start()
    for copy in mine + sent:
        copy.wait()


def exchange(kern, slot):
    count = slot.shape[0]
    return pl.pallas_call(
        functools.partial(exchange_kernel, count),
        in_specs=[pl.BlockSpec(memory_space=pltpu.VMEM)] * 2,
        out_specs=[pl.BlockSpec(memory_space=pltpu.VMEM)] * 2,
        out_shape=[jax.ShapeDtypeStruct((count, *kern.shape), kern.dtype), jax.ShapeDtypeStruct(slot.shape, slot.dtype)],
        scratch_shapes=[pltpu.SemaphoreType.DMA((count,))] * 4 + [pltpu.SemaphoreType.DMA((2,))],
        compiler_params=pltpu.CompilerParams(collective_id=2, has_side_effects=True, vmem_limit_bytes=VMEM_LIMIT),
        name="exchange",
    )(kern, slot)


def on_device(
    frames,
    send_rows,
    recv_counts,
    actions,
    target_dist,
    sample_weight,
    conv_first,
    conv_second,
    conv_third,
    hidden_mean,
    hidden_spread,
    hidden_bias,
    feature_noise,
    hidden_noise,
    value_mean,
    value_spread,
    advantage_mean,
    advantage_spread,
    output_noise,
    output_bias,
):
    dp_count = lax.axis_size("dp")
    slots = send_rows.shape[0]
    capacity = slots // dp_count
    atoms = value_mean.shape[1]
    acts = advantage_mean.shape[1] // atoms
    rows = frames.shape[0]
    feat, own = hidden_mean.shape[1:]
    outs = atoms * (acts + 1)

    x = frames.transpose(1, 0, 2).reshape(21, 4, rows, 336)
    bias = output_bias[None, :]
    mean_t = hidden_mean.transpose(0, 2, 1)
    spread_t = hidden_spread.transpose(0, 2, 1)

    if (dp_count, lax.axis_size("mp"), own, slots) == (8, 4, 16, 512):
        noise = output_noise[None, :]
        shared = [mean_t, spread_t, hidden_bias, feature_noise, hidden_noise]
        shared += [value_mean, value_spread, advantage_mean, advantage_spread, noise]
        shared += [target_dist.T, recv_counts[None, :], actions[None, :], sample_weight[None, :]]
        kernels = [conv_first, conv_second, conv_third.T]
        a1, s1, a2, s2, feats, s3, y, y0, weights, per_slot, kern2, kern3 = torso_forward(x, kernels, shared)
        weights, per_slot = weights.reshape(2, 512, HALF), per_slot.reshape(slots, 128)
        dweights, feat_grad, prio, stat = heads(atoms, acts, feats, weights, bias, per_slot, send_rows, paired=True)
        summed = [dweights, stat]
        summed = torso_backward(y, y0, a1, s1, a2, s2, s3, feat_grad, kern2, kern3, summed=summed)
        loss, g1, g2, g3t, mean_g, spread_g, bias_g, *outer, out_g = outputs(
            *summed, feature_noise, hidden_noise, noise, atoms
        )
        return (
            loss[0, 0],
            g1,
            g2,
            g3t.T,
            mean_g.transpose(0, 2, 1),
            spread_g.transpose(0, 2, 1),
            bias_g,
            *outer,
            out_g[0],
            prio[0],
        )

    sizes = [w.size for w in (conv_first, conv_second, conv_third)]
    flat = jnp.concatenate([w.astype(BF16).reshape(-1) for w in (conv_first, conv_second, conv_third)])
    tall = -(-flat.size // 2048) * 16
    flat = jnp.pad(flat, (0, tall * 128 - flat.size)).reshape(tall, 128)
    is_valid = jnp.arange(capacity, dtype=jnp.int32)[None, :] < recv_counts[:, None]
    is_valid = is_valid.astype(F32).reshape(slots)
    per_slot = jnp.stack([is_valid * sample_weight, is_valid, actions.astype(F32)], axis=1)
    per_slot = jnp.concatenate([target_dist, per_slot, jnp.zeros((slots, 125 - atoms), F32)], axis=1)
    flat, per_slot = exchange(flat, per_slot.reshape(dp_count, capacity, 128))
    per_slot = per_slot.reshape(slots, 128)
    flat = flat.reshape(dp_count, -1)
    kern1 = jnp.tile(flat[:, : sizes[0]].reshape(-1, 32), (1, 4))
    kern2 = jnp.tile(flat[:, sizes[0] : sizes[0] + sizes[1]].reshape(-1, 64), (1, 2))
    kern3 = jnp.tile(flat[:, sizes[0] + sizes[1] : sum(sizes)].reshape(-1, 64), (1, 2))

    wide_one = mean_t + spread_t * feature_noise[:, None, :] * hidden_noise[0][:, :, None]
    wide_one = jnp.concatenate([wide_one, hidden_bias[:, :, None], jnp.zeros((2, own, 63), F32)], axis=2)
    wide_val = value_mean + value_spread * hidden_noise[1, 0][:, None] * output_noise[None, :atoms]
    wide_adv = advantage_mean + advantage_spread * hidden_noise[1, 1][:, None] * output_noise[None, atoms:]
    wide_out = jnp.concatenate([wide_val, wide_adv, jnp.zeros((own, 1024 - outs), F32)], axis=1)
    wide_out = wide_out.reshape(own, 2, 512).transpose(1, 0, 2)
    shard = jnp.concatenate([wide_one, wide_out], axis=2).astype(BF16)
    weights = lax.all_gather(shard, ("mp", "dp"), axis=1, tiled=True)

    a1, s1, a2, s2, feats, s3, y, y0 = torso_forward(x, [kern1, kern2, kern3])
    dweights, feat_grad, prio, stat = heads(atoms, acts, feats, weights, bias, per_slot, send_rows)
    dshard = lax.psum_scatter(dweights, ("mp", "dp"), scatter_dimension=1, tiled=True).astype(F32)
    stat = lax.psum(stat, ("dp", "mp"))
    inverse = 1.0 / stat[9, 0]
    k1, k2, k3 = torso_backward(y, y0, a1, s1, a2, s2, s3, feat_grad, kern2, kern3)
    kflat = jnp.concatenate([g.reshape(dp_count, -1) for g in (k1[:, :32], k2[:, :64], k3[:, :64])], axis=1)
    kflat = lax.psum(lax.psum_scatter(kflat, "dp", scatter_dimension=0, tiled=True)[0], "mp") * inverse
    conv_grads = (
        kflat[: sizes[0]].reshape(conv_first.shape),
        kflat[sizes[0] : sizes[0] + sizes[1]].reshape(conv_second.shape),
        kflat[sizes[0] + sizes[1] :].reshape(conv_third.shape),
    )
    dshard = dshard * inverse
    mean_grad_t = dshard[:, :, :feat]
    spread_grad_t = mean_grad_t * feature_noise[:, None, :] * hidden_noise[0][:, :, None]
    out_grad = dshard[:, :, 3200:].transpose(1, 0, 2).reshape(own, 1024)
    value_mean_grad = out_grad[:, :atoms]
    adv_mean_grad = out_grad[:, atoms:outs]
    return (
        stat[8, 0] * inverse,
        *conv_grads,
        mean_grad_t.transpose(0, 2, 1),
        spread_grad_t.transpose(0, 2, 1),
        dshard[:, :, feat],
        value_mean_grad,
        value_mean_grad * hidden_noise[1, 0][:, None] * output_noise[None, :atoms],
        adv_mean_grad,
        adv_mean_grad * hidden_noise[1, 1][:, None] * output_noise[None, atoms:],
        stat[:8].reshape(-1)[:outs] * inverse,
        prio[0],
    )


def solution(mesh):
    both, heads_dim = P(("dp", "mp")), P(("mp", "dp"), None)
    return jax.shard_map(
        on_device,
        mesh=mesh,
        in_specs=(
            P(("dp", "mp"), None, None),
            both,
            both,
            both,
            P(("dp", "mp"), None),
            both,
            P("dp", None),
            P("dp", None),
            P("dp", None),
            P(None, None, ("mp", "dp")),
            P(None, None, ("mp", "dp")),
            P(None, ("mp", "dp")),
            P(),
            P(None, None, ("mp", "dp")),
            heads_dim,
            heads_dim,
            heads_dim,
            heads_dim,
            P(),
            P(),
        ),
        out_specs=(
            P(),
            P("dp", None),
            P("dp", None),
            P("dp", None),
            P(None, None, ("mp", "dp")),
            P(None, None, ("mp", "dp")),
            P(None, ("mp", "dp")),
            heads_dim,
            heads_dim,
            heads_dim,
            heads_dim,
            P(),
            both,
        ),
        check_vma=False,
    )
```
